128 devices in a mesh: row: 16 (over z_lo, y, core), col: 8 (over x, z_hi).
Axes of the slice: x: 4, y: 4, z: 4 (z_hi: 2, z_lo: 2; z = z_hi * 2 + z_lo), core: 2. Of those that a mesh axis runs over, the one named last changes fastest.
Arguments:
- homolog_features: bfloat16 [1024, 128, 256], P('row', 'col'), may hold values from -6 to 6
- pair_input: bfloat16 [128, 128, 128], P('row', 'col'), may hold values from -6 to 6
- cotangent: bfloat16 [128, 128, 128], P('row', 'col'), may hold values from -6 to 6
- homolog_factor_matrix: bfloat16 [256, 64], replicated, may hold values from -0.375 to 0.375
- outer_output_weight: bfloat16 [1024, 128], replicated, may hold values from -6 to 6
- outgoing_input_weight: bfloat16 [128, 640], replicated, may hold values from -0.5 to 0.5
- outgoing_output_weight: bfloat16 [128, 128], replicated, may hold values from -0.5 to 0.5
- incoming_input_weight: bfloat16 [128, 640], replicated, may hold values from -0.5 to 0.5
- incoming_output_weight: bfloat16 [128, 128], replicated, may hold values from -0.5 to 0.5
Outputs:
- pair_output: bfloat16 [128, 128, 128], P('row', 'col')
- pair_input_gradient: float32 [128, 128, 128], P('row', 'col')
- alignment_gradient: float32 [1024, 128, 256], P('row', 'col')
The draws below stay inside these ranges and needn't reach their ends.
All inputs are finite; a program needn't handle non-finite values.
Results may differ from the reference program's by a relative error of at most 0.025.
Values may be sent and summed in bfloat16 or wider, within the bound.
A program may use at most 64 MiB of HBM per device.

```python
import jax
import jax.numpy as jnp
from jax import lax

FEATURE_DEPTH = 256
PAIR_WIDTH = 128
MIDDLE_DEPTH = 32
AMINO_TOTAL = 128
HOMOLOG_TOTAL = 1024


def block_levels(stream_key, dims, split, smallest, top_value):
    factor_of = 1.0
    for axis_at, parts in split:
        steps = jax.random.uniform(jax.random.fold_in(jax.random.fold_in(stream_key, 6), axis_at), (parts,), jnp.float32, smallest / len(split), top_value / len(split))
        factor_of = factor_of * jnp.repeat(jnp.exp(steps), dims[axis_at] // parts).reshape((-1,) + (1,) * (len(dims) - 1 - axis_at))
    return factor_of


def normal_values(stream_key, shape, width, reach, cuts=(), held_as=jnp.bfloat16):
    gain = block_levels(stream_key, shape, cuts, -0.22, 0.18) if cuts else 1.0
    result = jax.random.normal(stream_key, shape, jnp.float32) * width * gain
    return jnp.minimum(jnp.maximum(result, -reach), reach).astype(held_as)


def setup_inputs(seed: int = 0) -> dict:
    streams_of = jax.random.split(jax.random.key(seed), 10)
    homolog_features = normal_values(streams_of[0], (HOMOLOG_TOTAL, AMINO_TOTAL, FEATURE_DEPTH), 1.0, 6.0, ((0, 16), (1, 8)))
    pair_input = normal_values(streams_of[1], (AMINO_TOTAL, AMINO_TOTAL, PAIR_WIDTH), 1.0, 6.0, ((0, 16), (1, 8)))
    cotangent = normal_values(streams_of[2], (AMINO_TOTAL, AMINO_TOTAL, PAIR_WIDTH), 1.0, 6.0, ((0, 16), (1, 8)))
    homolog_factor_matrix = normal_values(streams_of[3], (FEATURE_DEPTH, 2 * MIDDLE_DEPTH), FEATURE_DEPTH ** -0.5, 0.375)
    outer_output_weight = normal_values(streams_of[4], (MIDDLE_DEPTH * MIDDLE_DEPTH, PAIR_WIDTH), (max(1, MIDDLE_DEPTH * MIDDLE_DEPTH // HOMOLOG_TOTAL)) ** -0.5, 6.0)
    outgoing_input_weight = normal_values(streams_of[5], (PAIR_WIDTH, 5 * PAIR_WIDTH), PAIR_WIDTH ** -0.5, 0.5)
    outgoing_output_weight = normal_values(streams_of[6], (PAIR_WIDTH, PAIR_WIDTH), PAIR_WIDTH ** -0.5, 0.5)
    incoming_input_weight = normal_values(streams_of[7], (PAIR_WIDTH, 5 * PAIR_WIDTH), PAIR_WIDTH ** -0.5, 0.5)
    incoming_output_weight = normal_values(streams_of[8], (PAIR_WIDTH, PAIR_WIDTH), PAIR_WIDTH ** -0.5, 0.5)
    return dict(homolog_features=homolog_features, pair_input=pair_input, cotangent=cotangent, homolog_factor_matrix=homolog_factor_matrix, outer_output_weight=outer_output_weight, outgoing_input_weight=outgoing_input_weight, outgoing_output_weight=outgoing_output_weight, incoming_input_weight=incoming_input_weight, incoming_output_weight=incoming_output_weight)


EPSILON = 1e-05

def normalize_layer(inputs):
    average = lax.optimization_barrier(jnp.mean(inputs, axis=-1, keepdims=True))
    centered = inputs - average
    spread = lax.optimization_barrier(jnp.mean(centered * centered, axis=-1, keepdims=True))
    return centered * lax.rsqrt(spread + EPSILON)

def norm_backprop(inputs, upstream):
    unused, pullback = jax.vjp(normalize_layer, inputs)
    return pullback(upstream)[0]

def gated_factor(projected_input, channels):
    return (jax.nn.sigmoid(projected_input[..., :channels]) * projected_input[..., channels:2 * channels]).astype(jnp.bfloat16)

def gated_pairs(projected_input, channels):
    return (gated_factor(projected_input, channels), gated_factor(projected_input[..., 2 * channels:], channels))

def triangle_inputs(pair_map, weight_in):
    normalized = normalize_layer(pair_map.astype(jnp.float32)).astype(jnp.bfloat16)
    projected_input = jnp.dot(normalized, weight_in, preferred_element_type=jnp.float32)
    return (normalized, projected_input)

def triangle_output(pair_map, projected_input, mixing, weight_out):
    channels = weight_out.shape[1]
    gating = jax.nn.sigmoid(projected_input[..., 4 * channels:])
    mixing_normed = normalize_layer(mixing).astype(jnp.bfloat16)
    update = jnp.dot(mixing_normed, weight_out, preferred_element_type=jnp.float32)
    return (pair_map.astype(jnp.float32) + gating * update).astype(jnp.bfloat16)

def output_pullback(projected_input, mixing, weight_out, upstream):
    channels = weight_out.shape[1]
    gating = jax.nn.sigmoid(projected_input[..., 4 * channels:])
    mixing_normed = normalize_layer(mixing).astype(jnp.bfloat16)
    update = jnp.dot(mixing_normed, weight_out, preferred_element_type=jnp.float32)
    update_cot = (upstream * gating).astype(jnp.bfloat16)
    normalized_gradient = jnp.dot(update_cot, weight_out.T, preferred_element_type=jnp.float32)
    mixing_cot = norm_backprop(mixing, normalized_gradient).astype(jnp.bfloat16)
    gating_cot = upstream * update * gating * (1.0 - gating)
    return (mixing_cot, gating_cot)

def input_pullback(pair_map, projected_input, left_cot, right_cot, gating_cot, weight_in, upstream):
    channels = left_cot.shape[-1]
    left_sigmoid = jax.nn.sigmoid(projected_input[..., :channels])
    right_sigmoid = jax.nn.sigmoid(projected_input[..., 2 * channels:3 * channels])
    pieces = [left_cot * projected_input[..., channels:2 * channels] * left_sigmoid * (1.0 - left_sigmoid), left_cot * left_sigmoid, right_cot * projected_input[..., 3 * channels:4 * channels] * right_sigmoid * (1.0 - right_sigmoid), right_cot * right_sigmoid, gating_cot]
    proj_cot = jnp.concatenate(pieces, axis=-1).astype(jnp.bfloat16)
    normalized_gradient = jnp.dot(proj_cot, weight_in.T, preferred_element_type=jnp.float32)
    return upstream + norm_backprop(pair_map.astype(jnp.float32), normalized_gradient)

def homolog_mapped(homolog_features, homolog_factor_matrix):
    hidden_state = homolog_factor_matrix.shape[1] // 2
    normalized = normalize_layer(homolog_features.astype(jnp.float32)).astype(jnp.bfloat16)
    projected_input = jnp.dot(normalized, homolog_factor_matrix, preferred_element_type=jnp.float32)
    return (projected_input[..., :hidden_state].astype(jnp.bfloat16), projected_input[..., hidden_state:].astype(jnp.bfloat16))

def reference(homolog_features, pair_input, cotangent, homolog_factor_matrix, outer_output_weight, outgoing_input_weight, outgoing_output_weight, incoming_input_weight, incoming_output_weight):
    left_alignment, right_alignment = homolog_mapped(homolog_features, homolog_factor_matrix)
    widened_left = left_alignment.astype(jnp.float32)
    widened_right = right_alignment.astype(jnp.float32)
    outer_mean = (jnp.einsum('sic,sjd->ijcd', widened_left, widened_right) / HOMOLOG_TOTAL).reshape(AMINO_TOTAL, AMINO_TOTAL, MIDDLE_DEPTH * MIDDLE_DEPTH).astype(jnp.bfloat16)
    pair_first = (pair_input.astype(jnp.float32) + jnp.dot(outer_mean, outer_output_weight, preferred_element_type=jnp.float32)).astype(jnp.bfloat16)
    unused, proj_out = triangle_inputs(pair_first, outgoing_input_weight)
    left_out, right_out = gated_pairs(proj_out, PAIR_WIDTH)
    mixing_out = jnp.einsum('ikc,jkc->ijc', left_out.astype(jnp.float32), right_out.astype(jnp.float32))
    pair_second = triangle_output(pair_first, proj_out, mixing_out, outgoing_output_weight)
    unused, proj_in = triangle_inputs(pair_second, incoming_input_weight)
    left_in, right_in = gated_pairs(proj_in, PAIR_WIDTH)
    mixing_in = jnp.einsum('kic,kjc->ijc', left_in.astype(jnp.float32), right_in.astype(jnp.float32))
    pair_output = triangle_output(pair_second, proj_in, mixing_in, incoming_output_weight)
    upstream = cotangent.astype(jnp.float32)
    mixing_cot, gating_cot = output_pullback(proj_in, mixing_in, incoming_output_weight, upstream)
    mix_wide = mixing_cot.astype(jnp.float32)
    left_cot = jnp.einsum('ijc,kjc->kic', mix_wide, right_in.astype(jnp.float32))
    right_cot = jnp.einsum('ijc,kic->kjc', mix_wide, left_in.astype(jnp.float32))
    second_cot = input_pullback(pair_second, proj_in, left_cot, right_cot, gating_cot, incoming_input_weight, upstream)
    mixing_cot, gating_cot = output_pullback(proj_out, mixing_out, outgoing_output_weight, second_cot)
    mix_wide = mixing_cot.astype(jnp.float32)
    left_cot = jnp.einsum('ijc,jkc->ikc', mix_wide, right_out.astype(jnp.float32))
    right_cot = jnp.einsum('ijc,ikc->jkc', mix_wide, left_out.astype(jnp.float32))
    pair_input_gradient = input_pullback(pair_first, proj_out, left_cot, right_cot, gating_cot, outgoing_input_weight, second_cot)
    pair_gradient_flow = lax.optimization_barrier(pair_input_gradient.astype(jnp.bfloat16)).astype(jnp.float32)
    weight_cube = outer_output_weight.astype(jnp.float32).reshape(MIDDLE_DEPTH, MIDDLE_DEPTH, PAIR_WIDTH)
    count_of_blocks = AMINO_TOTAL // 8

    def block_left_part(row_block):
        mixed_part = jnp.einsum('sjd,ije->side', widened_right, row_block)
        mixed_part = lax.optimization_barrier(mixed_part.astype(jnp.bfloat16)).astype(jnp.float32)
        return jnp.einsum('side,cde->sic', mixed_part, weight_cube) / HOMOLOG_TOTAL

    def block_right_part(target_tile):
        mixed_part = jnp.einsum('sic,ije->sjce', widened_left, target_tile)
        mixed_part = lax.optimization_barrier(mixed_part.astype(jnp.bfloat16)).astype(jnp.float32)
        return jnp.einsum('sjce,cde->sjd', mixed_part, weight_cube) / HOMOLOG_TOTAL
    left_alignment_gradient = lax.map(block_left_part, pair_gradient_flow.reshape(count_of_blocks, 8, AMINO_TOTAL, PAIR_WIDTH))
    left_alignment_gradient = left_alignment_gradient.transpose(1, 0, 2, 3).reshape(HOMOLOG_TOTAL, AMINO_TOTAL, MIDDLE_DEPTH)
    right_alignment_gradient = lax.map(block_right_part, pair_gradient_flow.reshape(AMINO_TOTAL, count_of_blocks, 8, PAIR_WIDTH).transpose(1, 0, 2, 3))
    right_alignment_gradient = right_alignment_gradient.transpose(1, 0, 2, 3).reshape(HOMOLOG_TOTAL, AMINO_TOTAL, MIDDLE_DEPTH)
    alignment_projection_gradient = jnp.concatenate([left_alignment_gradient, right_alignment_gradient], axis=-1).astype(jnp.bfloat16)
    normalized_gradient = jnp.dot(alignment_projection_gradient, homolog_factor_matrix.T, preferred_element_type=jnp.float32)
    alignment_gradient = norm_backprop(homolog_features.astype(jnp.float32), normalized_gradient)
    return (pair_output, pair_input_gradient, alignment_gradient)
```

```python
import jax
import jax.numpy as jnp
from jax import lax
from jax.experimental import pallas as pl
from jax.experimental.pallas import tpu as pltpu
from jax.sharding import PartitionSpec as P

SEQUENCES = 1024
EPSILON = 1e-05
MESH = pl.DeviceIdType.MESH
F32 = jnp.float32
BF16 = jnp.bfloat16
GRID = 8
BLOCK = 16
WIDTH = 128
HIDDEN = 32


def dot(lhs, rhs, dims=((1,), (0,))):
    return lax.dot_general(lhs, rhs, (dims, ((), ())), preferred_element_type=F32)


def layer_norm(inputs):
    centered = inputs - jnp.mean(inputs, axis=-1, keepdims=True)
    spread = jnp.mean(centered * centered, axis=-1, keepdims=True)
    scale = lax.rsqrt(spread + EPSILON)
    return centered * scale, scale


def layer_norm_pullback(normed, scale, upstream):
    along = jnp.mean(upstream * normed, axis=-1, keepdims=True)
    return scale * (upstream - jnp.mean(upstream, axis=-1, keepdims=True) - normed * along)


def pair_kernel(
    left_ic,
    left_ci,
    right_dj,
    pair_input,
    cotangent,
    outer_weight,
    spread_weight_hbm,
    out_in_weight,
    out_out_weight,
    in_in_weight,
    in_out_weight,
    pair_output,
    pair_gradient,
    msa_cots,
    pair_block,
    cot_block,
    relay_left,
    relay_right,
    msa_left,
    msa_right,
    msa_rows,
    o_left,
    o_right,
    o_right_stage,
    i_left,
    i_right,
    i_left_stage,
    ib_right,
    ib_left,
    ib_cot,
    ib_cot_turned,
    ib_cot_stage,
    ob_right,
    ob_left,
    ob_cot_row,
    ob_cot_col,
    ob_cot_stage,
    final_cot,
    spread_weight,
    outer32,
    wide,
    flat,
    proj_out,
    proj_in,
    mixing_out,
    first,
    second,
    upstream32,
    stacked,
    grad_table,
    msa_cot_own,
    msa_cot_got,
    output_stage,
    output_got,
    gradient_stage,
    gradient_got,
    relay_sem,
    block_sem,
    msa_sem,
    rows_sem,
    pair_sem,
    final_sem,
    small_sem,
    send_sem,
    weight_sem,
):
    row, col = lax.axis_index("row"), lax.axis_index("col")
    a, h, b = row // 2, row % 2, col
    other = 1 - h
    own_i = a * other + b * h
    own_j = b * other + a * h
    diagonal = a == b

    def row_chip(n):
        return a * other + n * h, n * other + b * h

    def col_chip(n):
        return n * other + a * h, b * other + n * h

    def remote(src, dst, send, recv, chip, core):
        return pltpu.make_async_remote_copy(
            src_ref=src,
            dst_ref=dst,
            send_sem=send,
            recv_sem=recv,
            device_id=(2 * chip[0] + core, chip[1]),
            device_id_type=MESH,
        )

    def wait_for(ref, sem):
        pltpu.make_async_copy(ref, ref, sem).wait()

    weight_copy = pltpu.make_async_copy(spread_weight_hbm, spread_weight, weight_sem)
    weight_copy.start()

    barrier = pltpu.get_barrier_semaphore()

    def greet(chip, core):
        pl.semaphore_signal(
            barrier, inc=1, device_id=(2 * chip[0] + core, chip[1]), device_id_type=MESH
        )

    def greet_step(k, carry):
        for core in range(2):
            greet(((a + k) % GRID, b), core)
            greet((a, (b + k) % GRID), core)
        return carry

    lax.fori_loop(1, GRID, greet_step, 0)
    greet((a, b), other)

    @pl.when(jnp.logical_not(diagonal))
    def _():
        greet((b, a), 0)
        greet((b, a), 1)
        pl.semaphore_wait(barrier, 31)

    @pl.when(diagonal)
    def _():
        pl.semaphore_wait(barrier, 29)

    for slot, (src, dst) in enumerate(((left_ic, relay_left), (right_dj, relay_right))):

        @pl.when(jnp.logical_not(diagonal))
        def _():
            remote(src, dst, send_sem.at[slot], relay_sem.at[slot], (b, a), h).start()

        @pl.when(diagonal)
        def _():
            pltpu.make_async_copy(src, dst, relay_sem.at[slot]).start()

    def msa_send(src, dst, sems, slot, chips, own, core, send):
        def step(k, carry):
            n = (own + k) % GRID

            @pl.when(jnp.logical_or(k > 0, h != core))
            def _():
                remote(src, dst.at[slot], send, sems.at[slot], chips(n), core).start()

            return carry

        lax.fori_loop(0, GRID, step, 0)

        @pl.when(h == core)
        def _():
            pltpu.make_async_copy(src, dst.at[slot], sems.at[slot]).start()

    def column(n):
        return n, b

    def line(n):
        return a, n

    def msa_sent(src, dst, core, send):
        @pl.when(h == core)
        def _():
            wait_for(dst.at[pl.ds(0, 7)], send)

        @pl.when(h != core)
        def _():
            wait_for(dst.at[pl.ds(0, 8)], send)

    msa_send(right_dj, msa_right, msa_sem.at[1], row, column, a, 0, send_sem.at[2])
    msa_send(left_ic, msa_left, msa_sem.at[0], row, column, a, 1, send_sem.at[3])

    for slot, (src, dst) in enumerate(((pair_input, pair_block), (cotangent, cot_block))):
        half = dst.at[pl.ds(h * 8, 8)]
        sem = block_sem.at[slot, h]

        @pl.when(h == 0)
        def _():
            pltpu.make_async_copy(src, half, sem).start()

        @pl.when(h == 1)
        def _():
            remote(src, half, send_sem.at[4 + slot], sem, (a, b), 0).start()

        @pl.when(jnp.logical_and(h == 1, diagonal))
        def _():
            pltpu.make_async_copy(src, half, sem).start()

        @pl.when(jnp.logical_not(jnp.logical_and(h == 1, diagonal)))
        def _():
            remote(src, half, send_sem.at[6 + slot], sem, (b, a), 1).start()

    def block_sent(slot, src):
        @pl.when(h == 1)
        def _():
            wait_for(src, send_sem.at[4 + slot])

        @pl.when(jnp.logical_not(jnp.logical_and(h == 1, diagonal)))
        def _():
            wait_for(src, send_sem.at[6 + slot])

    relay_slot = 2 * b + h
    wait_for(relay_left, relay_sem.at[0])
    msa_send(relay_left, msa_left, msa_sem.at[0], relay_slot, line, b, 0, send_sem.at[8])
    wait_for(relay_right, relay_sem.at[1])
    msa_send(relay_right, msa_right, msa_sem.at[1], relay_slot, line, b, 1, send_sem.at[9])

    def msa_wait(n, carry):
        wait_for(msa_left.at[n], msa_sem.at[0, n])
        wait_for(msa_right.at[n], msa_sem.at[1, n])
        return carry

    lax.fori_loop(0, 2 * GRID, msa_wait, 0)
    everything = msa_left[...].reshape(SEQUENCES, BLOCK * HIDDEN)
    outer32[...] = dot(
        msa_right[...].reshape(SEQUENCES, BLOCK * HIDDEN), everything, ((0,), (0,))
    ) * (1.0 / SEQUENCES)
    lane_part = lax.broadcasted_iota(jnp.int32, (BLOCK, WIDTH), 1) // HIDDEN

    def project_step(d2, total):
        columns = []
        for part in range(2):
            tile = outer32[pl.ds(pl.multiple_of((2 * d2 + part) * BLOCK, BLOCK), BLOCK), :]
            columns.append(
                jnp.concatenate(
                    [
                        jnp.where(lane_part == q, tile[:, g * WIDTH : (g + 1) * WIDTH], 0.0)
                        for q in range(4)
                        for g in range(4)
                    ],
                    axis=0,
                )
            )
        picked = jnp.concatenate(columns, axis=1).astype(BF16)
        weight = outer_weight[pl.ds(pl.multiple_of(d2 * 2 * WIDTH, 2 * WIDTH), 2 * WIDTH), :]
        return total + dot(picked, weight)

    projected = lax.fori_loop(
        0, HIDDEN // 2, project_step, jnp.zeros((BLOCK * BLOCK, WIDTH), F32)
    )
    for part in range(2):
        wait_for(pair_block.at[pl.ds(part * 8, 8)], block_sem.at[0, part])
        wait_for(cot_block.at[pl.ds(part * 8, 8)], block_sem.at[1, part])
    for i in range(BLOCK):
        start = ((i % 4) * 4 + i // 4) * BLOCK
        first[pl.ds(i * BLOCK, BLOCK), :] = (
            (pair_block[i].astype(F32) + projected[start : start + BLOCK]).astype(BF16).astype(F32)
        )

    def send_same(dst, sems, chips, own, send):
        def step(k, carry):
            remote(
                dst.at[own], dst.at[own], send, sems.at[own], chips((own + k) % GRID), h
            ).start()
            return carry

        lax.fori_loop(1, GRID, step, 0)

    def send_other(src, dst, sems, chips, own, send):
        def step(k, carry):
            remote(
                src, dst.at[own], send, sems.at[own], chips((own + k) % GRID), other
            ).start()
            return carry

        lax.fori_loop(0, GRID, step, 0)

    def contract(left, left_sem, left_own, left_by_column, right, right_sem, right_own, own):
        def arrive(ref, sems, slot, skip):
            if skip is None:
                wait_for(ref.at[slot], sems.at[slot])
            else:

                @pl.when(slot != skip)
                def _():
                    wait_for(ref.at[slot], sems.at[slot])

        def block_step(k, totals):
            slot = (own + k) % GRID
            arrive(left, left_sem, slot, left_own)
            arrive(right, right_sem, slot, right_own)
            wide[...] = left[slot].astype(F32)

            def inner(group, totals):
                totals = list(totals)
                for u in range(4):
                    t = group * 4 + u
                    across = right[slot, t].astype(F32)
                    for p in range(BLOCK):
                        if left_by_column:
                            one = wide[t, pl.ds(p, 1), :]
                        else:
                            one = wide[p, pl.ds(t, 1), :]
                        totals[p] = totals[p] + one * across
                return tuple(totals)

            return lax.fori_loop(0, BLOCK // 4, inner, totals)

        zeros = tuple(jnp.zeros((BLOCK, WIDTH), F32) for _ in range(BLOCK))
        totals = lax.fori_loop(0, GRID, block_step, zeros)
        return jnp.concatenate(totals, axis=0)

    def turned(value, store):
        flat[...] = value
        for j in range(BLOCK):
            store(j, flat[pl.ds(j, BLOCK, stride=BLOCK), :].astype(BF16))

    def blocked(value):
        return value.astype(BF16).reshape(BLOCK, BLOCK, WIDTH)

    def gates(projected, at):
        return jax.nn.sigmoid(projected[:, at * WIDTH : (at + 1) * WIDTH])

    def channels(projected, at):
        return projected[:, at * WIDTH : (at + 1) * WIDTH]

    normed, unused = layer_norm(first[...])
    projected = dot(normed.astype(BF16), out_in_weight[...])
    proj_out[...] = projected
    o_left[own_j] = blocked(gates(projected, 0) * channels(projected, 1))
    send_same(o_left, pair_sem.at[0], row_chip, own_j, send_sem.at[10])
    right = gates(projected, 2) * channels(projected, 3)

    def store_right(j, value):
        o_right_stage[j] = value

    turned(right, store_right)
    send_other(o_right_stage, o_right, pair_sem.at[1], row_chip, own_j, send_sem.at[11])
    ob_left[own_i] = o_left[own_j]
    ob_right[own_i] = blocked(right)
    send_same(ob_left, pair_sem.at[2], col_chip, own_i, send_sem.at[12])
    send_same(ob_right, pair_sem.at[3], col_chip, own_i, send_sem.at[13])
    mixing = contract(
        o_left, pair_sem.at[0], own_j, False, o_right, pair_sem.at[1], None, own_j
    )
    mixing_out[...] = mixing
    normed, unused = layer_norm(mixing)
    update = dot(normed.astype(BF16), out_out_weight[...])
    second[...] = (first[...] + gates(proj_out[...], 4) * update).astype(BF16).astype(F32)

    normed, unused = layer_norm(second[...])
    projected = dot(normed.astype(BF16), in_in_weight[...])
    proj_in[...] = projected
    i_right[own_i] = blocked(gates(projected, 2) * channels(projected, 3))
    send_same(i_right, pair_sem.at[4], col_chip, own_i, send_sem.at[14])
    i_left_stage[...] = blocked(gates(projected, 0) * channels(projected, 1))
    send_other(i_left_stage, i_left, pair_sem.at[5], col_chip, own_i, send_sem.at[15])
    ib_right[own_j] = i_right[own_i]
    ib_left[own_j] = i_left_stage[...]
    send_same(ib_right, pair_sem.at[6], row_chip, own_j, send_sem.at[16])
    send_same(ib_left, pair_sem.at[7], row_chip, own_j, send_sem.at[17])
    mixing = contract(
        i_left, pair_sem.at[5], None, True, i_right, pair_sem.at[4], own_i, own_i
    )
    normed, scale = layer_norm(mixing)
    update = dot(normed.astype(BF16), in_out_weight[...])
    gating = gates(proj_in[...], 4)
    result = (second[...] + gating * update).astype(BF16)

    def output_pullback(normed, scale, update, gating, weight, upstream):
        update_cot = (upstream * gating).astype(BF16)
        normed_cot = dot(update_cot, weight[...], ((1,), (1,)))
        mixing_cot = layer_norm_pullback(normed, scale, normed_cot)
        return mixing_cot, upstream * update * gating * (1.0 - gating)

    def input_pullback(projected, left_cot, right_cot, gating_cot, weight, inputs, upstream):
        left_gate, right_gate = gates(projected, 0), gates(projected, 2)
        left_part, right_part = left_cot * left_gate, right_cot * right_gate
        pieces = [
            left_part * channels(projected, 1) * (1.0 - left_gate),
            left_part,
            right_part * channels(projected, 3) * (1.0 - right_gate),
            right_part,
            gating_cot,
        ]
        proj_cot = jnp.concatenate([piece.astype(BF16) for piece in pieces], axis=1)
        normed_cot = dot(proj_cot, weight[...], ((1,), (1,)))
        normed, scale = layer_norm(inputs)
        return upstream + layer_norm_pullback(normed, scale, normed_cot)

    upstream = cot_block[...].reshape(BLOCK * BLOCK, WIDTH).astype(F32)
    mixing_cot, gating_cot = output_pullback(
        normed, scale, update, gating, in_out_weight, upstream
    )
    ib_cot[own_i] = blocked(mixing_cot)
    send_same(ib_cot, pair_sem.at[8], col_chip, own_i, send_sem.at[18])

    def store_cot(j, value):
        ib_cot_stage[j] = value

    turned(mixing_cot, store_cot)
    send_other(ib_cot_stage, ib_cot_turned, pair_sem.at[9], row_chip, own_j, send_sem.at[19])

    @pl.when(h == 0)
    def _():
        pair_output[...] = result[: BLOCK * BLOCK // 2].reshape(8, BLOCK, WIDTH)
        output_stage[...] = result[BLOCK * BLOCK // 2 :].reshape(8, BLOCK, WIDTH)
        remote(output_stage, output_got, send_sem.at[20], small_sem.at[0], (a, b), 1).start()

    line_slot = b

    def rows_send(src, core, send):
        target = msa_rows.at[line_slot, pl.ds(pl.multiple_of(h * 64, 64), 64)]

        def step(k, carry):
            @pl.when(jnp.logical_or(k > 0, h != core))
            def _():
                remote(
                    src, target, send, rows_sem.at[line_slot, h], (a, (b + k) % GRID), core
                ).start()

            return carry

        lax.fori_loop(0, GRID, step, 0)

        @pl.when(h == core)
        def _():
            pltpu.make_async_copy(src, target, rows_sem.at[line_slot, h]).start()

    rows_send(left_ci, 0, send_sem.at[21])

    left_cot = contract(
        ib_right,
        pair_sem.at[6],
        own_j,
        False,
        ib_cot_turned,
        pair_sem.at[9],
        None,
        own_j,
    )
    upstream32[...] = left_cot
    right_cot = contract(
        ib_left, pair_sem.at[7], own_j, False, ib_cot, pair_sem.at[8], own_i, own_j
    )
    second_cot = input_pullback(
        proj_in[...],
        upstream32[...],
        right_cot,
        gating_cot,
        in_in_weight,
        second[...],
        upstream,
    )
    upstream32[...] = second_cot

    normed, scale = layer_norm(mixing_out[...])
    update = dot(normed.astype(BF16), out_out_weight[...])
    mixing_cot, gating_cot = output_pullback(
        normed, scale, update, gates(proj_out[...], 4), out_out_weight, second_cot
    )
    ob_cot_row[own_j] = blocked(mixing_cot)
    send_same(ob_cot_row, pair_sem.at[10], row_chip, own_j, send_sem.at[22])
    ob_cot_stage[...] = blocked(mixing_cot)
    send_other(ob_cot_stage, ob_cot_col, pair_sem.at[11], col_chip, own_i, send_sem.at[23])
    rows_send(right_dj, 1, send_sem.at[24])
    left_cot = contract(
        ob_cot_row, pair_sem.at[10], own_j, False, ob_right, pair_sem.at[3], own_i, own_j
    )
    flat[...] = left_cot
    right_cot = contract(
        ob_cot_col, pair_sem.at[11], None, True, ob_left, pair_sem.at[2], own_i, own_i
    )
    gradient = input_pullback(
        proj_out[...],
        flat[...],
        right_cot,
        gating_cot,
        out_in_weight,
        first[...],
        upstream32[...],
    )

    @pl.when(h == 0)
    def _():
        pair_gradient[...] = gradient[: BLOCK * BLOCK // 2].reshape(8, BLOCK, WIDTH)
        gradient_stage[...] = gradient[BLOCK * BLOCK // 2 :].reshape(8, BLOCK, WIDTH)
        remote(
            gradient_stage, gradient_got, send_sem.at[25], small_sem.at[1], (a, b), 1
        ).start()
        flat[...] = gradient
        for j in range(BLOCK):
            final_cot[a, j] = flat[pl.ds(j, BLOCK, stride=BLOCK), :].astype(BF16)

    @pl.when(h == 1)
    def _():
        final_cot[a] = blocked(gradient)

    send_same(final_cot, final_sem, column, a, send_sem.at[26])

    weight_copy.wait()

    def final_wait(k, carry):
        slot = (a + k) % GRID
        wait_for(final_cot.at[slot], final_sem.at[slot])
        return carry

    lax.fori_loop(1, GRID, final_wait, 0)
    for g in range(4):
        for q in range(4):
            stacked[g * WIDTH : (g + 1) * WIDTH, q * WIDTH : (q + 1) * WIDTH] = final_cot[
                :, 4 * g + q
            ].reshape(WIDTH, WIDTH)

    def table_step(x2, carry):
        at = pl.multiple_of(x2 * 2 * WIDTH, 2 * WIDTH)
        chunk = dot(stacked[...], spread_weight[:, pl.ds(at, 2 * WIDTH)]).astype(BF16)
        for part in range(2):
            start = pl.multiple_of((2 * x2 + part) * BLOCK, BLOCK)
            for g in range(4):
                grad_table[:, pl.ds(start, BLOCK), g * WIDTH : (g + 1) * WIDTH] = chunk[
                    g * WIDTH : (g + 1) * WIDTH, part * WIDTH : (part + 1) * WIDTH
                ].reshape(GRID, BLOCK, WIDTH)
        return carry

    lax.fori_loop(0, HIDDEN // 2, table_step, 0)

    def rows_wait(n, carry):
        for part in range(2):
            wait_for(msa_rows.at[n, pl.ds(part * 64, 64)], rows_sem.at[n, part])
        return carry

    lax.fori_loop(0, GRID, rows_wait, 0)

    def cot_step(n, total):
        return total + dot(msa_rows[n], grad_table[n])

    total = lax.fori_loop(0, GRID, cot_step, jnp.zeros((128, BLOCK * HIDDEN), F32))
    msa_cot_own[...] = (total * (1.0 / SEQUENCES)).astype(BF16)
    remote(
        msa_cot_own.at[pl.ds(pl.multiple_of(other * 64, 64), 64)],
        msa_cot_got,
        send_sem.at[27],
        small_sem.at[2],
        (a, b),
        other,
    ).start()
    msa_cots[other] = msa_cot_own[pl.ds(pl.multiple_of(h * 64, 64), 64), :]
    wait_for(msa_cot_got, small_sem.at[2])
    msa_cots[h] = msa_cot_got[...]

    @pl.when(h == 1)
    def _():
        wait_for(output_got, small_sem.at[0])
        pair_output[...] = output_got[...]
        wait_for(gradient_got, small_sem.at[1])
        pair_gradient[...] = gradient_got[...]

    @pl.when(jnp.logical_not(diagonal))
    def _():
        wait_for(relay_left, send_sem.at[0])
        wait_for(relay_right, send_sem.at[1])

    msa_sent(right_dj, msa_right, 0, send_sem.at[2])
    msa_sent(left_ic, msa_left, 1, send_sem.at[3])
    block_sent(0, pair_input)
    block_sent(1, cotangent)
    msa_sent(relay_left, msa_left, 0, send_sem.at[8])
    msa_sent(relay_right, msa_right, 1, send_sem.at[9])
    for at in (10, 12, 13, 14, 16, 17, 18, 22, 26):
        wait_for(o_left.at[pl.ds(0, 7)], send_sem.at[at])
    for at in (11, 15, 19, 23):
        wait_for(o_left, send_sem.at[at])
    msa_sent(left_ci, msa_left, 0, send_sem.at[21])
    msa_sent(right_dj, msa_left, 1, send_sem.at[24])
    wait_for(msa_cot_got, send_sem.at[27])

    @pl.when(h == 0)
    def _():
        wait_for(output_stage, send_sem.at[20])
        wait_for(gradient_stage, send_sem.at[25])


def pair_updates(left_ic, left_ci, right_dj, pair_input, cotangent, outer_weight, spread, weights):
    gathered = pltpu.VMEM((GRID, BLOCK, BLOCK, WIDTH), BF16)
    block = pltpu.VMEM((BLOCK, BLOCK, WIDTH), BF16)
    flat = pltpu.VMEM((BLOCK * BLOCK, WIDTH), F32)
    shares = pltpu.VMEM((64, BLOCK * HIDDEN), BF16)
    all_sequences = pltpu.VMEM((2 * GRID, 64, BLOCK * HIDDEN), BF16)
    half_block = pltpu.VMEM((8, BLOCK, WIDTH), BF16)
    half_wide = pltpu.VMEM((8, BLOCK, WIDTH), F32)
    projected = pltpu.VMEM((BLOCK * BLOCK, 5 * WIDTH), F32)
    dma = pltpu.SemaphoreType.DMA
    vmem = pl.BlockSpec(memory_space=pltpu.VMEM)
    return pl.pallas_call(
        pair_kernel,
        out_shape=(
            jax.ShapeDtypeStruct((8, BLOCK, WIDTH), BF16),
            jax.ShapeDtypeStruct((8, BLOCK, WIDTH), F32),
            jax.ShapeDtypeStruct((2, 64, BLOCK * HIDDEN), BF16),
        ),
        in_specs=[vmem] * 6 + [pl.BlockSpec(memory_space=pl.ANY)] + [vmem] * 4,
        out_specs=(vmem, vmem, vmem),
        scratch_shapes=[
            block,
            block,
            shares,
            shares,
            all_sequences,
            all_sequences,
            pltpu.VMEM((GRID, 128, BLOCK * HIDDEN), BF16),
            gathered,
            gathered,
            block,
            gathered,
            gathered,
            block,
            gathered,
            gathered,
            gathered,
            gathered,
            block,
            gathered,
            gathered,
            gathered,
            gathered,
            block,
            gathered,
            pltpu.VMEM((4 * WIDTH, HIDDEN * WIDTH), BF16),
            pltpu.VMEM((BLOCK * HIDDEN, BLOCK * HIDDEN), F32),
            pltpu.VMEM((BLOCK, BLOCK, WIDTH), F32),
            flat,
            projected,
            projected,
            flat,
            flat,
            flat,
            flat,
            pltpu.VMEM((4 * WIDTH, 4 * WIDTH), BF16),
            pltpu.VMEM((GRID, BLOCK * HIDDEN, BLOCK * HIDDEN), BF16),
            pltpu.VMEM((128, BLOCK * HIDDEN), BF16),
            shares,
            half_block,
            half_block,
            half_wide,
            half_wide,
            dma((2,)),
            dma((2, 2)),
            dma((2, 2 * GRID)),
            dma((GRID, 2)),
            dma((12, GRID)),
            dma((GRID,)),
            dma((3,)),
            dma((28,)),
            dma(()),
        ],
        compiler_params=pltpu.CompilerParams(
            collective_id=1, has_side_effects=True, vmem_limit_bytes=48 << 20
        ),
        name="pair_updates",
    )(left_ic, left_ci, right_dj, pair_input, cotangent, outer_weight, spread, *weights)


def body(
    homolog_features,
    pair_input,
    cotangent,
    homolog_factor_matrix,
    outer_output_weight,
    outgoing_input_weight,
    outgoing_output_weight,
    incoming_input_weight,
    incoming_output_weight,
):
    sequences, residues, depth = homolog_features.shape
    core = lax.axis_index("row") % 2
    normed, scale = layer_norm(homolog_features.astype(F32))
    projected = jnp.dot(
        normed.astype(BF16), homolog_factor_matrix, preferred_element_type=F32
    ).astype(BF16)
    left, right = projected[..., :HIDDEN], projected[..., HIDDEN:]
    left_ic = left.reshape(sequences, residues * HIDDEN)
    left_ci = left.transpose(0, 2, 1).reshape(sequences, residues * HIDDEN)
    right_dj = right.transpose(0, 2, 1).reshape(sequences, residues * HIDDEN)
    cube = outer_output_weight.reshape(HIDDEN, HIDDEN, WIDTH)
    outer_weight = jnp.broadcast_to(
        cube.transpose(1, 0, 2)[:, None], (HIDDEN, 4, HIDDEN, WIDTH)
    ).reshape(4 * HIDDEN * HIDDEN, WIDTH)
    picked = jnp.where(core == 0, cube.transpose(2, 0, 1), cube.transpose(2, 1, 0))
    spread = (
        jnp.eye(4, dtype=BF16)[:, None, None, :, None] * picked[None, :, :, None, :]
    ).reshape(4 * WIDTH, HIDDEN * WIDTH)
    pair_output, pair_gradient, cots = pair_updates(
        left_ic,
        left_ci,
        right_dj,
        pair_input,
        cotangent,
        outer_weight,
        spread,
        (
            outgoing_input_weight,
            outgoing_output_weight,
            incoming_input_weight,
            incoming_output_weight,
        ),
    )
    cots = cots.reshape(2, sequences, residues, HIDDEN)
    projection_cot = jnp.concatenate([cots[0], cots[1]], axis=-1)
    normed_cot = jnp.dot(
        projection_cot, homolog_factor_matrix.T, preferred_element_type=F32
    )
    normed, scale = layer_norm(homolog_features.astype(F32))
    alignment_gradient = layer_norm_pullback(normed, scale, normed_cot)
    return pair_output, pair_gradient, alignment_gradient


def solution(mesh):
    split = P("row", "col", None)
    return jax.shard_map(
        body,
        mesh=mesh,
        in_specs=(split, split, split, P(), P(), P(), P(), P(), P()),
        out_specs=(split, split, split),
        check_vma=False,
    )
```

```python
import jax
import jax.numpy as jnp
from jax import lax
from jax.experimental import pallas as pl
from jax.experimental.pallas import tpu as pltpu
from jax.sharding import PartitionSpec as P

SEQUENCES = 1024
EPSILON = 1e-05
MESH = pl.DeviceIdType.MESH
F32 = jnp.float32
BF16 = jnp.bfloat16
GRID = 8
BLOCK = 16
WIDTH = 128
HIDDEN = 32


def dot(lhs, rhs, dims=((1,), (0,))):
    return lax.dot_general(lhs, rhs, (dims, ((), ())), preferred_element_type=F32)


def layer_norm(inputs):
    centered = inputs - jnp.mean(inputs, axis=-1, keepdims=True)
    spread = jnp.mean(centered * centered, axis=-1, keepdims=True)
    scale = lax.rsqrt(spread + EPSILON)
    return centered * scale, scale


def layer_norm_pullback(normed, scale, upstream):
    along = jnp.mean(upstream * normed, axis=-1, keepdims=True)
    return scale * (upstream - jnp.mean(upstream, axis=-1, keepdims=True) - normed * along)


def pair_kernel(
    left_ic,
    left_ci,
    right_dj,
    pair_input,
    cotangent,
    outer_weight,
    out_in_weight,
    out_out_weight,
    in_in_weight,
    in_out_weight,
    pair_output,
    pair_gradient,
    msa_cots,
    pair_block,
    cot_block,
    relay_left,
    relay_right,
    msa_left,
    msa_right,
    msa_rows,
    o_left,
    o_right,
    o_right_stage,
    i_left,
    i_right,
    i_left_stage,
    ib_right,
    ib_left,
    ob_right,
    ob_left,
    left_parts,
    right_parts,
    left_parts2,
    right_parts2,
    final_cot,
    wide_weight,
    table_weight,
    spread_weight,
    outer32,
    wide,
    cot_wide,
    cot_turned,
    flat,
    proj_out,
    proj_in,
    mixing_out,
    first,
    second,
    upstream32,
    stacked,
    grad_table,
    msa_cot_own,
    msa_cot_got,
    output_stage,
    output_got,
    gradient_stage,
    gradient_got,
    relay_sem,
    block_sem,
    msa_sem,
    rows_sem,
    pair_sem,
    final_sem,
    small_sem,
    send_sem,
    output_sem,
    gradient_sem,
):
    row, col = lax.axis_index("row"), lax.axis_index("col")
    a, h, b = row // 2, row % 2, col
    other = 1 - h
    odd = b % 2
    at = (a + 4 * odd) % GRID
    own_i = at * other + b * h
    own_j = b * other + at * h
    stays = jnp.logical_and(a == b, odd == 0)

    def chip_at(i, j):
        return (i + 4 * (j % 2)) % GRID, j

    def row_chip(n):
        return chip_at(at * other + n * h, n * other + b * h)

    def col_chip(n):
        return chip_at(n * other + at * h, b * other + n * h)

    def column(n):
        return n, b

    def line(n):
        return chip_at(at, n)

    def remote(src, dst, send, recv, chip, core):
        return pltpu.make_async_remote_copy(
            src_ref=src,
            dst_ref=dst,
            send_sem=send,
            recv_sem=recv,
            device_id=(2 * chip[0] + core, chip[1]),
            device_id_type=MESH,
        )

    def wait_for(ref, sem):
        pltpu.make_async_copy(ref, ref, sem).wait()

    barrier = pltpu.get_barrier_semaphore()

    def greet(chip, core):
        pl.semaphore_signal(
            barrier, inc=1, device_id=(2 * chip[0] + core, chip[1]), device_id_type=MESH
        )

    def greet_step(k, carry):
        for core in range(2):
            greet(column((a + k) % GRID), core)
            greet(line((b + k) % GRID), core)
        return carry

    def greet_across(k, carry):
        for core in range(2):
            greet((a, 2 * k + 1 - odd), core)
        return carry

    lax.fori_loop(1, GRID, greet_step, 0)
    lax.fori_loop(0, GRID // 2, greet_across, 0)
    greet((a, b), other)

    @pl.when(jnp.logical_not(stays))
    def _():
        greet((b, at), 0)
        greet((b, at), 1)

    wide_weight[...] = outer_weight[...].astype(F32)
    spread_weight[...] = jnp.zeros(spread_weight.shape, BF16)

    def weight_step(n, carry):
        by_d = wide_weight[pl.ds(n, HIDDEN, stride=HIDDEN), :].astype(BF16)
        start = pl.multiple_of(n * WIDTH, WIDTH)
        for q in range(4):
            table_weight[pl.ds(start + q * HIDDEN, HIDDEN), :] = by_d

        def spread(piece):
            for q in range(4):
                spread_weight[
                    pl.ds(start + q * HIDDEN, HIDDEN), q * WIDTH : (q + 1) * WIDTH
                ] = piece

        @pl.when(h == 0)
        def _():
            spread(outer_weight[pl.ds(pl.multiple_of(n * HIDDEN, HIDDEN), HIDDEN), :])

        @pl.when(h == 1)
        def _():
            spread(by_d)

        return carry

    lax.fori_loop(0, HIDDEN, weight_step, 0)

    @pl.when(jnp.logical_not(stays))
    def _():
        pl.semaphore_wait(barrier, 39)

    @pl.when(stays)
    def _():
        pl.semaphore_wait(barrier, 37)

    for slot, (src, dst) in enumerate(((left_ic, relay_left), (right_dj, relay_right))):

        @pl.when(jnp.logical_not(stays))
        def _():
            remote(src, dst, send_sem.at[slot], relay_sem.at[slot], chip_at(b, a), h).start()

        @pl.when(stays)
        def _():
            pltpu.make_async_copy(src, dst, relay_sem.at[slot]).start()

    def msa_send(src, dst, sems, slot, chips, own, core, send):
        def step(k, carry):
            n = (own + k) % GRID

            @pl.when(jnp.logical_or(k > 0, h != core))
            def _():
                remote(src, dst.at[slot], send, sems.at[slot], chips(n), core).start()

            return carry

        lax.fori_loop(0, GRID, step, 0)

        @pl.when(h == core)
        def _():
            pltpu.make_async_copy(src, dst.at[slot], sems.at[slot]).start()

    def msa_sent(src, dst, core, send):
        @pl.when(h == core)
        def _():
            wait_for(dst.at[pl.ds(0, 7)], send)

        @pl.when(h != core)
        def _():
            wait_for(dst.at[pl.ds(0, 8)], send)

    msa_send(right_dj, msa_right, msa_sem.at[1], row, column, a, 0, send_sem.at[2])
    msa_send(left_ic, msa_left, msa_sem.at[0], row, column, a, 1, send_sem.at[3])

    keeps_first = jnp.logical_and(h == 0, odd == 0)
    keeps_second = jnp.logical_and(h == 1, stays)
    for slot, (src, dst) in enumerate(((pair_input, pair_block), (cotangent, cot_block))):
        half = dst.at[pl.ds(h * 8, 8)]
        sem = block_sem.at[slot, h]

        @pl.when(keeps_first)
        def _():
            pltpu.make_async_copy(src, half, sem).start()

        @pl.when(jnp.logical_not(keeps_first))
        def _():
            remote(src, half, send_sem.at[4 + slot], sem, chip_at(a, b), 0).start()

        @pl.when(keeps_second)
        def _():
            pltpu.make_async_copy(src, half, sem).start()

        @pl.when(jnp.logical_not(keeps_second))
        def _():
            remote(src, half, send_sem.at[6 + slot], sem, chip_at(b, a), 1).start()

    def block_sent(slot, src):
        @pl.when(jnp.logical_not(keeps_first))
        def _():
            wait_for(src, send_sem.at[4 + slot])

        @pl.when(jnp.logical_not(keeps_second))
        def _():
            wait_for(src, send_sem.at[6 + slot])

    relay_slot = 2 * b + h
    wait_for(relay_left, relay_sem.at[0])
    msa_send(relay_left, msa_left, msa_sem.at[0], relay_slot, line, b, 0, send_sem.at[8])
    wait_for(relay_right, relay_sem.at[1])
    msa_send(relay_right, msa_right, msa_sem.at[1], relay_slot, line, b, 1, send_sem.at[9])

    def msa_wait(n, carry):
        wait_for(msa_left.at[n], msa_sem.at[0, n])
        wait_for(msa_right.at[n], msa_sem.at[1, n])
        return carry

    lax.fori_loop(0, 2 * GRID, msa_wait, 0)
    everything = msa_left[...].reshape(SEQUENCES, BLOCK * HIDDEN)
    outer32[...] = dot(
        msa_right[...].reshape(SEQUENCES, BLOCK * HIDDEN), everything, ((0,), (0,))
    ) * (1.0 / SEQUENCES)
    lane_part = lax.broadcasted_iota(jnp.int32, (BLOCK, WIDTH), 1) // HIDDEN

    def project_step(d2, total):
        columns = []
        for part in range(2):
            tile = outer32[pl.ds(pl.multiple_of((2 * d2 + part) * BLOCK, BLOCK), BLOCK), :]
            columns.append(
                jnp.concatenate(
                    [
                        jnp.where(lane_part == q, tile[:, g * WIDTH : (g + 1) * WIDTH], 0.0)
                        for q in range(4)
                        for g in range(4)
                    ],
                    axis=0,
                )
            )
        picked = jnp.concatenate(columns, axis=1).astype(BF16)
        weight = table_weight[pl.ds(pl.multiple_of(d2 * 2 * WIDTH, 2 * WIDTH), 2 * WIDTH), :]
        return total + dot(picked, weight)

    projected = lax.fori_loop(
        0, HIDDEN // 2, project_step, jnp.zeros((BLOCK * BLOCK, WIDTH), F32)
    )
    for part in range(2):
        wait_for(pair_block.at[pl.ds(part * 8, 8)], block_sem.at[0, part])
        wait_for(cot_block.at[pl.ds(part * 8, 8)], block_sem.at[1, part])
    for i in range(BLOCK):
        start = ((i % 4) * 4 + i // 4) * BLOCK
        first[pl.ds(i * BLOCK, BLOCK), :] = (
            (pair_block[i].astype(F32) + projected[start : start + BLOCK]).astype(BF16).astype(F32)
        )

    def rows_send(src, core, send, first_step, last_step):
        target = msa_rows.at[b, pl.ds(pl.multiple_of(h * 64, 64), 64)]

        def step(k, carry):
            @pl.when(jnp.logical_or(k > 0, h != core))
            def _():
                remote(
                    src, target, send, rows_sem.at[b, h], (a, (b + k) % GRID), core
                ).start()

            return carry

        lax.fori_loop(first_step, last_step, step, 0)

        if first_step == 0:

            @pl.when(h == core)
            def _():
                pltpu.make_async_copy(src, target, rows_sem.at[b, h]).start()

    def send_same(dst, sems, chips, own, send):
        def step(k, carry):
            remote(
                dst.at[own], dst.at[own], send, sems.at[own], chips((own + k) % GRID), h
            ).start()
            return carry

        lax.fori_loop(1, GRID, step, 0)

    def send_other(src, dst, sems, chips, own, send):
        def step(k, carry):
            remote(
                src, dst.at[own], send, sems.at[own], chips((own + k) % GRID), other
            ).start()
            return carry

        lax.fori_loop(0, GRID, step, 0)

    def block_product(totals, left, by_column, right):
        def inner(group, totals):
            totals = list(totals)
            for u in range(4):
                t = group * 4 + u
                across = right(t)
                for p in range(BLOCK):
                    one = left[t, pl.ds(p, 1), :] if by_column else left[p, pl.ds(t, 1), :]
                    totals[p] = totals[p] + one * across
            return tuple(totals)

        return lax.fori_loop(0, BLOCK // 4, inner, totals)

    def no_totals():
        return tuple(jnp.zeros((BLOCK, WIDTH), F32) for _ in range(BLOCK))

    def contract(left, left_sem, left_own, by_column, right, right_sem, right_own, own):
        def arrive(ref, sems, slot, skip):
            if skip is None:
                wait_for(ref.at[slot], sems.at[slot])
            else:

                @pl.when(slot != skip)
                def _():
                    wait_for(ref.at[slot], sems.at[slot])

        def block_step(k, totals):
            slot = (own + k) % GRID
            arrive(left, left_sem, slot, left_own)
            arrive(right, right_sem, slot, right_own)
            wide[...] = left[slot].astype(F32)
            return block_product(totals, wide, by_column, lambda t: right[slot, t].astype(F32))

        totals = lax.fori_loop(0, GRID, block_step, no_totals())
        return jnp.concatenate(totals, axis=0)

    def partial(part, n, totals):
        for p in range(BLOCK):
            part[n, p] = totals[p].astype(BF16)

    def sum_of(parts, sems, skip, own):
        def step(k, total):
            slot = (own + k) % GRID
            if skip is None:
                wait_for(parts.at[slot], sems.at[slot])
            else:

                @pl.when(slot != skip)
                def _():
                    wait_for(parts.at[slot], sems.at[slot])

            return total + parts[slot].reshape(BLOCK * BLOCK, WIDTH).astype(F32)

        return lax.fori_loop(0, GRID, step, jnp.zeros((BLOCK * BLOCK, WIDTH), F32))

    def send_part(part, n, dst, slot, sems, chips, core, send):
        remote(part.at[n], dst.at[slot], send, sems.at[slot], chips(n), core).start()

    def turned(value, store):
        flat[...] = value
        for j in range(BLOCK):
            store(j, flat[pl.ds(j, BLOCK, stride=BLOCK), :].astype(BF16))

    def turn_cot(value):
        rounded = value.astype(BF16).astype(F32)
        cot_wide[...] = rounded.reshape(BLOCK, BLOCK, WIDTH)
        flat[...] = rounded
        for j in range(BLOCK):
            cot_turned[j] = flat[pl.ds(j, BLOCK, stride=BLOCK), :]

    def blocked(value):
        return value.astype(BF16).reshape(BLOCK, BLOCK, WIDTH)

    def gates(projected, at):
        return jax.nn.sigmoid(projected[:, at * WIDTH : (at + 1) * WIDTH])

    def channels(projected, at):
        return projected[:, at * WIDTH : (at + 1) * WIDTH]

    normed, unused = layer_norm(first[...])
    projected = dot(normed.astype(BF16), out_in_weight[...])
    proj_out[...] = projected
    o_left[own_j] = blocked(gates(projected, 0) * channels(projected, 1))
    send_same(o_left, pair_sem.at[0], row_chip, own_j, send_sem.at[10])
    right = gates(projected, 2) * channels(projected, 3)

    def store_right(j, value):
        o_right_stage[j] = value

    turned(right, store_right)
    send_other(o_right_stage, o_right, pair_sem.at[1], row_chip, own_j, send_sem.at[11])
    rows_send(left_ci, 0, send_sem.at[21], 0, 4)
    mixing = contract(
        o_left, pair_sem.at[0], own_j, False, o_right, pair_sem.at[1], None, own_j
    )
    mixing_out[...] = mixing
    normed, unused = layer_norm(mixing)
    update = dot(normed.astype(BF16), out_out_weight[...])
    second[...] = (first[...] + gates(proj_out[...], 4) * update).astype(BF16).astype(F32)

    normed, unused = layer_norm(second[...])
    projected = dot(normed.astype(BF16), in_in_weight[...])
    proj_in[...] = projected
    i_right[own_i] = blocked(gates(projected, 2) * channels(projected, 3))
    send_same(i_right, pair_sem.at[4], col_chip, own_i, send_sem.at[14])
    i_left_stage[...] = blocked(gates(projected, 0) * channels(projected, 1))
    send_other(i_left_stage, i_left, pair_sem.at[5], col_chip, own_i, send_sem.at[15])
    rows_send(left_ci, 0, send_sem.at[21], 4, 8)
    mixing = contract(
        i_left, pair_sem.at[5], None, True, i_right, pair_sem.at[4], own_i, own_i
    )
    normed, scale = layer_norm(mixing)
    update = dot(normed.astype(BF16), in_out_weight[...])
    gating = gates(proj_in[...], 4)
    result = (second[...] + gating * update).astype(BF16)

    def output_pullback(normed, scale, update, gating, weight, upstream):
        update_cot = (upstream * gating).astype(BF16)
        normed_cot = dot(update_cot, weight[...], ((1,), (1,)))
        mixing_cot = layer_norm_pullback(normed, scale, normed_cot)
        return mixing_cot, upstream * update * gating * (1.0 - gating)

    def input_pullback(projected, left_cot, right_cot, gating_cot, weight, inputs, upstream):
        left_gate, right_gate = gates(projected, 0), gates(projected, 2)
        left_part, right_part = left_cot * left_gate, right_cot * right_gate
        pieces = [
            left_part * channels(projected, 1) * (1.0 - left_gate),
            left_part,
            right_part * channels(projected, 3) * (1.0 - right_gate),
            right_part,
            gating_cot,
        ]
        proj_cot = jnp.concatenate([piece.astype(BF16) for piece in pieces], axis=1)
        normed_cot = dot(proj_cot, weight[...], ((1,), (1,)))
        normed, scale = layer_norm(inputs)
        return upstream + layer_norm_pullback(normed, scale, normed_cot)

    upstream = cot_block[...].reshape(BLOCK * BLOCK, WIDTH).astype(F32)
    mixing_cot, gating_cot = output_pullback(
        normed, scale, update, gating, in_out_weight, upstream
    )
    turn_cot(mixing_cot)

    def incoming_step(k, carry):
        n = (own_i + 1 + k) % GRID
        wide[...] = i_right[n].astype(F32)
        totals = block_product(no_totals(), wide, False, lambda t: cot_turned[t])
        partial(left_parts, n, totals)
        send_part(
            left_parts, n, ib_left, own_j, pair_sem.at[2], row_chip, other, send_sem.at[12]
        )
        wide[...] = i_left[n].astype(F32)
        totals = block_product(no_totals(), wide, False, lambda t: cot_wide[t])

        @pl.when(n != own_i)
        def _():
            partial(right_parts, n, totals)
            send_part(
                right_parts, n, ib_right, own_i, pair_sem.at[3], col_chip, h, send_sem.at[13]
            )

        @pl.when(n == own_i)
        def _():
            partial(ib_right, n, totals)

        return carry

    lax.fori_loop(0, GRID, incoming_step, 0)
    rows_send(right_dj, 1, send_sem.at[24], 0, 4)

    def hand_over(value, stage, got, sem, send):
        stage[...] = value.reshape(2, 8, BLOCK, WIDTH)
        for part in range(2):
            order = remote(stage.at[part], got, send.at[part], sem, (at, b), part)
            if part == 0:
                pl.when(odd == 1)(order.start)
            else:
                order.start()

    @pl.when(h == 0)
    def _():
        hand_over(result, output_stage, output_got, small_sem.at[0], output_sem)

    upstream32[...] = sum_of(ib_left, pair_sem.at[2], None, own_j)
    right_cot = sum_of(ib_right, pair_sem.at[3], own_i, own_i)
    second_cot = input_pullback(
        proj_in[...],
        upstream32[...],
        right_cot,
        gating_cot,
        in_in_weight,
        second[...],
        upstream,
    )
    upstream32[...] = second_cot

    normed, scale = layer_norm(mixing_out[...])
    update = dot(normed.astype(BF16), out_out_weight[...])
    mixing_cot, gating_cot = output_pullback(
        normed, scale, update, gates(proj_out[...], 4), out_out_weight, second_cot
    )
    turn_cot(mixing_cot)

    def outgoing_step(k, carry):
        n = (own_j + 1 + k) % GRID
        wide[...] = o_right[n].astype(F32)
        totals = block_product(no_totals(), wide, False, lambda t: cot_turned[t])

        @pl.when(n != own_j)
        def _():
            partial(left_parts2, n, totals)
            send_part(
                left_parts2, n, ob_left, own_j, pair_sem.at[6], row_chip, h, send_sem.at[16]
            )

        @pl.when(n == own_j)
        def _():
            partial(ob_left, n, totals)

        totals = block_product(
            no_totals(), cot_wide, True, lambda t: o_left[n, t].astype(F32)
        )
        partial(right_parts2, n, totals)
        send_part(
            right_parts2, n, ob_right, own_i, pair_sem.at[7], col_chip, other, send_sem.at[17]
        )
        return carry

    lax.fori_loop(0, GRID, outgoing_step, 0)
    rows_send(right_dj, 1, send_sem.at[24], 4, 8)
    left_turned = sum_of(ob_left, pair_sem.at[6], own_j, own_j)
    right_cot = sum_of(ob_right, pair_sem.at[7], None, own_i)
    flat[...] = left_turned
    for j in range(BLOCK):
        mixing_out[pl.ds(j * BLOCK, BLOCK), :] = flat[pl.ds(j, BLOCK, stride=BLOCK), :]
    gradient = input_pullback(
        proj_out[...],
        mixing_out[...],
        right_cot,
        gating_cot,
        out_in_weight,
        first[...],
        upstream32[...],
    )

    @pl.when(h == 0)
    def _():
        hand_over(gradient, gradient_stage, gradient_got, small_sem.at[1], gradient_sem)
        flat[...] = gradient
        for j in range(BLOCK):
            final_cot[at, j] = flat[pl.ds(j, BLOCK, stride=BLOCK), :].astype(BF16)

    @pl.when(h == 1)
    def _():
        final_cot[at] = blocked(gradient)

    def final_chip(n):
        return chip_at(n, b)

    send_same(final_cot, final_sem, final_chip, at, send_sem.at[26])

    def final_wait(k, carry):
        slot = (at + k) % GRID
        wait_for(final_cot.at[slot], final_sem.at[slot])
        return carry

    lax.fori_loop(1, GRID, final_wait, 0)
    for g in range(4):
        for q in range(4):
            stacked[g * WIDTH : (g + 1) * WIDTH, q * WIDTH : (q + 1) * WIDTH] = final_cot[
                :, 4 * g + q
            ].reshape(WIDTH, WIDTH)

    def table_step(x2, carry):
        begin = pl.multiple_of(x2 * 2 * WIDTH, 2 * WIDTH)
        chunk = dot(
            stacked[...], spread_weight[pl.ds(begin, 2 * WIDTH), :], ((1,), (1,))
        ).astype(BF16)
        for part in range(2):
            start = pl.multiple_of((2 * x2 + part) * BLOCK, BLOCK)
            for g in range(4):
                grad_table[:, pl.ds(start, BLOCK), g * WIDTH : (g + 1) * WIDTH] = chunk[
                    g * WIDTH : (g + 1) * WIDTH, part * WIDTH : (part + 1) * WIDTH
                ].reshape(GRID, BLOCK, WIDTH)
        return carry

    lax.fori_loop(0, HIDDEN // 2, table_step, 0)

    def rows_wait(n, carry):
        for part in range(2):
            wait_for(msa_rows.at[n, pl.ds(part * 64, 64)], rows_sem.at[n, part])
        return carry

    lax.fori_loop(0, GRID, rows_wait, 0)

    def cot_step(n, total):
        return total + dot(msa_rows[n], grad_table[n])

    total = lax.fori_loop(0, GRID, cot_step, jnp.zeros((128, BLOCK * HIDDEN), F32))
    msa_cot_own[...] = (total * (1.0 / SEQUENCES)).astype(BF16)
    remote(
        msa_cot_own.at[pl.ds(pl.multiple_of(other * 64, 64), 64)],
        msa_cot_got,
        send_sem.at[27],
        small_sem.at[2],
        (a, b),
        other,
    ).start()
    msa_cots[other] = msa_cot_own[pl.ds(pl.multiple_of(h * 64, 64), 64), :]
    wait_for(msa_cot_got, small_sem.at[2])
    msa_cots[h] = msa_cot_got[...]

    @pl.when(keeps_first)
    def _():
        pair_output[...] = output_stage[0]
        pair_gradient[...] = gradient_stage[0]

    @pl.when(jnp.logical_not(keeps_first))
    def _():
        wait_for(output_got, small_sem.at[0])
        pair_output[...] = output_got[...]
        wait_for(gradient_got, small_sem.at[1])
        pair_gradient[...] = gradient_got[...]

    @pl.when(jnp.logical_not(stays))
    def _():
        wait_for(relay_left, send_sem.at[0])
        wait_for(relay_right, send_sem.at[1])

    msa_sent(right_dj, msa_right, 0, send_sem.at[2])
    msa_sent(left_ic, msa_left, 1, send_sem.at[3])
    block_sent(0, pair_input)
    block_sent(1, cotangent)
    msa_sent(relay_left, msa_left, 0, send_sem.at[8])
    msa_sent(relay_right, msa_right, 1, send_sem.at[9])
    for number in (10, 13, 14, 16, 26):
        wait_for(o_left.at[pl.ds(0, 7)], send_sem.at[number])
    for number in (11, 12, 15, 17):
        wait_for(o_left, send_sem.at[number])
    msa_sent(left_ci, msa_left, 0, send_sem.at[21])
    msa_sent(right_dj, msa_left, 1, send_sem.at[24])
    wait_for(msa_cot_got, send_sem.at[27])

    @pl.when(h == 0)
    def _():
        wait_for(output_got, output_sem.at[1])
        wait_for(gradient_got, gradient_sem.at[1])

        @pl.when(odd == 1)
        def _():
            wait_for(output_got, output_sem.at[0])
            wait_for(gradient_got, gradient_sem.at[0])


def pair_updates(left_ic, left_ci, right_dj, pair_input, cotangent, weights):
    gathered = pltpu.VMEM((GRID, BLOCK, BLOCK, WIDTH), BF16)
    block = pltpu.VMEM((BLOCK, BLOCK, WIDTH), BF16)
    flat = pltpu.VMEM((BLOCK * BLOCK, WIDTH), F32)
    shares = pltpu.VMEM((64, BLOCK * HIDDEN), BF16)
    all_sequences = pltpu.VMEM((2 * GRID, 64, BLOCK * HIDDEN), BF16)
    half_block = pltpu.VMEM((8, BLOCK, WIDTH), BF16)
    wide_block = pltpu.VMEM((BLOCK, BLOCK, WIDTH), F32)
    half_wide = pltpu.VMEM((8, BLOCK, WIDTH), F32)
    projected = pltpu.VMEM((BLOCK * BLOCK, 5 * WIDTH), F32)
    dma = pltpu.SemaphoreType.DMA
    vmem = pl.BlockSpec(memory_space=pltpu.VMEM)
    return pl.pallas_call(
        pair_kernel,
        out_shape=(
            jax.ShapeDtypeStruct((8, BLOCK, WIDTH), BF16),
            jax.ShapeDtypeStruct((8, BLOCK, WIDTH), F32),
            jax.ShapeDtypeStruct((2, 64, BLOCK * HIDDEN), BF16),
        ),
        in_specs=[vmem] * 10,
        out_specs=(vmem, vmem, vmem),
        scratch_shapes=[
            block,
            block,
            shares,
            shares,
            all_sequences,
            all_sequences,
            pltpu.VMEM((GRID, 128, BLOCK * HIDDEN), BF16),
            gathered,
            gathered,
            block,
            gathered,
            gathered,
            block,
            gathered,
            gathered,
            gathered,
            gathered,
            gathered,
            gathered,
            gathered,
            gathered,
            gathered,
            pltpu.VMEM((HIDDEN * HIDDEN, WIDTH), F32),
            pltpu.VMEM((HIDDEN * WIDTH, WIDTH), BF16),
            pltpu.VMEM((HIDDEN * WIDTH, 4 * WIDTH), BF16),
            pltpu.VMEM((BLOCK * HIDDEN, BLOCK * HIDDEN), F32),
            wide_block,
            wide_block,
            wide_block,
            flat,
            projected,
            projected,
            flat,
            flat,
            flat,
            flat,
            pltpu.VMEM((4 * WIDTH, 4 * WIDTH), BF16),
            pltpu.VMEM((GRID, BLOCK * HIDDEN, BLOCK * HIDDEN), BF16),
            pltpu.VMEM((128, BLOCK * HIDDEN), BF16),
            shares,
            pltpu.VMEM((2, 8, BLOCK, WIDTH), BF16),
            half_block,
            pltpu.VMEM((2, 8, BLOCK, WIDTH), F32),
            half_wide,
            dma((2,)),
            dma((2, 2)),
            dma((2, 2 * GRID)),
            dma((GRID, 2)),
            dma((8, GRID)),
            dma((GRID,)),
            dma((3,)),
            dma((28,)),
            dma((2,)),
            dma((2,)),
        ],
        compiler_params=pltpu.CompilerParams(
            collective_id=1, has_side_effects=True, vmem_limit_bytes=48 << 20
        ),
        name="pair_updates",
    )(left_ic, left_ci, right_dj, pair_input, cotangent, *weights)


def body(
    homolog_features,
    pair_input,
    cotangent,
    homolog_factor_matrix,
    outer_output_weight,
    outgoing_input_weight,
    outgoing_output_weight,
    incoming_input_weight,
    incoming_output_weight,
):
    sequences, residues, depth = homolog_features.shape
    normed, scale = layer_norm(homolog_features.astype(F32))
    projected = jnp.dot(
        normed.astype(BF16), homolog_factor_matrix, preferred_element_type=F32
    ).astype(BF16)
    left, right = projected[..., :HIDDEN], projected[..., HIDDEN:]
    left_ic = left.reshape(sequences, residues * HIDDEN)
    left_ci = left.transpose(0, 2, 1).reshape(sequences, residues * HIDDEN)
    right_dj = right.transpose(0, 2, 1).reshape(sequences, residues * HIDDEN)
    pair_output, pair_gradient, cots = pair_updates(
        left_ic,
        left_ci,
        right_dj,
        pair_input,
        cotangent,
        (
            outer_output_weight,
            outgoing_input_weight,
            outgoing_output_weight,
            incoming_input_weight,
            incoming_output_weight,
        ),
    )
    cots = cots.reshape(2, sequences, residues, HIDDEN)
    projection_cot = jnp.concatenate([cots[0], cots[1]], axis=-1)
    normed_cot = jnp.dot(
        projection_cot, homolog_factor_matrix.T, preferred_element_type=F32
    )
    normed, scale = layer_norm(homolog_features.astype(F32))
    alignment_gradient = layer_norm_pullback(normed, scale, normed_cot)
    return pair_output, pair_gradient, alignment_gradient


def solution(mesh):
    split = P("row", "col", None)
    return jax.shard_map(
        body,
        mesh=mesh,
        in_specs=(split, split, split, P(), P(), P(), P(), P(), P()),
        out_specs=(split, split, split),
        check_vma=False,
    )
```

```python
import jax
import jax.numpy as jnp
from jax import lax
from jax.experimental import pallas as pl
from jax.experimental.pallas import tpu as pltpu
from jax.sharding import PartitionSpec as P

SEQUENCES = 1024
EPSILON = 1e-05
MESH = pl.DeviceIdType.MESH
F32 = jnp.float32
BF16 = jnp.bfloat16
GRID = 8
BLOCK = 16
WIDTH = 128
HIDDEN = 32
ROWS_AT = 2


def dot(lhs, rhs, dims=((1,), (0,))):
    return lax.dot_general(lhs, rhs, (dims, ((), ())), preferred_element_type=F32)


def layer_norm(inputs):
    centered = inputs - jnp.mean(inputs, axis=-1, keepdims=True)
    spread = jnp.mean(centered * centered, axis=-1, keepdims=True)
    scale = lax.rsqrt(spread + EPSILON)
    return centered * scale, scale


def layer_norm_pullback(normed, scale, upstream):
    along = jnp.mean(upstream * normed, axis=-1, keepdims=True)
    return scale * (upstream - jnp.mean(upstream, axis=-1, keepdims=True) - normed * along)


def repeat_factor(factor_weight, spread_factor):
    hidden_row = lax.broadcasted_iota(jnp.int32, (2 * HIDDEN, 2 * WIDTH), 0)
    hidden_lane = lax.broadcasted_iota(jnp.int32, (2 * HIDDEN, 2 * WIDTH), 1)
    repeats = (hidden_lane % HIDDEN + HIDDEN * (hidden_lane // WIDTH) == hidden_row).astype(F32)
    repeated = dot(factor_weight[...], repeats.astype(BF16), ((0,), (0,)))
    lane_quarter = lax.broadcasted_iota(jnp.int32, (2 * WIDTH, 2 * WIDTH), 1) % WIDTH // HIDDEN
    for q in range(4):
        spread_factor[q * 2 * WIDTH : (q + 1) * 2 * WIDTH, :] = jnp.where(
            lane_quarter == q, repeated, 0.0
        ).astype(BF16)


def pair_kernel(
    homolog_hbm,
    factor_weight_hbm,
    pair_input,
    cotangent,
    outer_weight_hbm,
    out_in_weight_hbm,
    out_out_weight_hbm,
    in_in_weight_hbm,
    in_out_weight_hbm,
    pair_output,
    pair_gradient,
    msa_cots,
    homolog,
    factor_weight,
    outer_weight,
    out_in_weight,
    out_out_weight,
    in_in_weight,
    in_out_weight,
    normed_msa,
    spread_factor,
    left_ic,
    left_ci,
    right_dj,
    pair_block,
    cot_block,
    relay_left,
    relay_right,
    msa_left,
    msa_right,
    msa_rows,
    o_left,
    o_right,
    o_right_stage,
    i_left,
    i_right,
    i_left_stage,
    ib_right,
    ib_left,
    ob_right,
    ob_left,
    left_parts,
    right_parts,
    left_parts2,
    right_parts2,
    final_cot,
    wide_weight,
    table_weight,
    spread_weight,
    turned_weight,
    out_in_turned,
    out_out_turned,
    in_in_turned,
    in_out_turned,
    outer32,
    wide,
    cot_wide,
    cot_turned,
    flat,
    out_kept,
    in_kept,
    first,
    upstream32,
    stacked,
    grad_table,
    msa_cot_own,
    msa_cot_got,
    output_stage,
    output_got,
    gradient_stage,
    gradient_got,
    relay_sem,
    relay_send_sem,
    block_sem,
    msa_sem,
    rows_sem,
    pair_sem,
    final_sem,
    small_sem,
    send_sem,
    output_sem,
    gradient_sem,
    input_sem,
):
    row, col = lax.axis_index("row"), lax.axis_index("col")
    a, h, b = row // 2, row % 2, col
    other = 1 - h
    odd = b % 2
    at = (a + 4 * odd) % GRID
    own_i = at * other + b * h
    own_j = b * other + at * h
    stays = jnp.logical_and(a == b, odd == 0)

    def chip_at(i, j):
        return (i + 4 * (j % 2)) % GRID, j

    def row_chip(n):
        return chip_at(at * other + n * h, n * other + b * h)

    def col_chip(n):
        return chip_at(n * other + at * h, b * other + n * h)

    def apart(k):
        m = k // 2
        return m + (m // 2) * (5 - 2 * m), k % 2

    def along_rows(own, k):
        dm, dv = apart(k)
        return (own // 4 + dv) % 2 * 4 + (own % 4 + dm) % 4

    def along_columns(own, k):
        dm, dv = apart(k)
        return (own // 2 + dm) % 4 * 2 + (own % 2 + dv) % 2

    def step_i(k):
        return along_rows(at, k) * other + along_columns(b, k) * h

    def step_j(k):
        return along_columns(b, k) * other + along_rows(at, k) * h

    relay_column = (a % 4 + b // 2 + 2 * (b % 4)) % 4 * 2 + a // 4
    relay_chip = chip_at(b, relay_column)
    source_row = b % 2 * 4 + (b // 2 + 16 - at // 2 - 2 * (at % 4)) % 4
    relay_stays = jnp.logical_and(relay_column == b, relay_chip[0] == a)

    def column(n):
        return n, b

    def line(n):
        return chip_at(at, n)

    def remote(src, dst, send, recv, chip, core):
        return pltpu.make_async_remote_copy(
            src_ref=src,
            dst_ref=dst,
            send_sem=send,
            recv_sem=recv,
            device_id=(2 * chip[0] + core, chip[1]),
            device_id_type=MESH,
        )

    def wait_for(ref, sem):
        pltpu.make_async_copy(ref, ref, sem).wait()

    barrier = pltpu.get_barrier_semaphore()

    def greet(chip, core):
        pl.semaphore_signal(
            barrier, inc=1, device_id=(2 * chip[0] + core, chip[1]), device_id_type=MESH
        )

    def greet_step(k, carry):
        for core in range(2):
            greet(column(along_rows(a, GRID - k)), core)
            greet(line(along_columns(b, GRID - k)), core)
        return carry

    def greet_across(k, carry):
        for core in range(2):
            greet((a, 2 * k + 1 - odd), core)
        return carry

    @pl.when(jnp.logical_not(relay_stays))
    def _():
        greet((source_row, at), h)

    @pl.when(h == 1)
    def _():
        greet((b, at), 0)

    @pl.when(jnp.logical_and(h == 1, jnp.logical_not(stays)))
    def _():
        greet((b, at), 1)

    lax.fori_loop(0, GRID // 2, greet_across, 0)
    lax.fori_loop(1, GRID, greet_step, 0)
    greet((a, b), other)
    inputs = (
        (homolog_hbm, homolog),
        (factor_weight_hbm, factor_weight),
        (outer_weight_hbm, outer_weight),
        (out_in_weight_hbm, out_in_weight),
        (out_out_weight_hbm, out_out_weight),
        (in_in_weight_hbm, in_in_weight),
        (in_out_weight_hbm, in_out_weight),
    )
    copies = [
        pltpu.make_async_copy(src, dst, input_sem.at[number])
        for number, (src, dst) in enumerate(inputs)
    ]
    for copy in copies:
        copy.start()
    copies[0].wait()
    copies[1].wait()

    def normalize_step(n, carry):
        rows = pl.ds(pl.multiple_of(n * 256, 256), 256)
        normed, unused = layer_norm(homolog[rows, :].astype(F32))
        normed_msa[0][rows, :] = normed[:, :WIDTH]
        normed_msa[1][rows, :] = normed[:, WIDTH:]
        return carry

    lax.fori_loop(0, 4, normalize_step, 0)
    repeat_factor(factor_weight, spread_factor)
    groups = []
    for g in range(4):
        pieces = [
            normed_msa[part][pl.ds(4 * g + q, 64, stride=BLOCK), :].astype(BF16)
            for q in range(4)
            for part in range(2)
        ]
        groups.append(jnp.concatenate(pieces, axis=1))
    factors = dot(jnp.concatenate(groups, axis=0), spread_factor[...]).astype(BF16)
    left_value = jnp.concatenate(
        [factors[g * 64 : (g + 1) * 64, :WIDTH] for g in range(4)], axis=1
    )
    right_value = jnp.concatenate(
        [factors[g * 64 : (g + 1) * 64, WIDTH:] for g in range(4)], axis=1
    )
    left_ic[...] = left_value
    before = lax.broadcasted_iota(jnp.int32, (BLOCK * HIDDEN, BLOCK * HIDDEN), 0)
    after = lax.broadcasted_iota(jnp.int32, (BLOCK * HIDDEN, BLOCK * HIDDEN), 1)
    moved = (before == after % BLOCK * HIDDEN + after // BLOCK).astype(F32).astype(BF16)
    turned_factors = dot(jnp.concatenate([left_value, right_value], axis=0), moved).astype(BF16)
    left_ci[...] = turned_factors[:64]
    right_dj[...] = turned_factors[64:]

    for copy in copies[2:]:
        copy.wait()
    keeps_first = jnp.logical_and(h == 0, odd == 0)
    keeps_second = jnp.logical_and(h == 1, stays)
    pl.semaphore_wait(barrier, 39 - relay_stays.astype(jnp.int32) - keeps_second.astype(jnp.int32))

    for slot in range(4):
        src, dst = ((left_ic, relay_left), (right_dj, relay_right))[slot // 2]
        half = pl.ds(slot % 2 * 32, 32)

        @pl.when(jnp.logical_not(relay_stays))
        def _():
            remote(
                src.at[half],
                dst.at[half],
                relay_send_sem.at[slot],
                relay_sem.at[slot],
                relay_chip,
                h,
            ).start()

        @pl.when(relay_stays)
        def _():
            pltpu.make_async_copy(src.at[half], dst.at[half], relay_sem.at[slot]).start()

    def msa_send(src, dst, sems, slot, chip_of, core, send, half=None):
        whole = half is None
        source = src if whole else src.at[pl.ds(half * 32, 32)]
        target = dst.at[slot] if whole else dst.at[slot, pl.ds(half * 32, 32)]

        def step(k, carry):
            place = (GRID - 1 - k) * other + k * h

            @pl.when(jnp.logical_or(place > 0, h != core))
            def _():
                remote(source, target, send, sems.at[slot], chip_of(place), core).start()

            return carry

        lax.fori_loop(0, GRID, step, 0)

        @pl.when(h == core)
        def _():
            pltpu.make_async_copy(source, target, sems.at[slot]).start()

    def column_step(k):
        return column(along_rows(a, k))

    def line_step(k):
        return line(along_columns(b, k))

    def msa_sent(src, dst, core, send):
        @pl.when(h == core)
        def _():
            wait_for(dst.at[pl.ds(0, 7)], send)

        @pl.when(h != core)
        def _():
            wait_for(dst.at[pl.ds(0, 8)], send)

    msa_send(right_dj, msa_right, msa_sem.at[1], row, column_step, 0, send_sem.at[2])
    msa_send(left_ic, msa_left, msa_sem.at[0], row, column_step, 1, send_sem.at[3])

    for slot, (src, dst) in enumerate(((pair_input, pair_block), (cotangent, cot_block))):
        half = dst.at[pl.ds(h * 8, 8)]
        sem = block_sem.at[slot, h]

        @pl.when(keeps_first)
        def _():
            pltpu.make_async_copy(src, half, sem).start()

        @pl.when(jnp.logical_not(keeps_first))
        def _():
            remote(src, half, send_sem.at[4 + slot], sem, chip_at(a, b), 0).start()

        @pl.when(keeps_second)
        def _():
            pltpu.make_async_copy(src, half, sem).start()

        @pl.when(jnp.logical_not(keeps_second))
        def _():
            remote(src, half, send_sem.at[6 + slot], sem, chip_at(b, a), 1).start()

    def block_sent(slot, src):
        @pl.when(jnp.logical_not(keeps_first))
        def _():
            wait_for(src, send_sem.at[4 + slot])

        @pl.when(jnp.logical_not(keeps_second))
        def _():
            wait_for(src, send_sem.at[6 + slot])

    wide_weight[...] = outer_weight[...].astype(F32)
    spread_weight[...] = jnp.zeros(spread_weight.shape, BF16)

    def weight_step(n, carry):
        by_d = wide_weight[pl.ds(n, HIDDEN, stride=HIDDEN), :].astype(BF16)
        start = pl.multiple_of(n * WIDTH, WIDTH)
        for q in range(4):
            table_weight[pl.ds(start + q * HIDDEN, HIDDEN), :] = by_d

        def spread(piece):
            for q in range(4):
                spread_weight[
                    pl.ds(start + q * HIDDEN, HIDDEN), q * WIDTH : (q + 1) * WIDTH
                ] = piece

        @pl.when(h == 0)
        def _():
            spread(outer_weight[pl.ds(pl.multiple_of(n * HIDDEN, HIDDEN), HIDDEN), :])

        @pl.when(h == 1)
        def _():
            spread(by_d)

        return carry

    lax.fori_loop(0, HIDDEN, weight_step, 0)

    relay_slot = 2 * source_row + h
    for slot in range(4):
        half = slot % 2
        src, dst = ((relay_left, msa_left), (relay_right, msa_right))[slot // 2]
        wait_for(src.at[pl.ds(half * 32, 32)], relay_sem.at[slot])
        kind = slot // 2
        msa_send(
            src, dst, msa_sem.at[kind], relay_slot, line_step, kind, send_sem.at[8 + kind], half
        )

    def turn_step(n, carry):
        rows = pl.ds(pl.multiple_of(n * 2 * WIDTH, 2 * WIDTH), 2 * WIDTH)
        turned_weight[:, rows] = spread_weight[rows, :].T
        return carry

    lax.fori_loop(0, HIDDEN // 2, turn_step, 0)
    for weight, turned_one in (
        (out_in_weight, out_in_turned),
        (out_out_weight, out_out_turned),
        (in_in_weight, in_in_turned),
        (in_out_weight, in_out_turned),
    ):
        turned_one[...] = weight[...].T

    def outer_step(k, carry):
        n = (b // 2 + k) % 4

        def msa_wait(part, carry):
            slot = 4 * n + part
            wait_for(msa_left.at[slot], msa_sem.at[0, slot])
            wait_for(msa_right.at[slot], msa_sem.at[1, slot])
            return carry

        lax.fori_loop(0, 4, msa_wait, 0)
        four = pl.ds(4 * n, 4)
        outer32[...] += dot(
            msa_right[four].reshape(256, BLOCK * HIDDEN),
            msa_left[four].reshape(256, BLOCK * HIDDEN),
            ((0,), (0,)),
        )
        return carry

    outer32[...] = jnp.zeros(outer32.shape, F32)
    lax.fori_loop(0, 4, outer_step, 0)
    lane_part = lax.broadcasted_iota(jnp.int32, (BLOCK, WIDTH), 1) // HIDDEN

    def project_step(d8, total):
        columns = []
        for part in range(8):
            tile = outer32[pl.ds(pl.multiple_of((8 * d8 + part) * BLOCK, BLOCK), BLOCK), :]
            columns.append(
                jnp.concatenate(
                    [
                        jnp.where(lane_part == q, tile[:, g * WIDTH : (g + 1) * WIDTH], 0.0)
                        for q in range(4)
                        for g in range(4)
                    ],
                    axis=0,
                )
            )
        picked = (jnp.concatenate(columns, axis=1) * (1.0 / SEQUENCES)).astype(BF16)
        weight = table_weight[pl.ds(pl.multiple_of(d8 * 8 * WIDTH, 8 * WIDTH), 8 * WIDTH), :]
        return total + dot(picked, weight)

    projected = lax.fori_loop(
        0, HIDDEN // 8, project_step, jnp.zeros((BLOCK * BLOCK, WIDTH), F32)
    )
    for part in range(2):
        wait_for(pair_block.at[pl.ds(part * 8, 8)], block_sem.at[0, part])
        wait_for(cot_block.at[pl.ds(part * 8, 8)], block_sem.at[1, part])
    for i in range(BLOCK):
        start = ((i % 4) * 4 + i // 4) * BLOCK
        first[pl.ds(i * BLOCK, BLOCK), :] = (
            (pair_block[i].astype(F32) + projected[start : start + BLOCK]).astype(BF16).astype(F32)
        )

    def rows_send(src, core, send, first_step, last_step):
        target = msa_rows.at[b, pl.ds(pl.multiple_of(h * 64, 64), 64)]

        def step(k, carry):
            @pl.when(jnp.logical_or(k > 0, h != core))
            def _():
                remote(
                    src, target, send, rows_sem.at[b, h], (a, along_columns(b, k)), core
                ).start()

            return carry

        lax.fori_loop(first_step, last_step, step, 0)

        if first_step == 0:

            @pl.when(h == core)
            def _():
                pltpu.make_async_copy(src, target, rows_sem.at[b, h]).start()

    def send_same(dst, sems, chips, steps, send):
        own = steps(0)

        def step(k, carry):
            chip = chips(steps(GRID - k))
            remote(dst.at[own], dst.at[own], send, sems.at[own], chip, h).start()
            return carry

        lax.fori_loop(1, GRID, step, 0)

    def send_other(src, dst, sems, chips, steps, send):
        own = steps(0)

        def step(k, carry):
            chip = chips(steps(GRID - 1 - k))
            remote(src, dst.at[own], send, sems.at[own], chip, other).start()
            return carry

        lax.fori_loop(0, GRID, step, 0)

    def block_product(totals, left, by_column, right):
        def inner(group, totals):
            totals = list(totals)
            for u in range(4):
                t = group * 4 + u
                across = right(t)
                for p in range(BLOCK):
                    one = left[t, pl.ds(p, 1), :] if by_column else left[p, pl.ds(t, 1), :]
                    totals[p] = totals[p] + one * across
            return tuple(totals)

        return lax.fori_loop(0, BLOCK // 4, inner, totals)

    def no_totals():
        return tuple(jnp.zeros((BLOCK, WIDTH), F32) for _ in range(BLOCK))

    def send_rows_at(k, rows):
        @pl.when(k == ROWS_AT)
        def _():
            rows_send(*rows)

    def contract(left, left_sem, left_own, by_column, right, right_sem, right_own, steps, rows):
        def arrive(ref, sems, slot, skip):
            if skip is None:
                wait_for(ref.at[slot], sems.at[slot])
            else:

                @pl.when(slot != skip)
                def _():
                    wait_for(ref.at[slot], sems.at[slot])

        def block_step(k, totals):
            slot = steps(k)
            send_rows_at(k, rows)
            arrive(left, left_sem, slot, left_own)
            arrive(right, right_sem, slot, right_own)
            wide[...] = left[slot].astype(F32)
            return block_product(totals, wide, by_column, lambda t: right[slot, t].astype(F32))

        totals = lax.fori_loop(0, GRID, block_step, no_totals())
        return jnp.concatenate(totals, axis=0)

    def partial(part, n, totals):
        for p in range(BLOCK):
            part[n, p] = totals[p].astype(BF16)

    def sum_of(parts, sems, skip, steps, rows=None):
        def step(k, total):
            slot = steps(k)
            if rows is not None:
                send_rows_at(k, rows)
            if skip is None:
                wait_for(parts.at[slot], sems.at[slot])
            else:

                @pl.when(slot != skip)
                def _():
                    wait_for(parts.at[slot], sems.at[slot])

            return total + parts[slot].reshape(BLOCK * BLOCK, WIDTH).astype(F32)

        return lax.fori_loop(0, GRID, step, jnp.zeros((BLOCK * BLOCK, WIDTH), F32))

    def send_part(part, n, dst, slot, sems, chips, core, send):
        remote(part.at[n], dst.at[slot], send, sems.at[slot], chips(n), core).start()

    def turned(value, store):
        flat[...] = value
        for j in range(BLOCK):
            store(j, flat[pl.ds(j, BLOCK, stride=BLOCK), :].astype(BF16))

    def turn_cot(value):
        rounded = value.astype(BF16).astype(F32)
        cot_wide[...] = rounded.reshape(BLOCK, BLOCK, WIDTH)
        flat[...] = rounded
        for j in range(BLOCK):
            cot_turned[j] = flat[pl.ds(j, BLOCK, stride=BLOCK), :]

    def blocked(value):
        return value.astype(BF16).reshape(BLOCK, BLOCK, WIDTH)

    def gated(normed, weight, at):
        projected = dot(normed, weight[:, at * WIDTH : (at + 2) * WIDTH])
        gate, value = jax.nn.sigmoid(projected[:, :WIDTH]), projected[:, WIDTH:]
        return gate, value

    def keep_gated(ref, first_at, gate, value):
        ref[first_at] = value * gate * (1.0 - gate)
        ref[first_at + 1] = gate

    def keep_norm(ref, first_at, normed, scale):
        ref[first_at] = normed
        ref[first_at + 1] = jnp.broadcast_to(scale, normed.shape)

    normed, scale = layer_norm(first[...])
    rounded = normed.astype(BF16)
    left_gate, left_value = gated(rounded, out_in_weight, 0)
    o_left[own_j] = blocked(left_gate * left_value)
    send_same(o_left, pair_sem.at[0], row_chip, step_j, send_sem.at[10])
    right_gate, right_value = gated(rounded, out_in_weight, 2)

    def store_right(j, value):
        o_right_stage[j] = value

    turned(right_gate * right_value, store_right)
    send_other(o_right_stage, o_right, pair_sem.at[1], row_chip, step_j, send_sem.at[11])
    keep_gated(out_kept, 0, left_gate, left_value)
    keep_gated(out_kept, 2, right_gate, right_value)
    keep_norm(out_kept, 4, normed, scale)
    out_kept[6] = jax.nn.sigmoid(dot(rounded, out_in_weight[:, 4 * WIDTH :]))
    mixing = contract(
        o_left,
        pair_sem.at[0],
        own_j,
        False,
        o_right,
        pair_sem.at[1],
        None,
        step_j,
        (left_ci, 0, send_sem.at[21], 0, 4),
    )
    mixing_normed, mixing_scale = layer_norm(mixing)
    update = dot(mixing_normed.astype(BF16), out_out_weight[...])
    second = (first[...] + out_kept[6] * update).astype(BF16).astype(F32)

    normed, scale = layer_norm(second)
    rounded = normed.astype(BF16)
    right_gate, right_value = gated(rounded, in_in_weight, 2)
    i_right[own_i] = blocked(right_gate * right_value)
    send_same(i_right, pair_sem.at[4], col_chip, step_i, send_sem.at[14])
    left_gate, left_value = gated(rounded, in_in_weight, 0)
    i_left_stage[...] = blocked(left_gate * left_value)
    send_other(i_left_stage, i_left, pair_sem.at[5], col_chip, step_i, send_sem.at[15])
    keep_norm(out_kept, 7, mixing_normed, mixing_scale)
    out_kept[9] = update
    keep_gated(in_kept, 0, left_gate, left_value)
    keep_gated(in_kept, 2, right_gate, right_value)
    keep_norm(in_kept, 4, normed, scale)
    gating = jax.nn.sigmoid(dot(rounded, in_in_weight[:, 4 * WIDTH :]))
    in_kept[6] = gating
    in_kept[7] = second
    upstream = cot_block[...].reshape(BLOCK * BLOCK, WIDTH).astype(F32)
    upstream32[...] = upstream
    in_kept[8] = dot((upstream * gating).astype(BF16), in_out_turned[...])
    mixing = contract(
        i_left,
        pair_sem.at[5],
        None,
        True,
        i_right,
        pair_sem.at[4],
        own_i,
        step_i,
        (left_ci, 0, send_sem.at[21], 4, 8),
    )

    def input_pullback(kept, left_cot, right_cot, gating_part, weight, upstream):
        pieces = [
            (left_cot * kept[0]).astype(BF16),
            (left_cot * kept[1]).astype(BF16),
            (right_cot * kept[2]).astype(BF16),
            (right_cot * kept[3]).astype(BF16),
        ]
        normed_cot = gating_part + dot(
            jnp.concatenate(pieces, axis=1), weight[: 4 * WIDTH, :]
        )
        return upstream + layer_norm_pullback(kept[4], kept[5], normed_cot)

    normed, scale = layer_norm(mixing)
    turn_cot(layer_norm_pullback(normed, scale, in_kept[8]))

    def incoming_step(k, carry):
        n = step_i(GRID - 1 - k)
        wide[...] = i_right[n].astype(F32)
        totals = block_product(no_totals(), wide, False, lambda t: cot_turned[t])
        partial(left_parts, n, totals)
        send_part(
            left_parts, n, ib_left, own_j, pair_sem.at[2], row_chip, other, send_sem.at[12]
        )
        wide[...] = i_left[n].astype(F32)
        totals = block_product(no_totals(), wide, False, lambda t: cot_wide[t])

        @pl.when(n != own_i)
        def _():
            partial(right_parts, n, totals)
            send_part(
                right_parts, n, ib_right, own_i, pair_sem.at[3], col_chip, h, send_sem.at[13]
            )

        @pl.when(n == own_i)
        def _():
            partial(ib_right, n, totals)

        return carry

    lax.fori_loop(0, GRID, incoming_step, 0)
    gating = in_kept[6]
    update = dot(normed.astype(BF16), in_out_weight[...])
    result = (in_kept[7] + gating * update).astype(BF16)
    gating_cot = upstream32[...] * update * gating * (1.0 - gating)
    gating_part = dot(gating_cot.astype(BF16), in_in_turned[4 * WIDTH :, :])

    def hand_over(value, stage, got, sem, send):
        stage[...] = value.reshape(2, 8, BLOCK, WIDTH)
        for part in range(2):
            order = remote(stage.at[part], got, send.at[part], sem, (at, b), part)
            if part == 0:
                pl.when(odd == 1)(order.start)
            else:
                order.start()

    @pl.when(h == 0)
    def _():
        hand_over(result, output_stage, output_got, small_sem.at[0], output_sem)

    left_cot = sum_of(
        ib_left, pair_sem.at[2], None, step_j, (right_dj, 1, send_sem.at[24], 0, 4)
    )
    right_cot = sum_of(ib_right, pair_sem.at[3], own_i, step_i)
    second_cot = input_pullback(
        in_kept, left_cot, right_cot, gating_part, in_in_turned, upstream32[...]
    )

    normed_cot = dot((second_cot * out_kept[6]).astype(BF16), out_out_turned[...])
    turn_cot(layer_norm_pullback(out_kept[7], out_kept[8], normed_cot))

    def outgoing_step(k, carry):
        n = step_j(GRID - 1 - k)
        wide[...] = o_right[n].astype(F32)
        totals = block_product(no_totals(), wide, False, lambda t: cot_turned[t])

        @pl.when(n != own_j)
        def _():
            partial(left_parts2, n, totals)
            send_part(
                left_parts2, n, ob_left, own_j, pair_sem.at[6], row_chip, h, send_sem.at[16]
            )

        @pl.when(n == own_j)
        def _():
            partial(ob_left, n, totals)

        totals = block_product(
            no_totals(), cot_wide, True, lambda t: o_left[n, t].astype(F32)
        )
        partial(right_parts2, n, totals)
        send_part(
            right_parts2, n, ob_right, own_i, pair_sem.at[7], col_chip, other, send_sem.at[17]
        )
        return carry

    lax.fori_loop(0, GRID, outgoing_step, 0)
    gating = out_kept[6]
    gating_cot = second_cot * out_kept[9] * gating * (1.0 - gating)
    gating_part = dot(gating_cot.astype(BF16), out_in_turned[4 * WIDTH :, :])
    flat[...] = sum_of(
        ob_left, pair_sem.at[6], own_j, step_j, (right_dj, 1, send_sem.at[24], 4, 8)
    )
    left_cot = jnp.concatenate(
        [flat[pl.ds(j, BLOCK, stride=BLOCK), :] for j in range(BLOCK)], axis=0
    )
    right_cot = sum_of(ob_right, pair_sem.at[7], None, step_i)
    gradient = input_pullback(
        out_kept, left_cot, right_cot, gating_part, out_in_turned, second_cot
    )

    @pl.when(h == 0)
    def _():
        hand_over(gradient, gradient_stage, gradient_got, small_sem.at[1], gradient_sem)
        flat[...] = gradient
        for j in range(BLOCK):
            final_cot[at, j] = flat[pl.ds(j, BLOCK, stride=BLOCK), :].astype(BF16)

    @pl.when(h == 1)
    def _():
        final_cot[at] = blocked(gradient)

    def final_chip(n):
        return chip_at(n, b)

    def final_step(k):
        return along_rows(at, k)

    send_same(final_cot, final_sem, final_chip, final_step, send_sem.at[26])

    def final_half(part, total):
        def stack_step(k, carry):
            slot = final_step(4 * part + k)

            @pl.when(slot != at)
            def _():
                wait_for(final_cot.at[slot], final_sem.at[slot])

            for g in range(4):
                rows = pl.ds(pl.multiple_of(g * 64 + k * BLOCK, BLOCK), BLOCK)
                for q in range(4):
                    stacked[rows, q * WIDTH : (q + 1) * WIDTH] = final_cot[slot, 4 * g + q]
            return carry

        lax.fori_loop(0, 4, stack_step, 0)

        def table_step(x8, carry):
            begin = pl.multiple_of(x8 * 8 * WIDTH, 8 * WIDTH)
            chunk = dot(stacked[...], turned_weight[:, pl.ds(begin, 8 * WIDTH)]).astype(BF16)
            for piece in range(8):
                start = pl.multiple_of((8 * x8 + piece) * BLOCK, BLOCK)
                for g in range(4):
                    for k in range(4):
                        row = g * 64 + k * BLOCK
                        grad_table[k, pl.ds(start, BLOCK), g * WIDTH : (g + 1) * WIDTH] = chunk[
                            row : row + BLOCK, piece * WIDTH : (piece + 1) * WIDTH
                        ]
            return carry

        lax.fori_loop(0, HIDDEN // 8, table_step, 0)
        sequences = []
        for k in range(4):
            slot = final_step(4 * part + k)
            for piece in range(2):
                wait_for(msa_rows.at[slot, pl.ds(piece * 64, 64)], rows_sem.at[slot, piece])
            sequences.append(msa_rows[slot])
        return total + dot(
            jnp.concatenate(sequences, axis=1),
            grad_table[...].reshape(4 * BLOCK * HIDDEN, BLOCK * HIDDEN),
        )

    total = lax.fori_loop(0, 2, final_half, jnp.zeros((128, BLOCK * HIDDEN), F32))
    msa_cot_own[...] = (total * (1.0 / SEQUENCES)).astype(BF16)
    remote(
        msa_cot_own.at[pl.ds(pl.multiple_of(other * 64, 64), 64)],
        msa_cot_got,
        send_sem.at[27],
        small_sem.at[2],
        (a, b),
        other,
    ).start()
    msa_cots[other] = msa_cot_own[pl.ds(pl.multiple_of(h * 64, 64), 64), :]
    wait_for(msa_cot_got, small_sem.at[2])
    msa_cots[h] = msa_cot_got[...]

    @pl.when(keeps_first)
    def _():
        pair_output[...] = output_stage[0]
        pair_gradient[...] = gradient_stage[0]

    @pl.when(jnp.logical_not(keeps_first))
    def _():
        wait_for(output_got, small_sem.at[0])
        pair_output[...] = output_got[...]
        wait_for(gradient_got, small_sem.at[1])
        pair_gradient[...] = gradient_got[...]

    @pl.when(jnp.logical_not(relay_stays))
    def _():
        for slot in range(4):
            wait_for(relay_left.at[pl.ds(0, 32)], relay_send_sem.at[slot])

    msa_sent(right_dj, msa_right, 0, send_sem.at[2])
    msa_sent(left_ic, msa_left, 1, send_sem.at[3])
    block_sent(0, pair_input)
    block_sent(1, cotangent)
    msa_sent(relay_left, msa_left, 0, send_sem.at[8])
    msa_sent(relay_right, msa_right, 1, send_sem.at[9])
    for number in (10, 13, 14, 16, 26):
        wait_for(o_left.at[pl.ds(0, 7)], send_sem.at[number])
    for number in (11, 12, 15, 17):
        wait_for(o_left, send_sem.at[number])
    msa_sent(left_ci, msa_left, 0, send_sem.at[21])
    msa_sent(right_dj, msa_left, 1, send_sem.at[24])
    wait_for(msa_cot_got, send_sem.at[27])

    @pl.when(h == 0)
    def _():
        wait_for(output_got, output_sem.at[1])
        wait_for(gradient_got, gradient_sem.at[1])

        @pl.when(odd == 1)
        def _():
            wait_for(output_got, output_sem.at[0])
            wait_for(gradient_got, gradient_sem.at[0])


def pair_updates(homolog, factor_weight, pair_input, cotangent, weights):
    gathered = pltpu.VMEM((GRID, BLOCK, BLOCK, WIDTH), BF16)
    block = pltpu.VMEM((BLOCK, BLOCK, WIDTH), BF16)
    flat = pltpu.VMEM((BLOCK * BLOCK, WIDTH), F32)
    shares = pltpu.VMEM((64, BLOCK * HIDDEN), BF16)
    all_sequences = pltpu.VMEM((2 * GRID, 64, BLOCK * HIDDEN), BF16)
    half_block = pltpu.VMEM((8, BLOCK, WIDTH), BF16)
    wide_block = pltpu.VMEM((BLOCK, BLOCK, WIDTH), F32)
    half_wide = pltpu.VMEM((8, BLOCK, WIDTH), F32)
    dma = pltpu.SemaphoreType.DMA
    vmem = pl.BlockSpec(memory_space=pltpu.VMEM)
    return pl.pallas_call(
        pair_kernel,
        out_shape=(
            jax.ShapeDtypeStruct((8, BLOCK, WIDTH), BF16),
            jax.ShapeDtypeStruct((8, BLOCK, WIDTH), F32),
            jax.ShapeDtypeStruct((2, 64, BLOCK * HIDDEN), BF16),
        ),
        in_specs=[pl.BlockSpec(memory_space=pl.ANY)] * 9,
        out_specs=(vmem, vmem, vmem),
        scratch_shapes=[
            pltpu.VMEM((64 * BLOCK, 2 * WIDTH), BF16),
            pltpu.VMEM((2 * HIDDEN, 2 * WIDTH), BF16),
            pltpu.VMEM((HIDDEN * HIDDEN, WIDTH), BF16),
            pltpu.VMEM((WIDTH, 5 * WIDTH), BF16),
            pltpu.VMEM((WIDTH, WIDTH), BF16),
            pltpu.VMEM((WIDTH, 5 * WIDTH), BF16),
            pltpu.VMEM((WIDTH, WIDTH), BF16),
            [pltpu.VMEM((64 * BLOCK, WIDTH), F32)] * 2,
            pltpu.VMEM((8 * WIDTH, 2 * WIDTH), BF16),
            shares,
            shares,
            shares,
            block,
            block,
            shares,
            shares,
            all_sequences,
            all_sequences,
            pltpu.VMEM((GRID, 128, BLOCK * HIDDEN), BF16),
            gathered,
            gathered,
            block,
            gathered,
            gathered,
            block,
            gathered,
            gathered,
            gathered,
            gathered,
            gathered,
            gathered,
            gathered,
            gathered,
            gathered,
            pltpu.VMEM((HIDDEN * HIDDEN, WIDTH), F32),
            pltpu.VMEM((HIDDEN * WIDTH, WIDTH), BF16),
            pltpu.VMEM((HIDDEN * WIDTH, 4 * WIDTH), BF16),
            pltpu.VMEM((4 * WIDTH, HIDDEN * WIDTH), BF16),
            pltpu.VMEM((5 * WIDTH, WIDTH), BF16),
            pltpu.VMEM((WIDTH, WIDTH), BF16),
            pltpu.VMEM((5 * WIDTH, WIDTH), BF16),
            pltpu.VMEM((WIDTH, WIDTH), BF16),
            pltpu.VMEM((BLOCK * HIDDEN, BLOCK * HIDDEN), F32),
            wide_block,
            wide_block,
            wide_block,
            flat,
            pltpu.VMEM((10, BLOCK * BLOCK, WIDTH), F32),
            pltpu.VMEM((9, BLOCK * BLOCK, WIDTH), F32),
            flat,
            flat,
            pltpu.VMEM((2 * WIDTH, 4 * WIDTH), BF16),
            pltpu.VMEM((4, BLOCK * HIDDEN, BLOCK * HIDDEN), BF16),
            pltpu.VMEM((128, BLOCK * HIDDEN), BF16),
            shares,
            pltpu.VMEM((2, 8, BLOCK, WIDTH), BF16),
            half_block,
            pltpu.VMEM((2, 8, BLOCK, WIDTH), F32),
            half_wide,
            dma((4,)),
            dma((4,)),
            dma((2, 2)),
            dma((2, 2 * GRID)),
            dma((GRID, 2)),
            dma((8, GRID)),
            dma((GRID,)),
            dma((3,)),
            dma((28,)),
            dma((2,)),
            dma((2,)),
            dma((7,)),
        ],
        compiler_params=pltpu.CompilerParams(
            collective_id=1, has_side_effects=True, vmem_limit_bytes=62 << 20
        ),
        name="pair_updates",
    )(homolog, factor_weight, pair_input, cotangent, *weights)


def finish_kernel(
    homolog_hbm,
    factor_weight_hbm,
    msa_cots_hbm,
    pair_output,
    pair_gradient,
    pair_output_out,
    pair_gradient_out,
    alignment_gradient,
    homolog,
    factor_weight,
    msa_cots,
    wide,
    result,
    spread_factor,
    copy_sem,
):
    copies = [
        pltpu.make_async_copy(src, dst, copy_sem.at[number])
        for number, (src, dst) in enumerate(
            (
                (homolog_hbm, homolog),
                (factor_weight_hbm, factor_weight),
                (msa_cots_hbm, msa_cots),
                (pair_gradient, pair_gradient_out),
                (pair_output, pair_output_out),
            )
        )
    ]
    for copy in copies:
        copy.start()
    copies[0].wait()
    copies[1].wait()
    for part in range(2):
        wide[part][...] = homolog[:, part * WIDTH : (part + 1) * WIDTH].astype(F32)
    repeat_factor(factor_weight, spread_factor)
    copies[2].wait()
    cots = jnp.concatenate(
        [
            jnp.concatenate(
                [msa_cots[kind, :, g * WIDTH : (g + 1) * WIDTH] for kind in range(2)], axis=1
            )
            for g in range(4)
        ],
        axis=0,
    )
    for q in range(4):
        normed_cots = dot(
            cots, spread_factor[q * 2 * WIDTH : (q + 1) * 2 * WIDTH, :], ((1,), (1,))
        )
        for g in range(4):
            rows = pl.ds(4 * g + q, 64, stride=BLOCK)
            normed, scale = layer_norm(
                jnp.concatenate([wide[0][rows, :], wide[1][rows, :]], axis=1)
            )
            value = layer_norm_pullback(normed, scale, normed_cots[g * 64 : (g + 1) * 64])
            for part in range(2):
                result[part][rows, :] = value[:, part * WIDTH : (part + 1) * WIDTH]
    for part in range(2):
        alignment_gradient[:, part * WIDTH : (part + 1) * WIDTH] = result[part][...]
    copies[3].wait()
    copies[4].wait()


def body(
    homolog_features,
    pair_input,
    cotangent,
    homolog_factor_matrix,
    outer_output_weight,
    outgoing_input_weight,
    outgoing_output_weight,
    incoming_input_weight,
    incoming_output_weight,
):
    sequences, residues, depth = homolog_features.shape
    homolog = homolog_features.reshape(sequences * residues, depth)
    factor_weight = homolog_factor_matrix.T
    pair_output, pair_gradient, cots = pair_updates(
        homolog,
        factor_weight,
        pair_input,
        cotangent,
        (
            outer_output_weight,
            outgoing_input_weight,
            outgoing_output_weight,
            incoming_input_weight,
            incoming_output_weight,
        ),
    )
    vmem = pl.BlockSpec(memory_space=pltpu.VMEM)
    anywhere = pl.BlockSpec(memory_space=pl.ANY)
    pair_output, pair_gradient, alignment_gradient = pl.pallas_call(
        finish_kernel,
        out_shape=(
            jax.ShapeDtypeStruct(pair_output.shape, BF16),
            jax.ShapeDtypeStruct(pair_gradient.shape, F32),
            jax.ShapeDtypeStruct((sequences * residues, depth), F32),
        ),
        in_specs=[anywhere] * 5,
        out_specs=(anywhere, anywhere, vmem),
        scratch_shapes=[
            pltpu.VMEM((sequences * residues, depth), BF16),
            pltpu.VMEM((2 * HIDDEN, depth), BF16),
            pltpu.VMEM((2, sequences, residues * HIDDEN), BF16),
            [pltpu.VMEM((64 * BLOCK, WIDTH), F32)] * 2,
            [pltpu.VMEM((64 * BLOCK, WIDTH), F32)] * 2,
            pltpu.VMEM((8 * WIDTH, 2 * WIDTH), BF16),
            pltpu.SemaphoreType.DMA((5,)),
        ],
        compiler_params=pltpu.CompilerParams(vmem_limit_bytes=62 << 20),
        name="finish",
    )(homolog, factor_weight, cots, pair_output, pair_gradient)
    return pair_output, pair_gradient, alignment_gradient.reshape(sequences, residues, depth)


def solution(mesh):
    split = P("row", "col", None)
    return jax.shard_map(
        body,
        mesh=mesh,
        in_specs=(split, split, split, P(), P(), P(), P(), P(), P()),
        out_specs=(split, split, split),
        check_vma=False,
    )
```

```python
import jax
import jax.numpy as jnp
from jax import lax
from jax.experimental import pallas as pl
from jax.experimental.pallas import tpu as pltpu
from jax.sharding import PartitionSpec as P

SEQUENCES = 1024
EPSILON = 1e-05
MESH = pl.DeviceIdType.MESH
F32 = jnp.float32
BF16 = jnp.bfloat16
GRID = 8
BLOCK = 16
WIDTH = 128
HIDDEN = 32
ROWS_AT = 2
ROWS_PARTS = ((), (), (0, 7), (6, 5), (4, 3), (2, 1))


def dot(lhs, rhs, dims=((1,), (0,))):
    return lax.dot_general(lhs, rhs, (dims, ((), ())), preferred_element_type=F32)


def layer_norm(inputs):
    centered = inputs - jnp.mean(inputs, axis=-1, keepdims=True)
    spread = jnp.mean(centered * centered, axis=-1, keepdims=True)
    scale = lax.rsqrt(spread + EPSILON)
    return centered * scale, scale


def layer_norm_pullback(normed, scale, upstream):
    along = jnp.mean(upstream * normed, axis=-1, keepdims=True)
    return scale * (upstream - jnp.mean(upstream, axis=-1, keepdims=True) - normed * along)


def repeat_factor(factor_weight, spread_factor):
    hidden_row = lax.broadcasted_iota(jnp.int32, (2 * HIDDEN, 2 * WIDTH), 0)
    hidden_lane = lax.broadcasted_iota(jnp.int32, (2 * HIDDEN, 2 * WIDTH), 1)
    repeats = (hidden_lane % HIDDEN + HIDDEN * (hidden_lane // WIDTH) == hidden_row).astype(F32)
    repeated = dot(factor_weight[...], repeats.astype(BF16), ((0,), (0,)))
    lane_quarter = lax.broadcasted_iota(jnp.int32, (2 * WIDTH, 2 * WIDTH), 1) % WIDTH // HIDDEN
    for q in range(4):
        spread_factor[q * 2 * WIDTH : (q + 1) * 2 * WIDTH, :] = jnp.where(
            lane_quarter == q, repeated, 0.0
        ).astype(BF16)


def pair_kernel(
    homolog_hbm,
    factor_weight_hbm,
    pair_input,
    cotangent,
    outer_weight_hbm,
    out_in_weight_hbm,
    out_out_weight_hbm,
    in_in_weight_hbm,
    in_out_weight_hbm,
    pair_output,
    pair_gradient,
    alignment_gradient,
    homolog,
    factor_weight,
    outer_weight,
    out_in_weight,
    out_out_weight,
    in_in_weight,
    in_out_weight,
    normed_msa,
    msa_scale,
    alignment,
    spread_factor,
    left_ic,
    left_ci,
    right_dj,
    pair_block,
    cot_block,
    relay_left,
    relay_right,
    msa_left,
    msa_right,
    msa_rows,
    o_left,
    o_right,
    o_right_stage,
    i_left,
    i_right,
    i_left_stage,
    ib_right,
    ib_left,
    ob_right,
    ob_left,
    left_parts,
    right_parts,
    left_parts2,
    right_parts2,
    final_cot,
    wide_weight,
    table_weight,
    spread_weight,
    turned_weight,
    out_in_turned,
    out_out_turned,
    in_in_turned,
    in_out_turned,
    outer32,
    wide,
    cot_wide,
    cot_turned,
    flat,
    out_kept,
    in_kept,
    first,
    upstream32,
    stacked,
    grad_table,
    msa_cots,
    msa_cot_own,
    msa_cot_got,
    output_stage,
    output_got,
    gradient_stage,
    gradient_got,
    relay_sem,
    relay_send_sem,
    block_sem,
    msa_sem,
    rows_sem,
    pair_sem,
    final_sem,
    small_sem,
    send_sem,
    output_sem,
    gradient_sem,
    input_sem,
    alignment_sem,
):
    row, col = lax.axis_index("row"), lax.axis_index("col")
    a, h, b = row // 2, row % 2, col
    other = 1 - h
    odd = b % 2
    at = (a + 4 * odd) % GRID
    own_i = at * other + b * h
    own_j = b * other + at * h
    stays = jnp.logical_and(a == b, odd == 0)

    def chip_at(i, j):
        return (i + 4 * (j % 2)) % GRID, j

    def row_chip(n):
        return chip_at(at * other + n * h, n * other + b * h)

    def col_chip(n):
        return chip_at(n * other + at * h, b * other + n * h)

    def apart(k):
        m = k // 2
        return m + (m // 2) * (5 - 2 * m), k % 2

    def along_rows(own, k):
        dm, dv = apart(k)
        return (own // 4 + dv) % 2 * 4 + (own % 4 + dm) % 4

    def along_columns(own, k):
        dm, dv = apart(k)
        return (own // 2 + dm) % 4 * 2 + (own % 2 + dv) % 2

    def step_i(k):
        return along_rows(at, k) * other + along_columns(b, k) * h

    def step_j(k):
        return along_columns(b, k) * other + along_rows(at, k) * h

    relay_column = (a % 4 + b // 2 + 2 * (b % 4)) % 4 * 2 + a // 4
    relay_chip = chip_at(b, relay_column)
    source_row = b % 2 * 4 + (b // 2 + 16 - at // 2 - 2 * (at % 4)) % 4
    relay_stays = jnp.logical_and(relay_column == b, relay_chip[0] == a)

    def column(n):
        return n, b

    def line(n):
        return chip_at(at, n)

    def remote(src, dst, send, recv, chip, core):
        return pltpu.make_async_remote_copy(
            src_ref=src,
            dst_ref=dst,
            send_sem=send,
            recv_sem=recv,
            device_id=(2 * chip[0] + core, chip[1]),
            device_id_type=MESH,
        )

    def wait_for(ref, sem):
        pltpu.make_async_copy(ref, ref, sem).wait()

    barrier = pltpu.get_barrier_semaphore()

    def greet(chip, core):
        pl.semaphore_signal(
            barrier, inc=1, device_id=(2 * chip[0] + core, chip[1]), device_id_type=MESH
        )

    def greet_step(k, carry):
        for core in range(2):
            greet(column(along_rows(a, GRID - k)), core)
            greet(line(along_columns(b, GRID - k)), core)
        return carry

    def greet_across(k, carry):
        for core in range(2):
            greet((a, 2 * k + 1 - odd), core)
        return carry

    @pl.when(jnp.logical_not(relay_stays))
    def _():
        greet((source_row, at), h)

    @pl.when(h == 1)
    def _():
        greet((b, at), 0)

    @pl.when(jnp.logical_and(h == 1, jnp.logical_not(stays)))
    def _():
        greet((b, at), 1)

    lax.fori_loop(0, GRID // 2, greet_across, 0)
    lax.fori_loop(1, GRID, greet_step, 0)
    greet((a, b), other)
    inputs = (
        (homolog_hbm, homolog),
        (factor_weight_hbm, factor_weight),
        (outer_weight_hbm, outer_weight),
        (out_in_weight_hbm, out_in_weight),
        (out_out_weight_hbm, out_out_weight),
        (in_in_weight_hbm, in_in_weight),
        (in_out_weight_hbm, in_out_weight),
    )
    copies = [
        pltpu.make_async_copy(src, dst, input_sem.at[number])
        for number, (src, dst) in enumerate(inputs)
    ]
    for copy in copies:
        copy.start()
    copies[0].wait()
    copies[1].wait()

    def normalize_step(n, carry):
        rows = pl.ds(pl.multiple_of(n * 256, 256), 256)
        normed, scale = layer_norm(homolog[rows, :].astype(F32))
        msa_scale[rows, :] = jnp.broadcast_to(scale, (256, WIDTH))
        normed_msa[0][rows, :] = normed[:, :WIDTH]
        normed_msa[1][rows, :] = normed[:, WIDTH:]
        return carry

    lax.fori_loop(0, 4, normalize_step, 0)
    repeat_factor(factor_weight, spread_factor)
    groups = []
    for g in range(4):
        pieces = [
            normed_msa[part][pl.ds(4 * g + q, 64, stride=BLOCK), :].astype(BF16)
            for q in range(4)
            for part in range(2)
        ]
        groups.append(jnp.concatenate(pieces, axis=1))
    factors = dot(jnp.concatenate(groups, axis=0), spread_factor[...]).astype(BF16)
    left_value = jnp.concatenate(
        [factors[g * 64 : (g + 1) * 64, :WIDTH] for g in range(4)], axis=1
    )
    right_value = jnp.concatenate(
        [factors[g * 64 : (g + 1) * 64, WIDTH:] for g in range(4)], axis=1
    )
    left_ic[...] = left_value
    before = lax.broadcasted_iota(jnp.int32, (BLOCK * HIDDEN, BLOCK * HIDDEN), 0)
    after = lax.broadcasted_iota(jnp.int32, (BLOCK * HIDDEN, BLOCK * HIDDEN), 1)
    moved = (before == after % BLOCK * HIDDEN + after // BLOCK).astype(F32).astype(BF16)
    turned_factors = dot(jnp.concatenate([left_value, right_value], axis=0), moved).astype(BF16)
    left_ci[...] = turned_factors[:64]
    right_dj[...] = turned_factors[64:]

    for copy in copies[2:]:
        copy.wait()
    keeps_first = jnp.logical_and(h == 0, odd == 0)
    keeps_second = jnp.logical_and(h == 1, stays)
    pl.semaphore_wait(barrier, 39 - relay_stays.astype(jnp.int32) - keeps_second.astype(jnp.int32))

    for slot in range(4):
        src, dst = ((left_ic, relay_left), (right_dj, relay_right))[slot // 2]
        half = pl.ds(slot % 2 * 32, 32)

        @pl.when(jnp.logical_not(relay_stays))
        def _():
            remote(
                src.at[half],
                dst.at[half],
                relay_send_sem.at[slot],
                relay_sem.at[slot],
                relay_chip,
                h,
            ).start()

        @pl.when(relay_stays)
        def _():
            pltpu.make_async_copy(src.at[half], dst.at[half], relay_sem.at[slot]).start()

    def msa_send(src, dst, sems, slot, chip_of, core, send, half=None):
        whole = half is None
        source = src if whole else src.at[pl.ds(half * 32, 32)]
        target = dst.at[slot] if whole else dst.at[slot, pl.ds(half * 32, 32)]

        def step(k, carry):
            place = (GRID - 1 - k) * other + k * h

            @pl.when(jnp.logical_or(place > 0, h != core))
            def _():
                remote(source, target, send, sems.at[slot], chip_of(place), core).start()

            return carry

        lax.fori_loop(0, GRID, step, 0)

        @pl.when(h == core)
        def _():
            pltpu.make_async_copy(source, target, sems.at[slot]).start()

    def column_step(k):
        return column(along_rows(a, k))

    def line_step(k):
        return line(along_columns(b, k))

    def rows_send(src, core, send, steps):
        target = msa_rows.at[b, pl.ds(pl.multiple_of(h * 64, 64), 64)]
        sem = rows_sem.at[b, h]
        for k in steps:
            if k == 0:

                @pl.when(h == core)
                def _():
                    pltpu.make_async_copy(src, target, sem).start()

                @pl.when(h != core)
                def _():
                    remote(src, target, send, sem, (a, b), core).start()

            else:
                remote(src, target, send, sem, (a, along_columns(b, k)), core).start()

    def rows_pair(steps):
        rows_send(left_ci, 0, send_sem.at[21], steps)
        rows_send(right_dj, 1, send_sem.at[24], steps)

    def msa_sent(src, dst, core, send):
        @pl.when(h == core)
        def _():
            wait_for(dst.at[pl.ds(0, 7)], send)

        @pl.when(h != core)
        def _():
            wait_for(dst.at[pl.ds(0, 8)], send)

    msa_send(right_dj, msa_right, msa_sem.at[1], row, column_step, 0, send_sem.at[2])
    msa_send(left_ic, msa_left, msa_sem.at[0], row, column_step, 1, send_sem.at[3])

    rows_pair(ROWS_PARTS[0])

    for slot, (src, dst) in enumerate(((pair_input, pair_block), (cotangent, cot_block))):
        half = dst.at[pl.ds(h * 8, 8)]
        sem = block_sem.at[slot, h]

        @pl.when(keeps_first)
        def _():
            pltpu.make_async_copy(src, half, sem).start()

        @pl.when(jnp.logical_not(keeps_first))
        def _():
            remote(src, half, send_sem.at[4 + slot], sem, chip_at(a, b), 0).start()

        @pl.when(keeps_second)
        def _():
            pltpu.make_async_copy(src, half, sem).start()

        @pl.when(jnp.logical_not(keeps_second))
        def _():
            remote(src, half, send_sem.at[6 + slot], sem, chip_at(b, a), 1).start()

    def block_sent(slot, src):
        @pl.when(jnp.logical_not(keeps_first))
        def _():
            wait_for(src, send_sem.at[4 + slot])

        @pl.when(jnp.logical_not(keeps_second))
        def _():
            wait_for(src, send_sem.at[6 + slot])

    relay_slot = 2 * source_row + h
    for slot in range(4):
        half = slot % 2
        src, dst = ((relay_left, msa_left), (relay_right, msa_right))[slot // 2]
        wait_for(src.at[pl.ds(half * 32, 32)], relay_sem.at[slot])
        kind = slot // 2
        msa_send(
            src, dst, msa_sem.at[kind], relay_slot, line_step, kind, send_sem.at[8 + kind], half
        )

    wide_weight[...] = outer_weight[...].astype(F32)
    spread_weight[...] = jnp.zeros(spread_weight.shape, BF16)

    def weight_step(n, carry):
        by_d = wide_weight[pl.ds(n, HIDDEN, stride=HIDDEN), :].astype(BF16)
        start = pl.multiple_of(n * WIDTH, WIDTH)
        for q in range(4):
            table_weight[pl.ds(start + q * HIDDEN, HIDDEN), :] = by_d

        def spread(piece):
            for q in range(4):
                spread_weight[
                    pl.ds(start + q * HIDDEN, HIDDEN), q * WIDTH : (q + 1) * WIDTH
                ] = piece

        @pl.when(h == 0)
        def _():
            spread(outer_weight[pl.ds(pl.multiple_of(n * HIDDEN, HIDDEN), HIDDEN), :])

        @pl.when(h == 1)
        def _():
            spread(by_d)

        return carry

    lax.fori_loop(0, HIDDEN, weight_step, 0)

    rows_pair(ROWS_PARTS[1])

    def turn_step(n, carry):
        rows = pl.ds(pl.multiple_of(n * 2 * WIDTH, 2 * WIDTH), 2 * WIDTH)
        turned_weight[:, rows] = spread_weight[rows, :].T
        return carry

    lax.fori_loop(0, HIDDEN // 2, turn_step, 0)
    for weight, turned_one in (
        (out_in_weight, out_in_turned),
        (out_out_weight, out_out_turned),
        (in_in_weight, in_in_turned),
        (in_out_weight, in_out_turned),
    ):
        turned_one[...] = weight[...].T

    def outer_step(k, carry):
        n = (b // 2 + k) % 4

        def msa_wait(part, carry):
            slot = 4 * n + part
            wait_for(msa_left.at[slot], msa_sem.at[0, slot])
            wait_for(msa_right.at[slot], msa_sem.at[1, slot])
            return carry

        lax.fori_loop(0, 4, msa_wait, 0)
        four = pl.ds(4 * n, 4)
        outer32[...] += dot(
            msa_right[four].reshape(256, BLOCK * HIDDEN),
            msa_left[four].reshape(256, BLOCK * HIDDEN),
            ((0,), (0,)),
        )
        return carry

    outer32[...] = jnp.zeros(outer32.shape, F32)
    lax.fori_loop(0, 4, outer_step, 0)
    lane_part = lax.broadcasted_iota(jnp.int32, (BLOCK, WIDTH), 1) // HIDDEN

    def project_step(d8, total):
        columns = []
        for part in range(8):
            tile = outer32[pl.ds(pl.multiple_of((8 * d8 + part) * BLOCK, BLOCK), BLOCK), :]
            columns.append(
                jnp.concatenate(
                    [
                        jnp.where(lane_part == q, tile[:, g * WIDTH : (g + 1) * WIDTH], 0.0)
                        for q in range(4)
                        for g in range(4)
                    ],
                    axis=0,
                )
            )
        picked = (jnp.concatenate(columns, axis=1) * (1.0 / SEQUENCES)).astype(BF16)
        weight = table_weight[pl.ds(pl.multiple_of(d8 * 8 * WIDTH, 8 * WIDTH), 8 * WIDTH), :]
        return total + dot(picked, weight)

    projected = lax.fori_loop(
        0, HIDDEN // 8, project_step, jnp.zeros((BLOCK * BLOCK, WIDTH), F32)
    )
    for part in range(2):
        wait_for(pair_block.at[pl.ds(part * 8, 8)], block_sem.at[0, part])
        wait_for(cot_block.at[pl.ds(part * 8, 8)], block_sem.at[1, part])
    for i in range(BLOCK):
        start = ((i % 4) * 4 + i // 4) * BLOCK
        first[pl.ds(i * BLOCK, BLOCK), :] = (
            (pair_block[i].astype(F32) + projected[start : start + BLOCK]).astype(BF16).astype(F32)
        )

    def send_same(dst, sems, chips, steps, send):
        own = steps(0)

        def step(k, carry):
            chip = chips(steps(GRID - k))
            remote(dst.at[own], dst.at[own], send, sems.at[own], chip, h).start()
            return carry

        lax.fori_loop(1, GRID, step, 0)

    def send_other(src, dst, sems, chips, steps, send):
        own = steps(0)

        def step(k, carry):
            chip = chips(steps(GRID - 1 - k))
            remote(src, dst.at[own], send, sems.at[own], chip, other).start()
            return carry

        lax.fori_loop(0, GRID, step, 0)

    def block_product(totals, left, by_column, right):
        def inner(group, totals):
            totals = list(totals)
            for u in range(4):
                t = group * 4 + u
                across = right(t)
                for p in range(BLOCK):
                    one = left[t, pl.ds(p, 1), :] if by_column else left[p, pl.ds(t, 1), :]
                    totals[p] = totals[p] + one * across
            return tuple(totals)

        return lax.fori_loop(0, BLOCK // 4, inner, totals)

    def no_totals():
        return tuple(jnp.zeros((BLOCK, WIDTH), F32) for _ in range(BLOCK))

    def send_rows_at(k, rows):
        @pl.when(k == ROWS_AT)
        def _():
            rows_pair(rows)

    def contract(left, left_sem, left_own, by_column, right, right_sem, right_own, steps, rows):
        def arrive(ref, sems, slot, skip):
            if skip is None:
                wait_for(ref.at[slot], sems.at[slot])
            else:

                @pl.when(slot != skip)
                def _():
                    wait_for(ref.at[slot], sems.at[slot])

        def block_step(k, totals):
            slot = steps(k)
            send_rows_at(k, rows)
            arrive(left, left_sem, slot, left_own)
            arrive(right, right_sem, slot, right_own)
            wide[...] = left[slot].astype(F32)
            return block_product(totals, wide, by_column, lambda t: right[slot, t].astype(F32))

        totals = lax.fori_loop(0, GRID, block_step, no_totals())
        return jnp.concatenate(totals, axis=0)

    def partial(part, n, totals):
        for p in range(BLOCK):
            part[n, p] = totals[p].astype(BF16)

    def sum_of(parts, sems, skip, steps, rows=None):
        def step(k, total):
            slot = steps(k)
            if rows is not None:
                send_rows_at(k, rows)
            if skip is None:
                wait_for(parts.at[slot], sems.at[slot])
            else:

                @pl.when(slot != skip)
                def _():
                    wait_for(parts.at[slot], sems.at[slot])

            return total + parts[slot].reshape(BLOCK * BLOCK, WIDTH).astype(F32)

        return lax.fori_loop(0, GRID, step, jnp.zeros((BLOCK * BLOCK, WIDTH), F32))

    def send_part(part, n, dst, slot, sems, chips, core, send):
        remote(part.at[n], dst.at[slot], send, sems.at[slot], chips(n), core).start()

    def turned(value, store):
        flat[...] = value
        for j in range(BLOCK):
            store(j, flat[pl.ds(j, BLOCK, stride=BLOCK), :].astype(BF16))

    def turn_cot(value):
        rounded = value.astype(BF16).astype(F32)
        cot_wide[...] = rounded.reshape(BLOCK, BLOCK, WIDTH)
        flat[...] = rounded
        for j in range(BLOCK):
            cot_turned[j] = flat[pl.ds(j, BLOCK, stride=BLOCK), :]

    def blocked(value):
        return value.astype(BF16).reshape(BLOCK, BLOCK, WIDTH)

    def gated(normed, weight, at):
        projected = dot(normed, weight[:, at * WIDTH : (at + 2) * WIDTH])
        gate, value = jax.nn.sigmoid(projected[:, :WIDTH]), projected[:, WIDTH:]
        return gate, value

    def keep_gated(ref, first_at, gate, value):
        ref[first_at] = value * gate * (1.0 - gate)
        ref[first_at + 1] = gate

    def keep_norm(ref, first_at, normed, scale):
        ref[first_at] = normed
        ref[first_at + 1] = jnp.broadcast_to(scale, normed.shape)

    normed, scale = layer_norm(first[...])
    rounded = normed.astype(BF16)
    left_gate, left_value = gated(rounded, out_in_weight, 0)
    o_left[own_j] = blocked(left_gate * left_value)
    send_same(o_left, pair_sem.at[0], row_chip, step_j, send_sem.at[10])
    right_gate, right_value = gated(rounded, out_in_weight, 2)

    def store_right(j, value):
        o_right_stage[j] = value

    turned(right_gate * right_value, store_right)
    send_other(o_right_stage, o_right, pair_sem.at[1], row_chip, step_j, send_sem.at[11])
    keep_gated(out_kept, 0, left_gate, left_value)
    keep_gated(out_kept, 2, right_gate, right_value)
    keep_norm(out_kept, 4, normed, scale)
    out_kept[6] = jax.nn.sigmoid(dot(rounded, out_in_weight[:, 4 * WIDTH :]))
    mixing = contract(
        o_left,
        pair_sem.at[0],
        own_j,
        False,
        o_right,
        pair_sem.at[1],
        None,
        step_j,
        ROWS_PARTS[2],
    )
    mixing_normed, mixing_scale = layer_norm(mixing)
    update = dot(mixing_normed.astype(BF16), out_out_weight[...])
    second = (first[...] + out_kept[6] * update).astype(BF16).astype(F32)

    normed, scale = layer_norm(second)
    rounded = normed.astype(BF16)
    right_gate, right_value = gated(rounded, in_in_weight, 2)
    i_right[own_i] = blocked(right_gate * right_value)
    send_same(i_right, pair_sem.at[4], col_chip, step_i, send_sem.at[14])
    left_gate, left_value = gated(rounded, in_in_weight, 0)
    i_left_stage[...] = blocked(left_gate * left_value)
    send_other(i_left_stage, i_left, pair_sem.at[5], col_chip, step_i, send_sem.at[15])
    keep_norm(out_kept, 7, mixing_normed, mixing_scale)
    out_kept[9] = update
    keep_gated(in_kept, 0, left_gate, left_value)
    keep_gated(in_kept, 2, right_gate, right_value)
    keep_norm(in_kept, 4, normed, scale)
    gating = jax.nn.sigmoid(dot(rounded, in_in_weight[:, 4 * WIDTH :]))
    in_kept[6] = gating
    in_kept[7] = second
    upstream = cot_block[...].reshape(BLOCK * BLOCK, WIDTH).astype(F32)
    upstream32[...] = upstream
    in_kept[8] = dot((upstream * gating).astype(BF16), in_out_turned[...])
    mixing = contract(
        i_left,
        pair_sem.at[5],
        None,
        True,
        i_right,
        pair_sem.at[4],
        own_i,
        step_i,
        ROWS_PARTS[3],
    )

    def input_pullback(kept, left_cot, right_cot, gating_part, weight, upstream):
        pieces = [
            (left_cot * kept[0]).astype(BF16),
            (left_cot * kept[1]).astype(BF16),
            (right_cot * kept[2]).astype(BF16),
            (right_cot * kept[3]).astype(BF16),
        ]
        normed_cot = gating_part + dot(
            jnp.concatenate(pieces, axis=1), weight[: 4 * WIDTH, :]
        )
        return upstream + layer_norm_pullback(kept[4], kept[5], normed_cot)

    normed, scale = layer_norm(mixing)
    turn_cot(layer_norm_pullback(normed, scale, in_kept[8]))

    def incoming_step(k, carry):
        n = step_i(GRID - 1 - k)
        wide[...] = i_right[n].astype(F32)
        totals = block_product(no_totals(), wide, False, lambda t: cot_turned[t])
        partial(left_parts, n, totals)
        send_part(
            left_parts, n, ib_left, own_j, pair_sem.at[2], row_chip, other, send_sem.at[12]
        )
        wide[...] = i_left[n].astype(F32)
        totals = block_product(no_totals(), wide, False, lambda t: cot_wide[t])

        @pl.when(n != own_i)
        def _():
            partial(right_parts, n, totals)
            send_part(
                right_parts, n, ib_right, own_i, pair_sem.at[3], col_chip, h, send_sem.at[13]
            )

        @pl.when(n == own_i)
        def _():
            partial(ib_right, n, totals)

        return carry

    lax.fori_loop(0, GRID, incoming_step, 0)
    gating = in_kept[6]
    update = dot(normed.astype(BF16), in_out_weight[...])
    result = (in_kept[7] + gating * update).astype(BF16)
    gating_cot = upstream32[...] * update * gating * (1.0 - gating)
    gating_part = dot(gating_cot.astype(BF16), in_in_turned[4 * WIDTH :, :])

    def hand_over(value, stage, got, sem, send):
        stage[...] = value.reshape(2, 8, BLOCK, WIDTH)
        for part in range(2):
            order = remote(stage.at[part], got, send.at[part], sem, (at, b), part)
            if part == 0:
                pl.when(odd == 1)(order.start)
            else:
                order.start()

    @pl.when(h == 0)
    def _():
        hand_over(result, output_stage, output_got, small_sem.at[0], output_sem)

    left_cot = sum_of(
        ib_left, pair_sem.at[2], None, step_j, ROWS_PARTS[4]
    )
    right_cot = sum_of(ib_right, pair_sem.at[3], own_i, step_i)
    second_cot = input_pullback(
        in_kept, left_cot, right_cot, gating_part, in_in_turned, upstream32[...]
    )

    normed_cot = dot((second_cot * out_kept[6]).astype(BF16), out_out_turned[...])
    turn_cot(layer_norm_pullback(out_kept[7], out_kept[8], normed_cot))

    def outgoing_step(k, carry):
        n = step_j(GRID - 1 - k)
        wide[...] = o_right[n].astype(F32)
        totals = block_product(no_totals(), wide, False, lambda t: cot_turned[t])

        @pl.when(n != own_j)
        def _():
            partial(left_parts2, n, totals)
            send_part(
                left_parts2, n, ob_left, own_j, pair_sem.at[6], row_chip, h, send_sem.at[16]
            )

        @pl.when(n == own_j)
        def _():
            partial(ob_left, n, totals)

        totals = block_product(
            no_totals(), cot_wide, True, lambda t: o_left[n, t].astype(F32)
        )
        partial(right_parts2, n, totals)
        send_part(
            right_parts2, n, ob_right, own_i, pair_sem.at[7], col_chip, other, send_sem.at[17]
        )
        return carry

    lax.fori_loop(0, GRID, outgoing_step, 0)
    gating = out_kept[6]
    gating_cot = second_cot * out_kept[9] * gating * (1.0 - gating)
    gating_part = dot(gating_cot.astype(BF16), out_in_turned[4 * WIDTH :, :])
    flat[...] = sum_of(
        ob_left, pair_sem.at[6], own_j, step_j, ROWS_PARTS[5]
    )
    left_cot = jnp.concatenate(
        [flat[pl.ds(j, BLOCK, stride=BLOCK), :] for j in range(BLOCK)], axis=0
    )
    right_cot = sum_of(ob_right, pair_sem.at[7], None, step_i)
    gradient = input_pullback(
        out_kept, left_cot, right_cot, gating_part, out_in_turned, second_cot
    )

    @pl.when(h == 0)
    def _():
        hand_over(gradient, gradient_stage, gradient_got, small_sem.at[1], gradient_sem)
        flat[...] = gradient
        for j in range(BLOCK):
            final_cot[at, j] = flat[pl.ds(j, BLOCK, stride=BLOCK), :].astype(BF16)

    @pl.when(h == 1)
    def _():
        final_cot[at] = blocked(gradient)

    def final_chip(n):
        return chip_at(n, b)

    def final_step(k):
        return along_rows(at, k)

    send_same(final_cot, final_sem, final_chip, final_step, send_sem.at[26])

    def final_half(part, total):
        def stack_step(k, carry):
            slot = final_step(4 * part + k)

            @pl.when(slot != at)
            def _():
                wait_for(final_cot.at[slot], final_sem.at[slot])

            for g in range(4):
                rows = pl.ds(pl.multiple_of(g * 64 + k * BLOCK, BLOCK), BLOCK)
                for q in range(4):
                    stacked[rows, q * WIDTH : (q + 1) * WIDTH] = final_cot[slot, 4 * g + q]
            return carry

        lax.fori_loop(0, 4, stack_step, 0)

        def table_step(x8, carry):
            begin = pl.multiple_of(x8 * 8 * WIDTH, 8 * WIDTH)
            chunk = dot(stacked[...], turned_weight[:, pl.ds(begin, 8 * WIDTH)]).astype(BF16)
            for piece in range(8):
                start = pl.multiple_of((8 * x8 + piece) * BLOCK, BLOCK)
                for g in range(4):
                    for k in range(4):
                        row = g * 64 + k * BLOCK
                        grad_table[k, pl.ds(start, BLOCK), g * WIDTH : (g + 1) * WIDTH] = chunk[
                            row : row + BLOCK, piece * WIDTH : (piece + 1) * WIDTH
                        ]
            return carry

        lax.fori_loop(0, HIDDEN // 8, table_step, 0)
        sequences = []
        for k in range(4):
            slot = final_step(4 * part + k)
            for piece in range(2):
                wait_for(msa_rows.at[slot, pl.ds(piece * 64, 64)], rows_sem.at[slot, piece])
            sequences.append(msa_rows[slot])
        return total + dot(
            jnp.concatenate(sequences, axis=1),
            grad_table[...].reshape(4 * BLOCK * HIDDEN, BLOCK * HIDDEN),
        )

    total = lax.fori_loop(0, 2, final_half, jnp.zeros((128, BLOCK * HIDDEN), F32))
    msa_cot_own[...] = (total * (1.0 / SEQUENCES)).astype(BF16)
    remote(
        msa_cot_own.at[pl.ds(pl.multiple_of(other * 64, 64), 64)],
        msa_cot_got,
        send_sem.at[27],
        small_sem.at[2],
        (a, b),
        other,
    ).start()
    msa_cots[other] = msa_cot_own[pl.ds(pl.multiple_of(h * 64, 64), 64), :]
    wait_for(msa_cot_got, small_sem.at[2])
    msa_cots[h] = msa_cot_got[...]

    cots = jnp.concatenate(
        [
            jnp.concatenate(
                [msa_cots[kind, :, g * WIDTH : (g + 1) * WIDTH] for kind in range(2)], axis=1
            )
            for g in range(4)
        ],
        axis=0,
    )
    for q in range(4):
        normed_cots = dot(
            cots, spread_factor[q * 2 * WIDTH : (q + 1) * 2 * WIDTH, :], ((1,), (1,))
        )
        for g in range(4):
            rows = pl.ds(4 * g + q, 64, stride=BLOCK)
            value = layer_norm_pullback(
                jnp.concatenate([normed_msa[0][rows, :], normed_msa[1][rows, :]], axis=1),
                msa_scale[rows, :1],
                normed_cots[g * 64 : (g + 1) * 64],
            )
            for part in range(2):
                alignment[part][rows, :] = value[:, part * WIDTH : (part + 1) * WIDTH]
    alignment_copies = [
        pltpu.make_async_copy(
            alignment[part],
            alignment_gradient.at[:, pl.ds(part * WIDTH, WIDTH)],
            alignment_sem.at[part],
        )
        for part in range(2)
    ]
    for copy in alignment_copies:
        copy.start()

    @pl.when(keeps_first)
    def _():
        pair_output[...] = output_stage[0]
        pair_gradient[...] = gradient_stage[0]

    @pl.when(jnp.logical_not(keeps_first))
    def _():
        wait_for(output_got, small_sem.at[0])
        pair_output[...] = output_got[...]
        wait_for(gradient_got, small_sem.at[1])
        pair_gradient[...] = gradient_got[...]

    @pl.when(jnp.logical_not(relay_stays))
    def _():
        for slot in range(4):
            wait_for(relay_left.at[pl.ds(0, 32)], relay_send_sem.at[slot])

    msa_sent(right_dj, msa_right, 0, send_sem.at[2])
    msa_sent(left_ic, msa_left, 1, send_sem.at[3])
    block_sent(0, pair_input)
    block_sent(1, cotangent)
    msa_sent(relay_left, msa_left, 0, send_sem.at[8])
    msa_sent(relay_right, msa_right, 1, send_sem.at[9])
    for number in (10, 13, 14, 16, 26):
        wait_for(o_left.at[pl.ds(0, 7)], send_sem.at[number])
    for number in (11, 12, 15, 17):
        wait_for(o_left, send_sem.at[number])
    msa_sent(left_ci, msa_left, 0, send_sem.at[21])
    msa_sent(right_dj, msa_left, 1, send_sem.at[24])
    wait_for(msa_cot_got, send_sem.at[27])

    @pl.when(h == 0)
    def _():
        wait_for(output_got, output_sem.at[1])
        wait_for(gradient_got, gradient_sem.at[1])

        @pl.when(odd == 1)
        def _():
            wait_for(output_got, output_sem.at[0])
            wait_for(gradient_got, gradient_sem.at[0])

    for copy in alignment_copies:
        copy.wait()


def pair_updates(homolog, factor_weight, pair_input, cotangent, weights):
    gathered = pltpu.VMEM((GRID, BLOCK, BLOCK, WIDTH), BF16)
    block = pltpu.VMEM((BLOCK, BLOCK, WIDTH), BF16)
    flat = pltpu.VMEM((BLOCK * BLOCK, WIDTH), F32)
    shares = pltpu.VMEM((64, BLOCK * HIDDEN), BF16)
    all_sequences = pltpu.VMEM((2 * GRID, 64, BLOCK * HIDDEN), BF16)
    half_block = pltpu.VMEM((8, BLOCK, WIDTH), BF16)
    wide_block = pltpu.VMEM((BLOCK, BLOCK, WIDTH), F32)
    half_wide = pltpu.VMEM((8, BLOCK, WIDTH), F32)
    dma = pltpu.SemaphoreType.DMA
    vmem = pl.BlockSpec(memory_space=pltpu.VMEM)
    return pl.pallas_call(
        pair_kernel,
        out_shape=(
            jax.ShapeDtypeStruct((8, BLOCK, WIDTH), BF16),
            jax.ShapeDtypeStruct((8, BLOCK, WIDTH), F32),
            jax.ShapeDtypeStruct((64 * BLOCK, 2 * WIDTH), F32),
        ),
        in_specs=[pl.BlockSpec(memory_space=pl.ANY)] * 9,
        out_specs=(vmem, vmem, pl.BlockSpec(memory_space=pl.ANY)),
        scratch_shapes=[
            pltpu.VMEM((64 * BLOCK, 2 * WIDTH), BF16),
            pltpu.VMEM((2 * HIDDEN, 2 * WIDTH), BF16),
            pltpu.VMEM((HIDDEN * HIDDEN, WIDTH), BF16),
            pltpu.VMEM((WIDTH, 5 * WIDTH), BF16),
            pltpu.VMEM((WIDTH, WIDTH), BF16),
            pltpu.VMEM((WIDTH, 5 * WIDTH), BF16),
            pltpu.VMEM((WIDTH, WIDTH), BF16),
            [pltpu.VMEM((64 * BLOCK, WIDTH), F32)] * 2,
            pltpu.VMEM((64 * BLOCK, WIDTH), F32),
            [pltpu.VMEM((64 * BLOCK, WIDTH), F32)] * 2,
            pltpu.VMEM((8 * WIDTH, 2 * WIDTH), BF16),
            shares,
            shares,
            shares,
            block,
            block,
            shares,
            shares,
            all_sequences,
            all_sequences,
            pltpu.VMEM((GRID, 128, BLOCK * HIDDEN), BF16),
            gathered,
            gathered,
            block,
            gathered,
            gathered,
            block,
            gathered,
            gathered,
            gathered,
            gathered,
            gathered,
            gathered,
            gathered,
            gathered,
            gathered,
            pltpu.VMEM((HIDDEN * HIDDEN, WIDTH), F32),
            pltpu.VMEM((HIDDEN * WIDTH, WIDTH), BF16),
            pltpu.VMEM((HIDDEN * WIDTH, 4 * WIDTH), BF16),
            pltpu.VMEM((4 * WIDTH, HIDDEN * WIDTH), BF16),
            pltpu.VMEM((5 * WIDTH, WIDTH), BF16),
            pltpu.VMEM((WIDTH, WIDTH), BF16),
            pltpu.VMEM((5 * WIDTH, WIDTH), BF16),
            pltpu.VMEM((WIDTH, WIDTH), BF16),
            pltpu.VMEM((BLOCK * HIDDEN, BLOCK * HIDDEN), F32),
            wide_block,
            wide_block,
            wide_block,
            flat,
            pltpu.VMEM((10, BLOCK * BLOCK, WIDTH), F32),
            pltpu.VMEM((9, BLOCK * BLOCK, WIDTH), F32),
            flat,
            flat,
            pltpu.VMEM((2 * WIDTH, 4 * WIDTH), BF16),
            pltpu.VMEM((4, BLOCK * HIDDEN, BLOCK * HIDDEN), BF16),
            pltpu.VMEM((2, 64, BLOCK * HIDDEN), BF16),
            pltpu.VMEM((128, BLOCK * HIDDEN), BF16),
            shares,
            pltpu.VMEM((2, 8, BLOCK, WIDTH), BF16),
            half_block,
            pltpu.VMEM((2, 8, BLOCK, WIDTH), F32),
            half_wide,
            dma((4,)),
            dma((4,)),
            dma((2, 2)),
            dma((2, 2 * GRID)),
            dma((GRID, 2)),
            dma((8, GRID)),
            dma((GRID,)),
            dma((3,)),
            dma((28,)),
            dma((2,)),
            dma((2,)),
            dma((7,)),
            dma((2,)),
        ],
        compiler_params=pltpu.CompilerParams(
            collective_id=1, has_side_effects=True, vmem_limit_bytes=62 << 20
        ),
        name="pair_updates",
    )(homolog, factor_weight, pair_input, cotangent, *weights)


def hand_out_kernel(*refs):
    sources, targets, held = refs[:3], refs[3:6], refs[6:9]
    read_sem, write_sem = refs[9:]
    reads, writes = [], []
    for src, dst, buffer in zip(sources, targets, held):
        parts = 4 if src.shape[0] > 8 else 1
        rows = src.shape[0] // parts
        for part in range(parts):
            some = pl.ds(part * rows, rows)
            number = len(reads)
            reads.append(
                pltpu.make_async_copy(src.at[some], buffer.at[some], read_sem.at[number])
            )
            writes.append(
                pltpu.make_async_copy(buffer.at[some], dst.at[some], write_sem.at[number])
            )
    for copy in reads:
        copy.start()
    for read, write in zip(reads, writes):
        read.wait()
        write.start()
    for copy in writes:
        copy.wait()


def body(
    homolog_features,
    pair_input,
    cotangent,
    homolog_factor_matrix,
    outer_output_weight,
    outgoing_input_weight,
    outgoing_output_weight,
    incoming_input_weight,
    incoming_output_weight,
):
    sequences, residues, depth = homolog_features.shape
    homolog = homolog_features.reshape(sequences * residues, depth)
    factor_weight = homolog_factor_matrix.T
    results = pair_updates(
        homolog,
        factor_weight,
        pair_input,
        cotangent,
        (
            outer_output_weight,
            outgoing_input_weight,
            outgoing_output_weight,
            incoming_input_weight,
            incoming_output_weight,
        ),
    )
    anywhere = pl.BlockSpec(memory_space=pl.ANY)
    pair_output, pair_gradient, alignment_gradient = pl.pallas_call(
        hand_out_kernel,
        out_shape=tuple(jax.ShapeDtypeStruct(one.shape, one.dtype) for one in results),
        in_specs=[anywhere] * 3,
        out_specs=(anywhere,) * 3,
        scratch_shapes=[pltpu.VMEM(one.shape, one.dtype) for one in results]
        + [pltpu.SemaphoreType.DMA((6,))] * 2,
        compiler_params=pltpu.CompilerParams(vmem_limit_bytes=62 << 20),
        name="hand_out",
    )(*results)
    return pair_output, pair_gradient, alignment_gradient.reshape(sequences, residues, depth)


def solution(mesh):
    split = P("row", "col", None)
    return jax.shard_map(
        body,
        mesh=mesh,
        in_specs=(split, split, split, P(), P(), P(), P(), P(), P()),
        out_specs=(split, split, split),
        check_vma=False,
    )
```

```python
import jax
import jax.numpy as jnp
from jax import lax
from jax.experimental import pallas as pl
from jax.experimental.pallas import tpu as pltpu
from jax.sharding import PartitionSpec as P

SEQUENCES = 1024
EPSILON = 1e-05
MESH = pl.DeviceIdType.MESH
F32 = jnp.float32
BF16 = jnp.bfloat16
GRID = 8
BLOCK = 16
WIDTH = 128
HIDDEN = 32


def dot(lhs, rhs, dims=((1,), (0,))):
    return lax.dot_general(lhs, rhs, (dims, ((), ())), preferred_element_type=F32)


def layer_norm(inputs):
    centered = inputs - jnp.mean(inputs, axis=-1, keepdims=True)
    spread = jnp.mean(centered * centered, axis=-1, keepdims=True)
    scale = lax.rsqrt(spread + EPSILON)
    return centered * scale, scale


def layer_norm_pullback(normed, scale, upstream):
    along = jnp.mean(upstream * normed, axis=-1, keepdims=True)
    return scale * (upstream - jnp.mean(upstream, axis=-1, keepdims=True) - normed * along)


def repeat_factor(factor_weight, spread_factor):
    hidden_row = lax.broadcasted_iota(jnp.int32, (2 * HIDDEN, 2 * WIDTH), 0)
    hidden_lane = lax.broadcasted_iota(jnp.int32, (2 * HIDDEN, 2 * WIDTH), 1)
    repeats = (hidden_lane % HIDDEN + HIDDEN * (hidden_lane // WIDTH) == hidden_row).astype(F32)
    repeated = dot(factor_weight[...], repeats.astype(BF16), ((0,), (0,)))
    lane_quarter = lax.broadcasted_iota(jnp.int32, (2 * WIDTH, 2 * WIDTH), 1) % WIDTH // HIDDEN
    for q in range(4):
        spread_factor[q * 2 * WIDTH : (q + 1) * 2 * WIDTH, :] = jnp.where(
            lane_quarter == q, repeated, 0.0
        ).astype(BF16)


def pair_kernel(
    homolog_hbm,
    factor_weight_hbm,
    pair_input,
    cotangent,
    outer_weight_hbm,
    out_in_weight_hbm,
    out_out_weight_hbm,
    in_in_weight_hbm,
    in_out_weight_hbm,
    pair_output,
    pair_gradient,
    alignment_gradient,
    homolog,
    factor_weight,
    outer_weight,
    out_in_weight,
    out_out_weight,
    in_in_weight,
    in_out_weight,
    normed_msa,
    msa_scale,
    alignment,
    spread_factor,
    left_ic,
    left_ci,
    right_dj,
    right_jd,
    pair_block,
    cot_block,
    relay_left,
    relay_right,
    msa_relayed,
    msa_direct,
    o_left,
    o_right,
    o_right_stage,
    i_left,
    i_right,
    i_left_stage,
    ib_right,
    ib_left,
    ob_right,
    ob_left,
    left_parts,
    right_parts,
    left_parts2,
    right_parts2,
    wide_weight,
    table_weight,
    spread_weight,
    turned_weight,
    out_in_turned,
    out_out_turned,
    in_in_turned,
    in_out_turned,
    outer32,
    wide,
    cot_wide,
    cot_turned,
    flat,
    out_kept,
    in_kept,
    first,
    upstream32,
    stacked,
    grad_table,
    msa_cots,
    cot_parts,
    cot_got,
    output_stage,
    output_got,
    gradient_stage,
    gradient_got,
    relay_sem,
    relay_send_sem,
    block_sem,
    msa_sem,
    pair_sem,
    cot_sem,
    small_sem,
    send_sem,
    output_sem,
    gradient_sem,
    input_sem,
    alignment_sem,
):
    row, col = lax.axis_index("row"), lax.axis_index("col")
    a, h, b = row // 2, row % 2, col
    other = 1 - h
    odd = b % 2
    at = (a + 4 * odd) % GRID
    own_i = at * other + b * h
    own_j = b * other + at * h
    stays = jnp.logical_and(a == b, odd == 0)

    def chip_at(i, j):
        return (i + 4 * (j % 2)) % GRID, j

    def row_chip(n):
        return chip_at(at * other + n * h, n * other + b * h)

    def col_chip(n):
        return chip_at(n * other + at * h, b * other + n * h)

    def apart(k):
        m = k // 2
        return m + (m // 2) * (5 - 2 * m), k % 2

    def along_rows(own, k):
        dm, dv = apart(k)
        return (own // 4 + dv) % 2 * 4 + (own % 4 + dm) % 4

    def along_columns(own, k):
        dm, dv = apart(k)
        return (own // 2 + dm) % 4 * 2 + (own % 2 + dv) % 2

    def step_i(k):
        return along_rows(at, k) * other + along_columns(b, k) * h

    def step_j(k):
        return along_columns(b, k) * other + along_rows(at, k) * h

    relay_column = (a % 4 + b // 2 + 2 * (b % 4)) % 4 * 2 + a // 4
    relay_chip = chip_at(b, relay_column)
    source_row = b % 2 * 4 + (b // 2 + 16 - at // 2 - 2 * (at % 4)) % 4
    relay_stays = jnp.logical_and(relay_column == b, relay_chip[0] == a)

    def column(n):
        return n, b

    def line(n):
        return chip_at(at, n)

    def remote(src, dst, send, recv, chip, core):
        return pltpu.make_async_remote_copy(
            src_ref=src,
            dst_ref=dst,
            send_sem=send,
            recv_sem=recv,
            device_id=(2 * chip[0] + core, chip[1]),
            device_id_type=MESH,
        )

    def wait_for(ref, sem):
        pltpu.make_async_copy(ref, ref, sem).wait()

    barrier = pltpu.get_barrier_semaphore()

    def greet(chip, core):
        pl.semaphore_signal(
            barrier, inc=1, device_id=(2 * chip[0] + core, chip[1]), device_id_type=MESH
        )

    def greet_step(k, carry):
        for core in range(2):
            greet(column(along_rows(a, GRID - k)), core)
            greet(line(along_columns(b, GRID - k)), core)
        return carry

    @pl.when(jnp.logical_not(relay_stays))
    def _():
        greet((source_row, at), h)

    @pl.when(h == 1)
    def _():
        greet((b, at), 0)

    @pl.when(jnp.logical_and(h == 1, jnp.logical_not(stays)))
    def _():
        greet((b, at), 1)

    lax.fori_loop(1, GRID, greet_step, 0)
    greet((a, b), other)
    inputs = (
        (homolog_hbm, homolog),
        (factor_weight_hbm, factor_weight),
        (outer_weight_hbm, outer_weight),
        (out_in_weight_hbm, out_in_weight),
        (out_out_weight_hbm, out_out_weight),
        (in_in_weight_hbm, in_in_weight),
        (in_out_weight_hbm, in_out_weight),
    )
    copies = [
        pltpu.make_async_copy(src, dst, input_sem.at[number])
        for number, (src, dst) in enumerate(inputs)
    ]
    for copy in copies:
        copy.start()
    copies[0].wait()
    copies[1].wait()

    def normalize_step(n, carry):
        rows = pl.ds(pl.multiple_of(n * 256, 256), 256)
        normed, scale = layer_norm(homolog[rows, :].astype(F32))
        msa_scale[rows, :] = jnp.broadcast_to(scale, (256, WIDTH))
        normed_msa[0][rows, :] = normed[:, :WIDTH]
        normed_msa[1][rows, :] = normed[:, WIDTH:]
        return carry

    lax.fori_loop(0, 4, normalize_step, 0)
    repeat_factor(factor_weight, spread_factor)
    groups = []
    for g in range(4):
        pieces = [
            normed_msa[part][pl.ds(4 * g + q, 64, stride=BLOCK), :].astype(BF16)
            for q in range(4)
            for part in range(2)
        ]
        groups.append(jnp.concatenate(pieces, axis=1))
    factors = dot(jnp.concatenate(groups, axis=0), spread_factor[...]).astype(BF16)
    left_value = jnp.concatenate(
        [factors[g * 64 : (g + 1) * 64, :WIDTH] for g in range(4)], axis=1
    )
    right_value = jnp.concatenate(
        [factors[g * 64 : (g + 1) * 64, WIDTH:] for g in range(4)], axis=1
    )
    left_ic[...] = left_value
    right_jd[...] = right_value
    before = lax.broadcasted_iota(jnp.int32, (BLOCK * HIDDEN, BLOCK * HIDDEN), 0)
    after = lax.broadcasted_iota(jnp.int32, (BLOCK * HIDDEN, BLOCK * HIDDEN), 1)
    moved = (before == after % BLOCK * HIDDEN + after // BLOCK).astype(F32).astype(BF16)
    turned_factors = dot(jnp.concatenate([left_value, right_value], axis=0), moved).astype(BF16)
    left_ci[...] = turned_factors[:64]
    right_dj[...] = turned_factors[64:]

    for copy in copies[2:]:
        copy.wait()
    keeps_first = jnp.logical_and(h == 0, odd == 0)
    keeps_second = jnp.logical_and(h == 1, stays)
    pl.semaphore_wait(barrier, 31 - relay_stays.astype(jnp.int32) - keeps_second.astype(jnp.int32))

    for slot in range(4):
        src, dst = ((left_ci, relay_left), (right_dj, relay_right))[slot // 2]
        half = pl.ds(slot % 2 * 32, 32)

        @pl.when(jnp.logical_not(relay_stays))
        def _():
            remote(
                src.at[half],
                dst.at[half],
                relay_send_sem.at[slot],
                relay_sem.at[slot],
                relay_chip,
                h,
            ).start()

        @pl.when(relay_stays)
        def _():
            pltpu.make_async_copy(src.at[half], dst.at[half], relay_sem.at[slot]).start()

    def msa_send(src, dst, sems, slot, chip_of, core, send, half=None):
        whole = half is None
        source = src if whole else src.at[pl.ds(half * 32, 32)]
        target = dst.at[slot] if whole else dst.at[slot, pl.ds(half * 32, 32)]

        def step(k, carry):
            place = (GRID - 1 - k) * other + k * h

            @pl.when(jnp.logical_or(place > 0, h != core))
            def _():
                remote(source, target, send, sems.at[slot], chip_of(place), core).start()

            return carry

        lax.fori_loop(0, GRID, step, 0)

        @pl.when(h == core)
        def _():
            pltpu.make_async_copy(source, target, sems.at[slot]).start()

    def column_step(k):
        return column(along_rows(a, k))

    def line_step(k):
        return line(along_columns(b, k))

    def msa_sent(src, dst, core, send):
        @pl.when(h == core)
        def _():
            wait_for(dst.at[pl.ds(0, 7)], send)

        @pl.when(h != core)
        def _():
            wait_for(dst.at[pl.ds(0, 8)], send)

    msa_send(right_jd, msa_direct, msa_sem.at[1], row, column_step, 0, send_sem.at[2])
    msa_send(left_ic, msa_direct, msa_sem.at[1], row, column_step, 1, send_sem.at[3])

    for slot, (src, dst) in enumerate(((pair_input, pair_block), (cotangent, cot_block))):
        half = dst.at[pl.ds(h * 8, 8)]
        sem = block_sem.at[slot, h]

        @pl.when(keeps_first)
        def _():
            pltpu.make_async_copy(src, half, sem).start()

        @pl.when(jnp.logical_not(keeps_first))
        def _():
            remote(src, half, send_sem.at[4 + slot], sem, chip_at(a, b), 0).start()

        @pl.when(keeps_second)
        def _():
            pltpu.make_async_copy(src, half, sem).start()

        @pl.when(jnp.logical_not(keeps_second))
        def _():
            remote(src, half, send_sem.at[6 + slot], sem, chip_at(b, a), 1).start()

    def block_sent(slot, src):
        @pl.when(jnp.logical_not(keeps_first))
        def _():
            wait_for(src, send_sem.at[4 + slot])

        @pl.when(jnp.logical_not(keeps_second))
        def _():
            wait_for(src, send_sem.at[6 + slot])

    relay_slot = 2 * source_row + h
    for slot in range(4):
        half = slot % 2
        src = (relay_left, relay_right)[slot // 2]
        wait_for(src.at[pl.ds(half * 32, 32)], relay_sem.at[slot])
        kind = slot // 2
        msa_send(
            src, msa_relayed, msa_sem.at[0], relay_slot, line_step, kind, send_sem.at[8 + kind], half
        )

    wide_weight[...] = outer_weight[...].astype(F32)
    spread_weight[...] = jnp.zeros(spread_weight.shape, BF16)

    def weight_step(n, carry):
        start = pl.multiple_of(n * WIDTH, WIDTH)

        def lay_out(piece):
            for q in range(4):
                some = pl.ds(start + q * HIDDEN, HIDDEN)
                table_weight[some, :] = piece
                spread_weight[some, q * WIDTH : (q + 1) * WIDTH] = piece

        @pl.when(h == 0)
        def _():
            lay_out(outer_weight[pl.ds(pl.multiple_of(n * HIDDEN, HIDDEN), HIDDEN), :])

        @pl.when(h == 1)
        def _():
            lay_out(wide_weight[pl.ds(n, HIDDEN, stride=HIDDEN), :].astype(BF16))

        return carry

    lax.fori_loop(0, HIDDEN, weight_step, 0)

    def turn_step(n, carry):
        rows = pl.ds(pl.multiple_of(n * 2 * WIDTH, 2 * WIDTH), 2 * WIDTH)
        turned_weight[:, rows] = spread_weight[rows, :].T
        return carry

    lax.fori_loop(0, HIDDEN // 2, turn_step, 0)
    for weight, turned_one in (
        (out_in_weight, out_in_turned),
        (out_out_weight, out_out_turned),
        (in_in_weight, in_in_turned),
        (in_out_weight, in_out_turned),
    ):
        turned_one[...] = weight[...].T

    def outer_step(k, carry):
        n = (b // 2 + k) % 4

        def msa_wait(part, carry):
            slot = 4 * n + part
            wait_for(msa_relayed.at[slot], msa_sem.at[0, slot])
            wait_for(msa_direct.at[slot], msa_sem.at[1, slot])
            return carry

        lax.fori_loop(0, 4, msa_wait, 0)
        four = pl.ds(4 * n, 4)
        outer32[...] += dot(
            msa_relayed[four].reshape(256, BLOCK * HIDDEN),
            msa_direct[four].reshape(256, BLOCK * HIDDEN),
            ((0,), (0,)),
        )
        return carry

    outer32[...] = jnp.zeros(outer32.shape, F32)
    lax.fori_loop(0, 4, outer_step, 0)
    lane_part = lax.broadcasted_iota(jnp.int32, (BLOCK, WIDTH), 1) // HIDDEN

    def project_step(d8, total):
        columns = []
        for part in range(8):
            tile = outer32[pl.ds(pl.multiple_of((8 * d8 + part) * BLOCK, BLOCK), BLOCK), :]
            columns.append(
                jnp.concatenate(
                    [
                        jnp.where(lane_part == q, tile[:, g * WIDTH : (g + 1) * WIDTH], 0.0)
                        for q in range(4)
                        for g in range(4)
                    ],
                    axis=0,
                )
            )
        picked = (jnp.concatenate(columns, axis=1) * (1.0 / SEQUENCES)).astype(BF16)
        weight = table_weight[pl.ds(pl.multiple_of(d8 * 8 * WIDTH, 8 * WIDTH), 8 * WIDTH), :]
        return total + dot(picked, weight)

    projected = lax.fori_loop(
        0, HIDDEN // 8, project_step, jnp.zeros((BLOCK * BLOCK, WIDTH), F32)
    )
    for part in range(2):
        wait_for(pair_block.at[pl.ds(part * 8, 8)], block_sem.at[0, part])
        wait_for(cot_block.at[pl.ds(part * 8, 8)], block_sem.at[1, part])
    for r in range(BLOCK):
        start = ((r % 4) * 4 + r // 4) * BLOCK
        flat[pl.ds(r * BLOCK, BLOCK), :] = projected[start : start + BLOCK]

    def add_rows(i, value):
        first[pl.ds(i * BLOCK, BLOCK), :] = (
            (pair_block[i].astype(F32) + value).astype(BF16).astype(F32)
        )

    @pl.when(h == 0)
    def _():
        for i in range(BLOCK):
            add_rows(i, flat[pl.ds(i, BLOCK, stride=BLOCK), :])

    @pl.when(h == 1)
    def _():
        for i in range(BLOCK):
            add_rows(i, flat[pl.ds(i * BLOCK, BLOCK), :])

    def send_same(dst, sems, chips, steps, send):
        own = steps(0)

        def step(k, carry):
            chip = chips(steps(GRID - k))
            remote(dst.at[own], dst.at[own], send, sems.at[own], chip, h).start()
            return carry

        lax.fori_loop(1, GRID, step, 0)

    def send_other(src, dst, sems, chips, steps, send):
        own = steps(0)

        def step(k, carry):
            chip = chips(steps(GRID - 1 - k))
            remote(src, dst.at[own], send, sems.at[own], chip, other).start()
            return carry

        lax.fori_loop(0, GRID, step, 0)

    def block_product(totals, left, by_column, right):
        def inner(group, totals):
            totals = list(totals)
            for u in range(4):
                t = group * 4 + u
                across = right(t)
                for p in range(BLOCK):
                    one = left[t, pl.ds(p, 1), :] if by_column else left[p, pl.ds(t, 1), :]
                    totals[p] = totals[p] + one * across
            return tuple(totals)

        return lax.fori_loop(0, BLOCK // 4, inner, totals)

    def no_totals():
        return tuple(jnp.zeros((BLOCK, WIDTH), F32) for _ in range(BLOCK))

    def contract(left, left_sem, left_own, by_column, right, right_sem, right_own, steps):
        def arrive(ref, sems, slot, skip):
            if skip is None:
                wait_for(ref.at[slot], sems.at[slot])
            else:

                @pl.when(slot != skip)
                def _():
                    wait_for(ref.at[slot], sems.at[slot])

        def block_step(k, totals):
            slot = steps(k)
            arrive(left, left_sem, slot, left_own)
            arrive(right, right_sem, slot, right_own)
            wide[...] = left[slot].astype(F32)
            return block_product(totals, wide, by_column, lambda t: right[slot, t].astype(F32))

        totals = lax.fori_loop(0, GRID, block_step, no_totals())
        return jnp.concatenate(totals, axis=0)

    def partial(part, n, totals):
        for p in range(BLOCK):
            part[n, p] = totals[p].astype(BF16)

    def sum_of(parts, sems, skip, steps):
        def step(k, total):
            slot = steps(k)
            if skip is None:
                wait_for(parts.at[slot], sems.at[slot])
            else:

                @pl.when(slot != skip)
                def _():
                    wait_for(parts.at[slot], sems.at[slot])

            return total + parts[slot].reshape(BLOCK * BLOCK, WIDTH).astype(F32)

        return lax.fori_loop(0, GRID, step, jnp.zeros((BLOCK * BLOCK, WIDTH), F32))

    def send_part(part, n, dst, slot, sems, chips, core, send):
        remote(part.at[n], dst.at[slot], send, sems.at[slot], chips(n), core).start()

    def turned(value, store):
        flat[...] = value
        for j in range(BLOCK):
            store(j, flat[pl.ds(j, BLOCK, stride=BLOCK), :].astype(BF16))

    def turn_cot(value):
        rounded = value.astype(BF16).astype(F32)
        cot_wide[...] = rounded.reshape(BLOCK, BLOCK, WIDTH)
        flat[...] = rounded
        for j in range(BLOCK):
            cot_turned[j] = flat[pl.ds(j, BLOCK, stride=BLOCK), :]

    def blocked(value):
        return value.astype(BF16).reshape(BLOCK, BLOCK, WIDTH)

    def gated(normed, weight, at):
        projected = dot(normed, weight[:, at * WIDTH : (at + 2) * WIDTH])
        gate, value = jax.nn.sigmoid(projected[:, :WIDTH]), projected[:, WIDTH:]
        return gate, value

    def keep_gated(ref, first_at, gate, value):
        ref[first_at] = value * gate * (1.0 - gate)
        ref[first_at + 1] = gate

    def keep_norm(ref, first_at, normed, scale):
        ref[first_at] = normed
        ref[first_at + 1] = jnp.broadcast_to(scale, normed.shape)

    normed, scale = layer_norm(first[...])
    rounded = normed.astype(BF16)
    left_gate, left_value = gated(rounded, out_in_weight, 0)
    o_left[own_j] = blocked(left_gate * left_value)
    send_same(o_left, pair_sem.at[0], row_chip, step_j, send_sem.at[10])
    right_gate, right_value = gated(rounded, out_in_weight, 2)

    def store_right(j, value):
        o_right_stage[j] = value

    turned(right_gate * right_value, store_right)
    send_other(o_right_stage, o_right, pair_sem.at[1], row_chip, step_j, send_sem.at[11])
    keep_gated(out_kept, 0, left_gate, left_value)
    keep_gated(out_kept, 2, right_gate, right_value)
    keep_norm(out_kept, 4, normed, scale)
    out_kept[6] = jax.nn.sigmoid(dot(rounded, out_in_weight[:, 4 * WIDTH :]))
    mixing = contract(
        o_left,
        pair_sem.at[0],
        own_j,
        False,
        o_right,
        pair_sem.at[1],
        None,
        step_j,
    )
    mixing_normed, mixing_scale = layer_norm(mixing)
    update = dot(mixing_normed.astype(BF16), out_out_weight[...])
    second = (first[...] + out_kept[6] * update).astype(BF16).astype(F32)

    normed, scale = layer_norm(second)
    rounded = normed.astype(BF16)
    right_gate, right_value = gated(rounded, in_in_weight, 2)
    i_right[own_i] = blocked(right_gate * right_value)
    send_same(i_right, pair_sem.at[4], col_chip, step_i, send_sem.at[14])
    left_gate, left_value = gated(rounded, in_in_weight, 0)
    i_left_stage[...] = blocked(left_gate * left_value)
    send_other(i_left_stage, i_left, pair_sem.at[5], col_chip, step_i, send_sem.at[15])
    keep_norm(out_kept, 7, mixing_normed, mixing_scale)
    out_kept[9] = update
    keep_gated(in_kept, 0, left_gate, left_value)
    keep_gated(in_kept, 2, right_gate, right_value)
    keep_norm(in_kept, 4, normed, scale)
    gating = jax.nn.sigmoid(dot(rounded, in_in_weight[:, 4 * WIDTH :]))
    in_kept[6] = gating
    in_kept[7] = second
    upstream = cot_block[...].reshape(BLOCK * BLOCK, WIDTH).astype(F32)
    upstream32[...] = upstream
    in_kept[8] = dot((upstream * gating).astype(BF16), in_out_turned[...])
    mixing = contract(
        i_left,
        pair_sem.at[5],
        None,
        True,
        i_right,
        pair_sem.at[4],
        own_i,
        step_i,
    )

    def input_pullback(kept, left_cot, right_cot, gating_part, weight, upstream):
        pieces = [
            (left_cot * kept[0]).astype(BF16),
            (left_cot * kept[1]).astype(BF16),
            (right_cot * kept[2]).astype(BF16),
            (right_cot * kept[3]).astype(BF16),
        ]
        normed_cot = gating_part + dot(
            jnp.concatenate(pieces, axis=1), weight[: 4 * WIDTH, :]
        )
        return upstream + layer_norm_pullback(kept[4], kept[5], normed_cot)

    normed, scale = layer_norm(mixing)
    turn_cot(layer_norm_pullback(normed, scale, in_kept[8]))

    def incoming_step(k, carry):
        n = step_i(GRID - 1 - k)
        wide[...] = i_right[n].astype(F32)
        totals = block_product(no_totals(), wide, False, lambda t: cot_turned[t])
        partial(left_parts, n, totals)
        send_part(
            left_parts, n, ib_left, own_j, pair_sem.at[2], row_chip, other, send_sem.at[12]
        )
        wide[...] = i_left[n].astype(F32)
        totals = block_product(no_totals(), wide, False, lambda t: cot_wide[t])

        @pl.when(n != own_i)
        def _():
            partial(right_parts, n, totals)
            send_part(
                right_parts, n, ib_right, own_i, pair_sem.at[3], col_chip, h, send_sem.at[13]
            )

        @pl.when(n == own_i)
        def _():
            partial(ib_right, n, totals)

        return carry

    lax.fori_loop(0, GRID, incoming_step, 0)
    gating = in_kept[6]
    update = dot(normed.astype(BF16), in_out_weight[...])
    result = (in_kept[7] + gating * update).astype(BF16)
    gating_cot = upstream32[...] * update * gating * (1.0 - gating)
    gating_part = dot(gating_cot.astype(BF16), in_in_turned[4 * WIDTH :, :])

    def hand_over(value, stage, got, sem, send):
        stage[...] = value.reshape(2, 8, BLOCK, WIDTH)
        for part in range(2):
            order = remote(stage.at[part], got, send.at[part], sem, (at, b), part)
            if part == 0:
                pl.when(odd == 1)(order.start)
            else:
                order.start()

    @pl.when(h == 0)
    def _():
        hand_over(result, output_stage, output_got, small_sem.at[0], output_sem)

    left_cot = sum_of(ib_left, pair_sem.at[2], None, step_j)
    right_cot = sum_of(ib_right, pair_sem.at[3], own_i, step_i)
    second_cot = input_pullback(
        in_kept, left_cot, right_cot, gating_part, in_in_turned, upstream32[...]
    )

    normed_cot = dot((second_cot * out_kept[6]).astype(BF16), out_out_turned[...])
    turn_cot(layer_norm_pullback(out_kept[7], out_kept[8], normed_cot))

    def outgoing_step(k, carry):
        n = step_j(GRID - 1 - k)
        wide[...] = o_right[n].astype(F32)
        totals = block_product(no_totals(), wide, False, lambda t: cot_turned[t])

        @pl.when(n != own_j)
        def _():
            partial(left_parts2, n, totals)
            send_part(
                left_parts2, n, ob_left, own_j, pair_sem.at[6], row_chip, h, send_sem.at[16]
            )

        @pl.when(n == own_j)
        def _():
            partial(ob_left, n, totals)

        totals = block_product(
            no_totals(), cot_wide, True, lambda t: o_left[n, t].astype(F32)
        )
        partial(right_parts2, n, totals)
        send_part(
            right_parts2, n, ob_right, own_i, pair_sem.at[7], col_chip, other, send_sem.at[17]
        )
        return carry

    lax.fori_loop(0, GRID, outgoing_step, 0)
    gating = out_kept[6]
    gating_cot = second_cot * out_kept[9] * gating * (1.0 - gating)
    gating_part = dot(gating_cot.astype(BF16), out_in_turned[4 * WIDTH :, :])
    flat[...] = sum_of(ob_left, pair_sem.at[6], own_j, step_j)
    left_cot = jnp.concatenate(
        [flat[pl.ds(j, BLOCK, stride=BLOCK), :] for j in range(BLOCK)], axis=0
    )
    right_cot = sum_of(ob_right, pair_sem.at[7], None, step_i)
    gradient = input_pullback(
        out_kept, left_cot, right_cot, gating_part, out_in_turned, second_cot
    )

    @pl.when(h == 0)
    def _():
        hand_over(gradient, gradient_stage, gradient_got, small_sem.at[1], gradient_sem)

    def stack(r, value):
        g, q = r // 4, r % 4
        stacked[g * BLOCK : (g + 1) * BLOCK, q * WIDTH : (q + 1) * WIDTH] = value.astype(BF16)

    flat[...] = gradient

    @pl.when(h == 0)
    def _():
        for r in range(BLOCK):
            stack(r, flat[pl.ds(r, BLOCK, stride=BLOCK), :])

    @pl.when(h == 1)
    def _():
        for r in range(BLOCK):
            stack(r, flat[pl.ds(r * BLOCK, BLOCK), :])

    for x8 in range(HIDDEN // 8):
        chunk = dot(
            stacked[...], turned_weight[:, x8 * 8 * WIDTH : (x8 + 1) * 8 * WIDTH]
        ).astype(BF16)
        for piece in range(8):
            start = (8 * x8 + piece) * BLOCK
            for g in range(4):
                grad_table[start : start + BLOCK, g * WIDTH : (g + 1) * WIDTH] = chunk[
                    g * BLOCK : (g + 1) * BLOCK, piece * WIDTH : (piece + 1) * WIDTH
                ]

    def cot_step(step, carry):
        chips = [along_rows(a, GRID - 1 - 2 * step - n) for n in range(2)]
        sequences = jnp.concatenate(
            [
                msa_relayed[pl.ds(2 * chip, 2)].reshape(2 * 64, BLOCK * HIDDEN)
                for chip in chips
            ],
            axis=0,
        )
        sums = dot(sequences, grad_table[...]).astype(BF16)
        for n, chip in enumerate(chips):
            for core in range(2):
                start = (2 * n + core) * 64
                slot = 2 * chip + core
                cot_parts[slot] = sums[start : start + 64]
                target = cot_got.at[h, a]

                @pl.when(slot == row)
                def _():
                    pltpu.make_async_copy(cot_parts.at[slot], target, cot_sem.at[h, a]).start()

                @pl.when(slot != row)
                def _():
                    remote(
                        cot_parts.at[slot], target, send_sem.at[26], cot_sem.at[h, a], (chip, b), core
                    ).start()

        return carry

    lax.fori_loop(0, 4, cot_step, 0)
    for core in range(2):

        def cot_sum(k, total, core=core):
            n = along_rows(a, k)
            wait_for(cot_got.at[core, n], cot_sem.at[core, n])
            return total + cot_got[core, n].astype(F32)

        total = lax.fori_loop(0, GRID, cot_sum, jnp.zeros((64, BLOCK * HIDDEN), F32))
        msa_cots[1 - core] = (total * (1.0 / SEQUENCES)).astype(BF16)

    cots = jnp.concatenate(
        [
            jnp.concatenate(
                [msa_cots[kind, :, g * WIDTH : (g + 1) * WIDTH] for kind in range(2)], axis=1
            )
            for g in range(4)
        ],
        axis=0,
    )
    for q in range(4):
        normed_cots = dot(
            cots, spread_factor[q * 2 * WIDTH : (q + 1) * 2 * WIDTH, :], ((1,), (1,))
        )
        for g in range(4):
            rows = pl.ds(4 * g + q, 64, stride=BLOCK)
            value = layer_norm_pullback(
                jnp.concatenate([normed_msa[0][rows, :], normed_msa[1][rows, :]], axis=1),
                msa_scale[rows, :1],
                normed_cots[g * 64 : (g + 1) * 64],
            )
            for part in range(2):
                alignment[part][rows, :] = value[:, part * WIDTH : (part + 1) * WIDTH]
    alignment_copies = [
        pltpu.make_async_copy(
            alignment[part],
            alignment_gradient.at[:, pl.ds(part * WIDTH, WIDTH)],
            alignment_sem.at[part],
        )
        for part in range(2)
    ]
    for copy in alignment_copies:
        copy.start()

    @pl.when(keeps_first)
    def _():
        pair_output[...] = output_stage[0]
        pair_gradient[...] = gradient_stage[0]

    @pl.when(jnp.logical_not(keeps_first))
    def _():
        wait_for(output_got, small_sem.at[0])
        pair_output[...] = output_got[...]
        wait_for(gradient_got, small_sem.at[1])
        pair_gradient[...] = gradient_got[...]

    @pl.when(jnp.logical_not(relay_stays))
    def _():
        for slot in range(4):
            wait_for(relay_left.at[pl.ds(0, 32)], relay_send_sem.at[slot])

    msa_sent(right_jd, msa_direct, 0, send_sem.at[2])
    msa_sent(left_ic, msa_direct, 1, send_sem.at[3])
    block_sent(0, pair_input)
    block_sent(1, cotangent)
    msa_sent(relay_left, msa_relayed, 0, send_sem.at[8])
    msa_sent(relay_right, msa_relayed, 1, send_sem.at[9])
    for number in (10, 13, 14, 16):
        wait_for(o_left.at[pl.ds(0, 7)], send_sem.at[number])
    for number in (11, 12, 15, 17):
        wait_for(o_left, send_sem.at[number])
    wait_for(cot_parts.at[pl.ds(0, 15)], send_sem.at[26])

    @pl.when(h == 0)
    def _():
        wait_for(output_got, output_sem.at[1])
        wait_for(gradient_got, gradient_sem.at[1])

        @pl.when(odd == 1)
        def _():
            wait_for(output_got, output_sem.at[0])
            wait_for(gradient_got, gradient_sem.at[0])

    for copy in alignment_copies:
        copy.wait()


def pair_updates(homolog, factor_weight, pair_input, cotangent, weights):
    gathered = pltpu.VMEM((GRID, BLOCK, BLOCK, WIDTH), BF16)
    block = pltpu.VMEM((BLOCK, BLOCK, WIDTH), BF16)
    flat = pltpu.VMEM((BLOCK * BLOCK, WIDTH), F32)
    shares = pltpu.VMEM((64, BLOCK * HIDDEN), BF16)
    all_sequences = pltpu.VMEM((2 * GRID, 64, BLOCK * HIDDEN), BF16)
    half_block = pltpu.VMEM((8, BLOCK, WIDTH), BF16)
    wide_block = pltpu.VMEM((BLOCK, BLOCK, WIDTH), F32)
    half_wide = pltpu.VMEM((8, BLOCK, WIDTH), F32)
    dma = pltpu.SemaphoreType.DMA
    vmem = pl.BlockSpec(memory_space=pltpu.VMEM)
    return pl.pallas_call(
        pair_kernel,
        out_shape=(
            jax.ShapeDtypeStruct((8, BLOCK, WIDTH), BF16),
            jax.ShapeDtypeStruct((8, BLOCK, WIDTH), F32),
            jax.ShapeDtypeStruct((64 * BLOCK, 2 * WIDTH), F32),
        ),
        in_specs=[pl.BlockSpec(memory_space=pl.ANY)] * 9,
        out_specs=(vmem, vmem, pl.BlockSpec(memory_space=pl.ANY)),
        scratch_shapes=[
            pltpu.VMEM((64 * BLOCK, 2 * WIDTH), BF16),
            pltpu.VMEM((2 * HIDDEN, 2 * WIDTH), BF16),
            pltpu.VMEM((HIDDEN * HIDDEN, WIDTH), BF16),
            pltpu.VMEM((WIDTH, 5 * WIDTH), BF16),
            pltpu.VMEM((WIDTH, WIDTH), BF16),
            pltpu.VMEM((WIDTH, 5 * WIDTH), BF16),
            pltpu.VMEM((WIDTH, WIDTH), BF16),
            [pltpu.VMEM((64 * BLOCK, WIDTH), F32)] * 2,
            pltpu.VMEM((64 * BLOCK, WIDTH), F32),
            [pltpu.VMEM((64 * BLOCK, WIDTH), F32)] * 2,
            pltpu.VMEM((8 * WIDTH, 2 * WIDTH), BF16),
            shares,
            shares,
            shares,
            shares,
            block,
            block,
            shares,
            shares,
            all_sequences,
            all_sequences,
            gathered,
            gathered,
            block,
            gathered,
            gathered,
            block,
            gathered,
            gathered,
            gathered,
            gathered,
            gathered,
            gathered,
            gathered,
            gathered,
            pltpu.VMEM((HIDDEN * HIDDEN, WIDTH), F32),
            pltpu.VMEM((HIDDEN * WIDTH, WIDTH), BF16),
            pltpu.VMEM((HIDDEN * WIDTH, 4 * WIDTH), BF16),
            pltpu.VMEM((4 * WIDTH, HIDDEN * WIDTH), BF16),
            pltpu.VMEM((5 * WIDTH, WIDTH), BF16),
            pltpu.VMEM((WIDTH, WIDTH), BF16),
            pltpu.VMEM((5 * WIDTH, WIDTH), BF16),
            pltpu.VMEM((WIDTH, WIDTH), BF16),
            pltpu.VMEM((BLOCK * HIDDEN, BLOCK * HIDDEN), F32),
            wide_block,
            wide_block,
            wide_block,
            flat,
            pltpu.VMEM((10, BLOCK * BLOCK, WIDTH), F32),
            pltpu.VMEM((9, BLOCK * BLOCK, WIDTH), F32),
            flat,
            flat,
            pltpu.VMEM((64, 4 * WIDTH), BF16),
            pltpu.VMEM((BLOCK * HIDDEN, BLOCK * HIDDEN), BF16),
            pltpu.VMEM((2, 64, BLOCK * HIDDEN), BF16),
            all_sequences,
            pltpu.VMEM((2, GRID, 64, BLOCK * HIDDEN), BF16),
            pltpu.VMEM((2, 8, BLOCK, WIDTH), BF16),
            half_block,
            pltpu.VMEM((2, 8, BLOCK, WIDTH), F32),
            half_wide,
            dma((4,)),
            dma((4,)),
            dma((2, 2)),
            dma((2, 2 * GRID)),
            dma((8, GRID)),
            dma((2, GRID)),
            dma((2,)),
            dma((28,)),
            dma((2,)),
            dma((2,)),
            dma((7,)),
            dma((2,)),
        ],
        compiler_params=pltpu.CompilerParams(
            collective_id=1, has_side_effects=True, vmem_limit_bytes=62 << 20
        ),
        name="pair_updates",
    )(homolog, factor_weight, pair_input, cotangent, *weights)


def hand_out_kernel(*refs):
    sources, targets, held = refs[:3], refs[3:6], refs[6:9]
    read_sem, write_sem = refs[9:]
    reads, writes = [], []
    for src, dst, buffer in zip(sources, targets, held):
        parts = 4 if src.shape[0] > 8 else 1
        rows = src.shape[0] // parts
        for part in range(parts):
            some = pl.ds(part * rows, rows)
            number = len(reads)
            reads.append(
                pltpu.make_async_copy(src.at[some], buffer.at[some], read_sem.at[number])
            )
            writes.append(
                pltpu.make_async_copy(buffer.at[some], dst.at[some], write_sem.at[number])
            )
    for copy in reads:
        copy.start()
    for read, write in zip(reads, writes):
        read.wait()
        write.start()
    for copy in writes:
        copy.wait()


def body(
    homolog_features,
    pair_input,
    cotangent,
    homolog_factor_matrix,
    outer_output_weight,
    outgoing_input_weight,
    outgoing_output_weight,
    incoming_input_weight,
    incoming_output_weight,
):
    sequences, residues, depth = homolog_features.shape
    homolog = homolog_features.reshape(sequences * residues, depth)
    factor_weight = homolog_factor_matrix.T
    results = pair_updates(
        homolog,
        factor_weight,
        pair_input,
        cotangent,
        (
            outer_output_weight,
            outgoing_input_weight,
            outgoing_output_weight,
            incoming_input_weight,
            incoming_output_weight,
        ),
    )
    anywhere = pl.BlockSpec(memory_space=pl.ANY)
    pair_output, pair_gradient, alignment_gradient = pl.pallas_call(
        hand_out_kernel,
        out_shape=tuple(jax.ShapeDtypeStruct(one.shape, one.dtype) for one in results),
        in_specs=[anywhere] * 3,
        out_specs=(anywhere,) * 3,
        scratch_shapes=[pltpu.VMEM(one.shape, one.dtype) for one in results]
        + [pltpu.SemaphoreType.DMA((6,))] * 2,
        compiler_params=pltpu.CompilerParams(vmem_limit_bytes=62 << 20),
        name="hand_out",
    )(*results)
    return pair_output, pair_gradient, alignment_gradient.reshape(sequences, residues, depth)


def solution(mesh):
    split = P("row", "col", None)
    return jax.shard_map(
        body,
        mesh=mesh,
        in_specs=(split, split, split, P(), P(), P(), P(), P(), P()),
        out_specs=(split, split, split),
        check_vma=False,
    )
```

```python
import jax
import jax.numpy as jnp
from jax import lax
from jax.experimental import pallas as pl
from jax.experimental.pallas import tpu as pltpu
from jax.sharding import PartitionSpec as P

SEQUENCES = 1024
EPSILON = 1e-05
MESH = pl.DeviceIdType.MESH
F32 = jnp.float32
BF16 = jnp.bfloat16
GRID = 8
BLOCK = 16
WIDTH = 128
HIDDEN = 32


def dot(lhs, rhs, dims=((1,), (0,))):
    return lax.dot_general(lhs, rhs, (dims, ((), ())), preferred_element_type=F32)


def layer_norm(inputs):
    centered = inputs - jnp.mean(inputs, axis=-1, keepdims=True)
    spread = jnp.mean(centered * centered, axis=-1, keepdims=True)
    scale = lax.rsqrt(spread + EPSILON)
    return centered * scale, scale


def layer_norm_pullback(normed, scale, upstream):
    along = jnp.mean(upstream * normed, axis=-1, keepdims=True)
    return scale * (upstream - jnp.mean(upstream, axis=-1, keepdims=True) - normed * along)


def repeat_factor(factor_weight, spread_factor):
    hidden_row = lax.broadcasted_iota(jnp.int32, (2 * HIDDEN, 2 * WIDTH), 0)
    hidden_lane = lax.broadcasted_iota(jnp.int32, (2 * HIDDEN, 2 * WIDTH), 1)
    repeats = (hidden_lane % HIDDEN + HIDDEN * (hidden_lane // WIDTH) == hidden_row).astype(F32)
    repeated = dot(factor_weight[...], repeats.astype(BF16), ((0,), (0,)))
    lane_quarter = lax.broadcasted_iota(jnp.int32, (2 * WIDTH, 2 * WIDTH), 1) % WIDTH // HIDDEN
    for q in range(4):
        spread_factor[q * 2 * WIDTH : (q + 1) * 2 * WIDTH, :] = jnp.where(
            lane_quarter == q, repeated, 0.0
        ).astype(BF16)


def pair_kernel(
    homolog_hbm,
    factor_weight_hbm,
    pair_input,
    cotangent,
    outer_weight_hbm,
    out_in_weight_hbm,
    out_out_weight_hbm,
    in_in_weight_hbm,
    in_out_weight_hbm,
    pair_output,
    pair_gradient,
    alignment_first,
    alignment_second,
    homolog,
    factor_weight,
    outer_weight,
    out_in_weight,
    out_out_weight,
    in_in_weight,
    in_out_weight,
    normed_msa,
    msa_scale,
    spread_factor,
    left_ic,
    left_ci,
    right_dj,
    right_jd,
    pair_block,
    cot_block,
    relay_left,
    relay_right,
    msa_relayed,
    msa_direct,
    o_left,
    o_right,
    o_right_stage,
    i_left,
    i_right,
    i_left_stage,
    ib_right,
    ib_left,
    ob_right,
    ob_left,
    left_parts,
    right_parts,
    left_parts2,
    right_parts2,
    wide_weight,
    table_weight,
    spread_weight,
    turned_weight,
    out_in_turned,
    out_out_turned,
    in_in_turned,
    in_out_turned,
    outer32,
    wide,
    cot_wide,
    cot_turned,
    flat,
    out_kept,
    in_kept,
    first,
    upstream32,
    stacked,
    grad_table,
    msa_cots,
    cot_parts,
    cot_got,
    output_stage,
    output_got,
    gradient_stage,
    gradient_got,
    relay_sem,
    relay_send_sem,
    block_sem,
    msa_sem,
    pair_sem,
    cot_sem,
    small_sem,
    send_sem,
    output_sem,
    gradient_sem,
    input_sem,
):
    row, col = lax.axis_index("row"), lax.axis_index("col")
    a, h, b = row // 2, row % 2, col
    other = 1 - h
    odd = b % 2
    at = (a + 4 * odd) % GRID
    own_i = at * other + b * h
    own_j = b * other + at * h
    stays = jnp.logical_and(a == b, odd == 0)

    def chip_at(i, j):
        return (i + 4 * (j % 2)) % GRID, j

    def row_chip(n):
        return chip_at(at * other + n * h, n * other + b * h)

    def col_chip(n):
        return chip_at(n * other + at * h, b * other + n * h)

    def apart(k):
        m = k // 2
        return m + (m // 2) * (5 - 2 * m), k % 2

    def along_rows(own, k):
        dm, dv = apart(k)
        return (own // 4 + dv) % 2 * 4 + (own % 4 + dm) % 4

    def along_columns(own, k):
        dm, dv = apart(k)
        return (own // 2 + dm) % 4 * 2 + (own % 2 + dv) % 2

    def step_i(k):
        return along_rows(at, k) * other + along_columns(b, k) * h

    def step_j(k):
        return along_columns(b, k) * other + along_rows(at, k) * h

    relay_column = (a % 4 + b // 2 + 2 * (b % 4)) % 4 * 2 + a // 4
    relay_chip = chip_at(b, relay_column)
    source_row = b % 2 * 4 + (b // 2 + 16 - at // 2 - 2 * (at % 4)) % 4
    relay_stays = jnp.logical_and(relay_column == b, relay_chip[0] == a)

    def column(n):
        return n, b

    def line(n):
        return chip_at(at, n)

    def remote(src, dst, send, recv, chip, core):
        return pltpu.make_async_remote_copy(
            src_ref=src,
            dst_ref=dst,
            send_sem=send,
            recv_sem=recv,
            device_id=(2 * chip[0] + core, chip[1]),
            device_id_type=MESH,
        )

    def wait_for(ref, sem):
        pltpu.make_async_copy(ref, ref, sem).wait()

    barrier = pltpu.get_barrier_semaphore()

    def greet(chip, core):
        pl.semaphore_signal(
            barrier, inc=1, device_id=(2 * chip[0] + core, chip[1]), device_id_type=MESH
        )

    def greet_step(k, carry):
        for core in range(2):
            greet(column(along_rows(a, GRID - k)), core)
            greet(line(along_columns(b, GRID - k)), core)
        return carry

    @pl.when(jnp.logical_not(relay_stays))
    def _():
        greet((source_row, at), h)

    @pl.when(h == 1)
    def _():
        greet((b, at), 0)

    @pl.when(jnp.logical_and(h == 1, jnp.logical_not(stays)))
    def _():
        greet((b, at), 1)

    lax.fori_loop(1, GRID, greet_step, 0)
    greet((a, b), other)
    inputs = (
        (homolog_hbm, homolog),
        (factor_weight_hbm, factor_weight),
        (outer_weight_hbm, outer_weight),
        (out_in_weight_hbm, out_in_weight),
        (out_out_weight_hbm, out_out_weight),
        (in_in_weight_hbm, in_in_weight),
        (in_out_weight_hbm, in_out_weight),
    )
    copies = [
        pltpu.make_async_copy(src, dst, input_sem.at[number])
        for number, (src, dst) in enumerate(inputs)
    ]
    for copy in copies:
        copy.start()
    copies[0].wait()
    copies[1].wait()

    def normalize_step(n, carry):
        rows = pl.ds(pl.multiple_of(n * 256, 256), 256)
        normed, scale = layer_norm(homolog[rows, :].astype(F32))
        msa_scale[rows, :] = jnp.broadcast_to(scale, (256, WIDTH))
        normed_msa[0][rows, :] = normed[:, :WIDTH]
        normed_msa[1][rows, :] = normed[:, WIDTH:]
        return carry

    lax.fori_loop(0, 4, normalize_step, 0)
    repeat_factor(factor_weight, spread_factor)
    groups = []
    for g in range(4):
        pieces = [
            normed_msa[part][pl.ds(4 * g + q, 64, stride=BLOCK), :].astype(BF16)
            for q in range(4)
            for part in range(2)
        ]
        groups.append(jnp.concatenate(pieces, axis=1))
    factors = dot(jnp.concatenate(groups, axis=0), spread_factor[...]).astype(BF16)
    left_value = jnp.concatenate(
        [factors[g * 64 : (g + 1) * 64, :WIDTH] for g in range(4)], axis=1
    )
    right_value = jnp.concatenate(
        [factors[g * 64 : (g + 1) * 64, WIDTH:] for g in range(4)], axis=1
    )
    left_ic[...] = left_value
    right_jd[...] = right_value
    before = lax.broadcasted_iota(jnp.int32, (BLOCK * HIDDEN, BLOCK * HIDDEN), 0)
    after = lax.broadcasted_iota(jnp.int32, (BLOCK * HIDDEN, BLOCK * HIDDEN), 1)
    moved = (before == after % BLOCK * HIDDEN + after // BLOCK).astype(F32).astype(BF16)
    turned_factors = dot(jnp.concatenate([left_value, right_value], axis=0), moved).astype(BF16)
    left_ci[...] = turned_factors[:64]
    right_dj[...] = turned_factors[64:]

    for copy in copies[2:]:
        copy.wait()
    keeps_first = jnp.logical_and(h == 0, odd == 0)
    keeps_second = jnp.logical_and(h == 1, stays)
    pl.semaphore_wait(barrier, 31 - relay_stays.astype(jnp.int32) - keeps_second.astype(jnp.int32))

    for slot in range(4):
        src, dst = ((left_ci, relay_left), (right_dj, relay_right))[slot // 2]
        half = pl.ds(slot % 2 * 32, 32)

        @pl.when(jnp.logical_not(relay_stays))
        def _():
            remote(
                src.at[half],
                dst.at[half],
                relay_send_sem.at[slot],
                relay_sem.at[slot],
                relay_chip,
                h,
            ).start()

        @pl.when(relay_stays)
        def _():
            pltpu.make_async_copy(src.at[half], dst.at[half], relay_sem.at[slot]).start()

    def msa_send(src, dst, sems, slot, chip_of, core, send, half=None):
        whole = half is None
        source = src if whole else src.at[pl.ds(half * 32, 32)]
        target = dst.at[slot] if whole else dst.at[slot, pl.ds(half * 32, 32)]

        def step(k, carry):
            place = (GRID - 1 - k) * other + k * h

            @pl.when(jnp.logical_or(place > 0, h != core))
            def _():
                remote(source, target, send, sems.at[slot], chip_of(place), core).start()

            return carry

        lax.fori_loop(0, GRID, step, 0)

        @pl.when(h == core)
        def _():
            pltpu.make_async_copy(source, target, sems.at[slot]).start()

    def column_step(k):
        return column(along_rows(a, k))

    def line_step(k):
        return line(along_columns(b, k))

    def msa_sent(src, dst, core, send):
        @pl.when(h == core)
        def _():
            wait_for(dst.at[pl.ds(0, 7)], send)

        @pl.when(h != core)
        def _():
            wait_for(dst.at[pl.ds(0, 8)], send)

    msa_send(right_jd, msa_direct, msa_sem.at[1], row, column_step, 0, send_sem.at[2])
    msa_send(left_ic, msa_direct, msa_sem.at[1], row, column_step, 1, send_sem.at[3])

    for slot, (src, dst) in enumerate(((pair_input, pair_block), (cotangent, cot_block))):
        half = dst.at[pl.ds(h * 8, 8)]
        sem = block_sem.at[slot, h]

        @pl.when(keeps_first)
        def _():
            pltpu.make_async_copy(src, half, sem).start()

        @pl.when(jnp.logical_not(keeps_first))
        def _():
            remote(src, half, send_sem.at[4 + slot], sem, chip_at(a, b), 0).start()

        @pl.when(keeps_second)
        def _():
            pltpu.make_async_copy(src, half, sem).start()

        @pl.when(jnp.logical_not(keeps_second))
        def _():
            remote(src, half, send_sem.at[6 + slot], sem, chip_at(b, a), 1).start()

    def block_sent(slot, src):
        @pl.when(jnp.logical_not(keeps_first))
        def _():
            wait_for(src, send_sem.at[4 + slot])

        @pl.when(jnp.logical_not(keeps_second))
        def _():
            wait_for(src, send_sem.at[6 + slot])

    relay_slot = 2 * source_row + h
    for slot in range(4):
        half = slot % 2
        src = (relay_left, relay_right)[slot // 2]
        wait_for(src.at[pl.ds(half * 32, 32)], relay_sem.at[slot])
        kind = slot // 2
        msa_send(
            src, msa_relayed, msa_sem.at[0], relay_slot, line_step, kind, send_sem.at[8 + kind], half
        )

    wide_weight[...] = outer_weight[...].astype(F32)
    spread_weight[...] = jnp.zeros(spread_weight.shape, BF16)

    def weight_step(n, carry):
        start = pl.multiple_of(n * WIDTH, WIDTH)

        def lay_out(piece):
            for q in range(4):
                some = pl.ds(start + q * HIDDEN, HIDDEN)
                table_weight[some, :] = piece
                spread_weight[some, q * WIDTH : (q + 1) * WIDTH] = piece

        @pl.when(h == 0)
        def _():
            lay_out(outer_weight[pl.ds(pl.multiple_of(n * HIDDEN, HIDDEN), HIDDEN), :])

        @pl.when(h == 1)
        def _():
            lay_out(wide_weight[pl.ds(n, HIDDEN, stride=HIDDEN), :].astype(BF16))

        return carry

    lax.fori_loop(0, HIDDEN, weight_step, 0)

    def turn_step(n, carry):
        rows = pl.ds(pl.multiple_of(n * 2 * WIDTH, 2 * WIDTH), 2 * WIDTH)
        turned_weight[:, rows] = spread_weight[rows, :].T
        return carry

    lax.fori_loop(0, HIDDEN // 2, turn_step, 0)
    for weight, turned_one in (
        (out_in_weight, out_in_turned),
        (out_out_weight, out_out_turned),
        (in_in_weight, in_in_turned),
        (in_out_weight, in_out_turned),
    ):
        turned_one[...] = weight[...].T

    def outer_step(k, carry):
        n = (b // 2 + k) % 4

        def msa_wait(part, carry):
            slot = 4 * n + part
            wait_for(msa_relayed.at[slot], msa_sem.at[0, slot])
            wait_for(msa_direct.at[slot], msa_sem.at[1, slot])
            return carry

        lax.fori_loop(0, 4, msa_wait, 0)
        four = pl.ds(4 * n, 4)
        outer32[...] += dot(
            msa_relayed[four].reshape(256, BLOCK * HIDDEN),
            msa_direct[four].reshape(256, BLOCK * HIDDEN),
            ((0,), (0,)),
        )
        return carry

    outer32[...] = jnp.zeros(outer32.shape, F32)
    lax.fori_loop(0, 4, outer_step, 0)
    lane_part = lax.broadcasted_iota(jnp.int32, (BLOCK, WIDTH), 1) // HIDDEN

    def project_step(d8, total):
        columns = []
        for part in range(8):
            tile = outer32[pl.ds(pl.multiple_of((8 * d8 + part) * BLOCK, BLOCK), BLOCK), :]
            columns.append(
                jnp.concatenate(
                    [
                        jnp.where(lane_part == q, tile[:, g * WIDTH : (g + 1) * WIDTH], 0.0)
                        for q in range(4)
                        for g in range(4)
                    ],
                    axis=0,
                )
            )
        picked = jnp.concatenate(columns, axis=1).astype(BF16)
        weight = table_weight[pl.ds(pl.multiple_of(d8 * 8 * WIDTH, 8 * WIDTH), 8 * WIDTH), :]
        return total + dot(picked, weight)

    projected = lax.fori_loop(
        0, HIDDEN // 8, project_step, jnp.zeros((BLOCK * BLOCK, WIDTH), F32)
    )
    for part in range(2):
        wait_for(pair_block.at[pl.ds(part * 8, 8)], block_sem.at[0, part])
        wait_for(cot_block.at[pl.ds(part * 8, 8)], block_sem.at[1, part])
    for r in range(BLOCK):
        start = ((r % 4) * 4 + r // 4) * BLOCK
        flat[pl.ds(r * BLOCK, BLOCK), :] = projected[start : start + BLOCK] * (1.0 / SEQUENCES)

    def add_rows(i, value):
        first[pl.ds(i * BLOCK, BLOCK), :] = (
            (pair_block[i].astype(F32) + value).astype(BF16).astype(F32)
        )

    @pl.when(h == 0)
    def _():
        for i in range(BLOCK):
            add_rows(i, flat[pl.ds(i, BLOCK, stride=BLOCK), :])

    @pl.when(h == 1)
    def _():
        for i in range(BLOCK):
            add_rows(i, flat[pl.ds(i * BLOCK, BLOCK), :])

    def send_same(dst, sems, chips, steps, send):
        own = steps(0)

        def step(k):
            chip = chips(steps(GRID - k))
            remote(dst.at[own], dst.at[own], send, sems.at[own], chip, h).start()

        for k in range(1, GRID):
            step(k)

    def send_other(src, dst, sems, chips, steps, send):
        own = steps(0)

        def step(k):
            chip = chips(steps(GRID - 1 - k))
            remote(src, dst.at[own], send, sems.at[own], chip, other).start()

        for k in range(GRID):
            step(k)

    def block_product(totals, left, by_column, right):
        totals = list(totals)
        for t in range(BLOCK):
            across = right(t)
            for p in range(BLOCK):
                one = left[t, pl.ds(p, 1), :] if by_column else left[p, pl.ds(t, 1), :]
                totals[p] = totals[p] + one * across
        return tuple(totals)

    def no_totals():
        return tuple(jnp.zeros((BLOCK, WIDTH), F32) for _ in range(BLOCK))

    def contract(left, left_sem, left_own, by_column, right, right_sem, right_own, steps):
        def arrive(ref, sems, slot, skip):
            if skip is None:
                wait_for(ref.at[slot], sems.at[slot])
            else:

                @pl.when(slot != skip)
                def _():
                    wait_for(ref.at[slot], sems.at[slot])

        def block_step(k, totals):
            slot = steps(k)
            arrive(left, left_sem, slot, left_own)
            arrive(right, right_sem, slot, right_own)
            wide[...] = left[slot].astype(F32)
            return block_product(totals, wide, by_column, lambda t: right[slot, t].astype(F32))

        totals = lax.fori_loop(0, GRID, block_step, no_totals())
        return jnp.concatenate(totals, axis=0)

    def partial(part, n, totals):
        for p in range(BLOCK):
            part[n, p] = totals[p].astype(BF16)

    def sum_of(parts, sems, skip, steps):
        def step(k, total):
            slot = steps(k)
            if skip is None:
                wait_for(parts.at[slot], sems.at[slot])
            else:

                @pl.when(slot != skip)
                def _():
                    wait_for(parts.at[slot], sems.at[slot])

            return total + parts[slot].reshape(BLOCK * BLOCK, WIDTH).astype(F32)

        return lax.fori_loop(0, GRID, step, jnp.zeros((BLOCK * BLOCK, WIDTH), F32))

    def send_part(part, n, dst, slot, sems, chips, core, send):
        remote(part.at[n], dst.at[slot], send, sems.at[slot], chips(n), core).start()

    def turned(value, store):
        flat[...] = value
        for j in range(BLOCK):
            store(j, flat[pl.ds(j, BLOCK, stride=BLOCK), :].astype(BF16))

    def turn_cot(value):
        rounded = value.astype(BF16).astype(F32)
        cot_wide[...] = rounded.reshape(BLOCK, BLOCK, WIDTH)
        flat[...] = rounded
        for j in range(BLOCK):
            cot_turned[j] = flat[pl.ds(j, BLOCK, stride=BLOCK), :]

    def blocked(value):
        return value.astype(BF16).reshape(BLOCK, BLOCK, WIDTH)

    def gated(normed, weight, at):
        projected = dot(normed, weight[:, at * WIDTH : (at + 2) * WIDTH])
        gate, value = jax.nn.sigmoid(projected[:, :WIDTH]), projected[:, WIDTH:]
        return gate, value

    def keep_gated(ref, first_at, gate, value):
        ref[first_at] = value * gate * (1.0 - gate)
        ref[first_at + 1] = gate

    def keep_norm(ref, first_at, normed, scale):
        ref[first_at] = normed
        ref[first_at + 1] = jnp.broadcast_to(scale, normed.shape)

    normed, scale = layer_norm(first[...])
    rounded = normed.astype(BF16)
    left_gate, left_value = gated(rounded, out_in_weight, 0)
    o_left[own_j] = blocked(left_gate * left_value)
    send_same(o_left, pair_sem.at[0], row_chip, step_j, send_sem.at[10])
    right_gate, right_value = gated(rounded, out_in_weight, 2)

    def store_right(j, value):
        o_right_stage[j] = value

    turned(right_gate * right_value, store_right)
    send_other(o_right_stage, o_right, pair_sem.at[1], row_chip, step_j, send_sem.at[11])
    keep_gated(out_kept, 0, left_gate, left_value)
    keep_gated(out_kept, 2, right_gate, right_value)
    keep_norm(out_kept, 4, normed, scale)
    out_kept[6] = jax.nn.sigmoid(dot(rounded, out_in_weight[:, 4 * WIDTH :]))
    mixing = contract(
        o_left,
        pair_sem.at[0],
        own_j,
        False,
        o_right,
        pair_sem.at[1],
        None,
        step_j,
    )
    mixing_normed, mixing_scale = layer_norm(mixing)
    update = dot(mixing_normed.astype(BF16), out_out_weight[...])
    second = (first[...] + out_kept[6] * update).astype(BF16).astype(F32)

    normed, scale = layer_norm(second)
    rounded = normed.astype(BF16)
    right_gate, right_value = gated(rounded, in_in_weight, 2)
    i_right[own_i] = blocked(right_gate * right_value)
    send_same(i_right, pair_sem.at[4], col_chip, step_i, send_sem.at[14])
    left_gate, left_value = gated(rounded, in_in_weight, 0)
    i_left_stage[...] = blocked(left_gate * left_value)
    send_other(i_left_stage, i_left, pair_sem.at[5], col_chip, step_i, send_sem.at[15])
    keep_norm(out_kept, 7, mixing_normed, mixing_scale)
    out_kept[9] = update
    keep_gated(in_kept, 0, left_gate, left_value)
    keep_gated(in_kept, 2, right_gate, right_value)
    keep_norm(in_kept, 4, normed, scale)
    gating = jax.nn.sigmoid(dot(rounded, in_in_weight[:, 4 * WIDTH :]))
    in_kept[6] = gating
    in_kept[7] = second
    upstream = cot_block[...].reshape(BLOCK * BLOCK, WIDTH).astype(F32)
    upstream32[...] = upstream
    in_kept[8] = dot((upstream * gating).astype(BF16), in_out_turned[...])
    mixing = contract(
        i_left,
        pair_sem.at[5],
        None,
        True,
        i_right,
        pair_sem.at[4],
        own_i,
        step_i,
    )

    def input_pullback(kept, left_cot, right_cot, gating_part, weight, upstream):
        pieces = [
            (left_cot * kept[0]).astype(BF16),
            (left_cot * kept[1]).astype(BF16),
            (right_cot * kept[2]).astype(BF16),
            (right_cot * kept[3]).astype(BF16),
        ]
        normed_cot = gating_part + dot(
            jnp.concatenate(pieces, axis=1), weight[: 4 * WIDTH, :]
        )
        return upstream + layer_norm_pullback(kept[4], kept[5], normed_cot)

    normed, scale = layer_norm(mixing)
    turn_cot(layer_norm_pullback(normed, scale, in_kept[8]))

    def incoming_step(k, carry):
        n = step_i(GRID - 1 - k)
        wide[...] = i_right[n].astype(F32)
        totals = block_product(no_totals(), wide, False, lambda t: cot_turned[t])
        partial(left_parts, n, totals)
        send_part(
            left_parts, n, ib_left, own_j, pair_sem.at[2], row_chip, other, send_sem.at[12]
        )
        wide[...] = i_left[n].astype(F32)
        totals = block_product(no_totals(), wide, False, lambda t: cot_wide[t])

        @pl.when(n != own_i)
        def _():
            partial(right_parts, n, totals)
            send_part(
                right_parts, n, ib_right, own_i, pair_sem.at[3], col_chip, h, send_sem.at[13]
            )

        @pl.when(n == own_i)
        def _():
            partial(ib_right, n, totals)

        return carry

    lax.fori_loop(0, GRID, incoming_step, 0)
    gating = in_kept[6]
    update = dot(normed.astype(BF16), in_out_weight[...])
    result = (in_kept[7] + gating * update).astype(BF16)
    gating_cot = upstream32[...] * update * gating * (1.0 - gating)
    gating_part = dot(gating_cot.astype(BF16), in_in_turned[4 * WIDTH :, :])

    def hand_over(value, stage, got, sem, send):
        stage[...] = value.reshape(2, 8, BLOCK, WIDTH)
        for part in range(2):
            order = remote(stage.at[part], got, send.at[part], sem, (at, b), part)
            if part == 0:
                pl.when(odd == 1)(order.start)
            else:
                order.start()

    @pl.when(h == 0)
    def _():
        hand_over(result, output_stage, output_got, small_sem.at[0], output_sem)

    left_cot = sum_of(ib_left, pair_sem.at[2], None, step_j)
    right_cot = sum_of(ib_right, pair_sem.at[3], own_i, step_i)
    second_cot = input_pullback(
        in_kept, left_cot, right_cot, gating_part, in_in_turned, upstream32[...]
    )

    normed_cot = dot((second_cot * out_kept[6]).astype(BF16), out_out_turned[...])
    turn_cot(layer_norm_pullback(out_kept[7], out_kept[8], normed_cot))

    def outgoing_step(k, carry):
        n = step_j(GRID - 1 - k)
        wide[...] = o_right[n].astype(F32)
        totals = block_product(no_totals(), wide, False, lambda t: cot_turned[t])

        @pl.when(n != own_j)
        def _():
            partial(left_parts2, n, totals)
            send_part(
                left_parts2, n, ob_left, own_j, pair_sem.at[6], row_chip, h, send_sem.at[16]
            )

        @pl.when(n == own_j)
        def _():
            partial(ob_left, n, totals)

        totals = block_product(
            no_totals(), cot_wide, True, lambda t: o_left[n, t].astype(F32)
        )
        partial(right_parts2, n, totals)
        send_part(
            right_parts2, n, ob_right, own_i, pair_sem.at[7], col_chip, other, send_sem.at[17]
        )
        return carry

    lax.fori_loop(0, GRID, outgoing_step, 0)
    gating = out_kept[6]
    gating_cot = second_cot * out_kept[9] * gating * (1.0 - gating)
    gating_part = dot(gating_cot.astype(BF16), out_in_turned[4 * WIDTH :, :])
    flat[...] = sum_of(ob_left, pair_sem.at[6], own_j, step_j)
    left_cot = jnp.concatenate(
        [flat[pl.ds(j, BLOCK, stride=BLOCK), :] for j in range(BLOCK)], axis=0
    )
    right_cot = sum_of(ob_right, pair_sem.at[7], None, step_i)
    gradient = input_pullback(
        out_kept, left_cot, right_cot, gating_part, out_in_turned, second_cot
    )

    @pl.when(h == 0)
    def _():
        hand_over(gradient, gradient_stage, gradient_got, small_sem.at[1], gradient_sem)

    def stack(r, value):
        g, q = r // 4, r % 4
        stacked[g * BLOCK : (g + 1) * BLOCK, q * WIDTH : (q + 1) * WIDTH] = value.astype(BF16)

    flat[...] = gradient

    @pl.when(h == 0)
    def _():
        for r in range(BLOCK):
            stack(r, flat[pl.ds(r, BLOCK, stride=BLOCK), :])

    @pl.when(h == 1)
    def _():
        for r in range(BLOCK):
            stack(r, flat[pl.ds(r * BLOCK, BLOCK), :])

    for x8 in range(HIDDEN // 8):
        chunk = dot(
            stacked[...], turned_weight[:, x8 * 8 * WIDTH : (x8 + 1) * 8 * WIDTH]
        ).astype(BF16)
        for piece in range(8):
            start = (8 * x8 + piece) * BLOCK
            for g in range(4):
                grad_table[start : start + BLOCK, g * WIDTH : (g + 1) * WIDTH] = chunk[
                    g * BLOCK : (g + 1) * BLOCK, piece * WIDTH : (piece + 1) * WIDTH
                ]

    def cot_step(step, carry):
        chips = [along_rows(a, GRID - 1 - 2 * step - n) for n in range(2)]
        sequences = jnp.concatenate(
            [
                msa_relayed[pl.ds(2 * chip, 2)].reshape(2 * 64, BLOCK * HIDDEN)
                for chip in chips
            ],
            axis=0,
        )
        sums = dot(sequences, grad_table[...]).astype(BF16)
        for n, chip in enumerate(chips):
            for core in range(2):
                start = (2 * n + core) * 64
                slot = 2 * chip + core
                cot_parts[slot] = sums[start : start + 64]
                target = cot_got.at[h, a]

                @pl.when(slot == row)
                def _():
                    pltpu.make_async_copy(cot_parts.at[slot], target, cot_sem.at[h, a]).start()

                @pl.when(slot != row)
                def _():
                    remote(
                        cot_parts.at[slot], target, send_sem.at[26], cot_sem.at[h, a], (chip, b), core
                    ).start()

        return carry

    lax.fori_loop(0, 4, cot_step, 0)
    for core in range(2):

        def cot_sum(k, total, core=core):
            n = along_rows(a, k)
            wait_for(cot_got.at[core, n], cot_sem.at[core, n])
            return total + cot_got[core, n].astype(F32)

        total = lax.fori_loop(0, GRID, cot_sum, jnp.zeros((64, BLOCK * HIDDEN), F32))
        msa_cots[1 - core] = (total * (1.0 / SEQUENCES)).astype(BF16)

    cots = jnp.concatenate(
        [
            jnp.concatenate(
                [msa_cots[kind, :, g * WIDTH : (g + 1) * WIDTH] for kind in range(2)], axis=1
            )
            for g in range(4)
        ],
        axis=0,
    )
    for q in range(4):
        normed_cots = dot(
            cots, spread_factor[q * 2 * WIDTH : (q + 1) * 2 * WIDTH, :], ((1,), (1,))
        )
        for g in range(4):
            rows = pl.ds(4 * g + q, 64, stride=BLOCK)
            value = layer_norm_pullback(
                jnp.concatenate([normed_msa[0][rows, :], normed_msa[1][rows, :]], axis=1),
                msa_scale[rows, :1],
                normed_cots[g * 64 : (g + 1) * 64],
            )
            alignment_first[rows, :] = value[:, :WIDTH]
            alignment_second[rows, :] = value[:, WIDTH:]
    @pl.when(keeps_first)
    def _():
        pair_output[...] = output_stage[0]
        pair_gradient[...] = gradient_stage[0]

    @pl.when(jnp.logical_not(keeps_first))
    def _():
        wait_for(output_got, small_sem.at[0])
        pair_output[...] = output_got[...]
        wait_for(gradient_got, small_sem.at[1])
        pair_gradient[...] = gradient_got[...]

    @pl.when(jnp.logical_not(relay_stays))
    def _():
        for slot in range(4):
            wait_for(relay_left.at[pl.ds(0, 32)], relay_send_sem.at[slot])

    msa_sent(right_jd, msa_direct, 0, send_sem.at[2])
    msa_sent(left_ic, msa_direct, 1, send_sem.at[3])
    block_sent(0, pair_input)
    block_sent(1, cotangent)
    msa_sent(relay_left, msa_relayed, 0, send_sem.at[8])
    msa_sent(relay_right, msa_relayed, 1, send_sem.at[9])
    for number in (10, 13, 14, 16):
        wait_for(o_left.at[pl.ds(0, 7)], send_sem.at[number])
    for number in (11, 12, 15, 17):
        wait_for(o_left, send_sem.at[number])
    wait_for(cot_parts.at[pl.ds(0, 15)], send_sem.at[26])

    @pl.when(h == 0)
    def _():
        wait_for(output_got, output_sem.at[1])
        wait_for(gradient_got, gradient_sem.at[1])

        @pl.when(odd == 1)
        def _():
            wait_for(output_got, output_sem.at[0])
            wait_for(gradient_got, gradient_sem.at[0])


def pair_updates(homolog, factor_weight, pair_input, cotangent, weights):
    gathered = pltpu.VMEM((GRID, BLOCK, BLOCK, WIDTH), BF16)
    block = pltpu.VMEM((BLOCK, BLOCK, WIDTH), BF16)
    flat = pltpu.VMEM((BLOCK * BLOCK, WIDTH), F32)
    shares = pltpu.VMEM((64, BLOCK * HIDDEN), BF16)
    all_sequences = pltpu.VMEM((2 * GRID, 64, BLOCK * HIDDEN), BF16)
    half_block = pltpu.VMEM((8, BLOCK, WIDTH), BF16)
    wide_block = pltpu.VMEM((BLOCK, BLOCK, WIDTH), F32)
    half_wide = pltpu.VMEM((8, BLOCK, WIDTH), F32)
    whole_side = pltpu.VMEM((64 * BLOCK, WIDTH), F32)
    dma = pltpu.SemaphoreType.DMA
    vmem = pl.BlockSpec(memory_space=pltpu.VMEM)
    return pl.pallas_call(
        pair_kernel,
        out_shape=(half_block, half_wide, whole_side, whole_side),
        in_specs=[pl.BlockSpec(memory_space=pl.ANY)] * 9,
        out_specs=(vmem,) * 4,
        scratch_shapes=[
            pltpu.VMEM((64 * BLOCK, 2 * WIDTH), BF16),
            pltpu.VMEM((2 * HIDDEN, 2 * WIDTH), BF16),
            pltpu.VMEM((HIDDEN * HIDDEN, WIDTH), BF16),
            pltpu.VMEM((WIDTH, 5 * WIDTH), BF16),
            pltpu.VMEM((WIDTH, WIDTH), BF16),
            pltpu.VMEM((WIDTH, 5 * WIDTH), BF16),
            pltpu.VMEM((WIDTH, WIDTH), BF16),
            [pltpu.VMEM((64 * BLOCK, WIDTH), F32)] * 2,
            pltpu.VMEM((64 * BLOCK, WIDTH), F32),
            pltpu.VMEM((8 * WIDTH, 2 * WIDTH), BF16),
            shares,
            shares,
            shares,
            shares,
            block,
            block,
            shares,
            shares,
            all_sequences,
            all_sequences,
            gathered,
            gathered,
            block,
            gathered,
            gathered,
            block,
            gathered,
            gathered,
            gathered,
            gathered,
            gathered,
            gathered,
            gathered,
            gathered,
            pltpu.VMEM((HIDDEN * HIDDEN, WIDTH), F32),
            pltpu.VMEM((HIDDEN * WIDTH, WIDTH), BF16),
            pltpu.VMEM((HIDDEN * WIDTH, 4 * WIDTH), BF16),
            pltpu.VMEM((4 * WIDTH, HIDDEN * WIDTH), BF16),
            pltpu.VMEM((5 * WIDTH, WIDTH), BF16),
            pltpu.VMEM((WIDTH, WIDTH), BF16),
            pltpu.VMEM((5 * WIDTH, WIDTH), BF16),
            pltpu.VMEM((WIDTH, WIDTH), BF16),
            pltpu.VMEM((BLOCK * HIDDEN, BLOCK * HIDDEN), F32),
            wide_block,
            wide_block,
            wide_block,
            flat,
            pltpu.VMEM((10, BLOCK * BLOCK, WIDTH), F32),
            pltpu.VMEM((9, BLOCK * BLOCK, WIDTH), F32),
            flat,
            flat,
            pltpu.VMEM((64, 4 * WIDTH), BF16),
            pltpu.VMEM((BLOCK * HIDDEN, BLOCK * HIDDEN), BF16),
            pltpu.VMEM((2, 64, BLOCK * HIDDEN), BF16),
            all_sequences,
            pltpu.VMEM((2, GRID, 64, BLOCK * HIDDEN), BF16),
            pltpu.VMEM((2, 8, BLOCK, WIDTH), BF16),
            half_block,
            pltpu.VMEM((2, 8, BLOCK, WIDTH), F32),
            half_wide,
            dma((4,)),
            dma((4,)),
            dma((2, 2)),
            dma((2, 2 * GRID)),
            dma((8, GRID)),
            dma((2, GRID)),
            dma((2,)),
            dma((28,)),
            dma((2,)),
            dma((2,)),
            dma((7,)),
        ],
        compiler_params=pltpu.CompilerParams(
            collective_id=1, has_side_effects=True, vmem_limit_bytes=60 << 20
        ),
        name="pair_updates",
    )(homolog, factor_weight, pair_input, cotangent, *weights)


def hand_out_kernel(
    pair_output,
    pair_gradient,
    alignment_first,
    alignment_second,
    pair_output_out,
    pair_gradient_out,
    alignment_gradient,
    copy_sem,
):
    rows = alignment_first.shape[0] // 4
    pairs = [(pair_output, pair_output_out), (pair_gradient, pair_gradient_out)]
    for part in range(4):
        some = pl.ds(part * rows, rows)
        for side, held in enumerate((alignment_first, alignment_second)):
            target = alignment_gradient.at[some, pl.ds(side * WIDTH, WIDTH)]
            pairs.append((held.at[some], target))
    copies = [
        pltpu.make_async_copy(src, dst, copy_sem.at[number])
        for number, (src, dst) in enumerate(pairs)
    ]
    for copy in copies:
        copy.start()
    for copy in copies:
        copy.wait()


def body(
    homolog_features,
    pair_input,
    cotangent,
    homolog_factor_matrix,
    outer_output_weight,
    outgoing_input_weight,
    outgoing_output_weight,
    incoming_input_weight,
    incoming_output_weight,
):
    sequences, residues, depth = homolog_features.shape
    homolog = homolog_features.reshape(sequences * residues, depth)
    factor_weight = homolog_factor_matrix.T
    results = pair_updates(
        homolog,
        factor_weight,
        pair_input,
        cotangent,
        (
            outer_output_weight,
            outgoing_input_weight,
            outgoing_output_weight,
            incoming_input_weight,
            incoming_output_weight,
        ),
    )
    anywhere = pl.BlockSpec(memory_space=pl.ANY)
    pair_output, pair_gradient, alignment_gradient = pl.pallas_call(
        hand_out_kernel,
        out_shape=(
            jax.ShapeDtypeStruct(pair_input.shape, BF16),
            jax.ShapeDtypeStruct(pair_input.shape, F32),
            jax.ShapeDtypeStruct(homolog.shape, F32),
        ),
        in_specs=[pl.BlockSpec(memory_space=pltpu.VMEM)] * 4,
        out_specs=(anywhere,) * 3,
        scratch_shapes=[pltpu.SemaphoreType.DMA((10,))],
        compiler_params=pltpu.CompilerParams(vmem_limit_bytes=16 << 20),
        name="hand_out",
    )(*results)
    return pair_output, pair_gradient, alignment_gradient.reshape(sequences, residues, depth)


def solution(mesh):
    split = P("row", "col", None)
    return jax.shard_map(
        body,
        mesh=mesh,
        in_specs=(split, split, split, P(), P(), P(), P(), P(), P()),
        out_specs=(split, split, split),
        check_vma=False,
    )
```

```python
import jax
import jax.numpy as jnp
from jax import lax
from jax.experimental import pallas as pl
from jax.experimental.pallas import tpu as pltpu
from jax.sharding import PartitionSpec as P

SEQUENCES = 1024
EPSILON = 1e-05
MESH = pl.DeviceIdType.MESH
F32 = jnp.float32
BF16 = jnp.bfloat16
GRID = 8
BLOCK = 16
WIDTH = 128
HIDDEN = 32


def dot(lhs, rhs, dims=((1,), (0,))):
    return lax.dot_general(lhs, rhs, (dims, ((), ())), preferred_element_type=F32)


def layer_norm(inputs):
    centered = inputs - jnp.mean(inputs, axis=-1, keepdims=True)
    spread = jnp.mean(centered * centered, axis=-1, keepdims=True)
    scale = lax.rsqrt(spread + EPSILON)
    return centered * scale, scale


def layer_norm_pullback(normed, scale, upstream):
    along = jnp.mean(upstream * normed, axis=-1, keepdims=True)
    return scale * (upstream - jnp.mean(upstream, axis=-1, keepdims=True) - normed * along)


def repeat_factor(factor_weight, spread_factor):
    hidden_row = lax.broadcasted_iota(jnp.int32, (2 * HIDDEN, 2 * WIDTH), 0)
    hidden_lane = lax.broadcasted_iota(jnp.int32, (2 * HIDDEN, 2 * WIDTH), 1)
    repeats = (hidden_lane % HIDDEN + HIDDEN * (hidden_lane // WIDTH) == hidden_row).astype(F32)
    repeated = dot(factor_weight[...], repeats.astype(BF16), ((0,), (0,)))
    lane_quarter = lax.broadcasted_iota(jnp.int32, (2 * WIDTH, 2 * WIDTH), 1) % WIDTH // HIDDEN
    for q in range(4):
        spread_factor[q * 2 * WIDTH : (q + 1) * 2 * WIDTH, :] = jnp.where(
            lane_quarter == q, repeated, 0.0
        ).astype(BF16)


def pair_kernel(
    homolog_hbm,
    factor_weight_hbm,
    pair_input,
    cotangent,
    outer_weight_hbm,
    out_in_weight_hbm,
    out_out_weight_hbm,
    in_in_weight_hbm,
    in_out_weight_hbm,
    pair_output,
    pair_gradient,
    alignment_first,
    alignment_second,
    homolog,
    factor_weight,
    outer_weight,
    out_in_weight,
    out_out_weight,
    in_in_weight,
    in_out_weight,
    normed_msa,
    msa_scale,
    spread_factor,
    left_ic,
    left_ci,
    right_dj,
    right_jd,
    pair_block,
    cot_block,
    relay_left,
    relay_right,
    msa_relayed,
    msa_direct,
    o_left,
    o_right,
    o_right_stage,
    i_left,
    i_right,
    i_left_stage,
    ib_right,
    ib_left,
    ob_right,
    ob_left,
    left_parts,
    right_parts,
    left_parts2,
    right_parts2,
    wide_weight,
    table_weight,
    spread_weight,
    turned_weight,
    out_in_turned,
    out_out_turned,
    in_in_turned,
    in_out_turned,
    outer32,
    wide,
    wide_too,
    cot_wide,
    cot_turned,
    flat,
    out_kept,
    in_kept,
    first,
    upstream32,
    stacked,
    grad_table,
    msa_cots,
    cot_parts,
    cot_got,
    output_stage,
    output_got,
    gradient_stage,
    gradient_got,
    relay_sem,
    relay_send_sem,
    block_sem,
    msa_sem,
    pair_sem,
    cot_sem,
    small_sem,
    send_sem,
    output_sem,
    gradient_sem,
    input_sem,
):
    row, col = lax.axis_index("row"), lax.axis_index("col")
    a, h, b = row // 2, row % 2, col
    other = 1 - h
    odd = b % 2
    at = (a + 4 * odd) % GRID
    own_i = at * other + b * h
    own_j = b * other + at * h
    stays = jnp.logical_and(a == b, odd == 0)

    def chip_at(i, j):
        return (i + 4 * (j % 2)) % GRID, j

    def row_chip(n):
        return chip_at(at * other + n * h, n * other + b * h)

    def col_chip(n):
        return chip_at(n * other + at * h, b * other + n * h)

    def apart(k):
        m = k // 2
        return m + (m // 2) * (5 - 2 * m), k % 2

    def along_rows(own, k):
        dm, dv = apart(k)
        return (own // 4 + dv) % 2 * 4 + (own % 4 + dm) % 4

    def along_columns(own, k):
        dm, dv = apart(k)
        return (own // 2 + dm) % 4 * 2 + (own % 2 + dv) % 2

    def step_i(k):
        return along_rows(at, k) * other + along_columns(b, k) * h

    def step_j(k):
        return along_columns(b, k) * other + along_rows(at, k) * h

    relay_column = (a % 4 + b // 2 + 2 * (b % 4)) % 4 * 2 + a // 4
    relay_chip = chip_at(b, relay_column)
    source_row = b % 2 * 4 + (b // 2 + 16 - at // 2 - 2 * (at % 4)) % 4
    relay_stays = jnp.logical_and(relay_column == b, relay_chip[0] == a)

    def column(n):
        return n, b

    def line(n):
        return chip_at(at, n)

    def remote(src, dst, send, recv, chip, core):
        return pltpu.make_async_remote_copy(
            src_ref=src,
            dst_ref=dst,
            send_sem=send,
            recv_sem=recv,
            device_id=(2 * chip[0] + core, chip[1]),
            device_id_type=MESH,
        )

    def wait_for(ref, sem):
        pltpu.make_async_copy(ref, ref, sem).wait()

    inputs = (
        (homolog_hbm, homolog),
        (factor_weight_hbm, factor_weight),
        (outer_weight_hbm, outer_weight),
        (out_in_weight_hbm, out_in_weight),
        (out_out_weight_hbm, out_out_weight),
        (in_in_weight_hbm, in_in_weight),
        (in_out_weight_hbm, in_out_weight),
    )
    copies = [
        pltpu.make_async_copy(src, dst, input_sem.at[number])
        for number, (src, dst) in enumerate(inputs)
    ]
    for copy in copies:
        copy.start()

    barrier = pltpu.get_barrier_semaphore()

    def greet(chip, core):
        pl.semaphore_signal(
            barrier, inc=1, device_id=(2 * chip[0] + core, chip[1]), device_id_type=MESH
        )

    def greet_step(k, carry):
        for core in range(2):
            greet(column(along_rows(a, GRID - k)), core)
            greet(line(along_columns(b, GRID - k)), core)
        return carry

    @pl.when(jnp.logical_not(relay_stays))
    def _():
        greet((source_row, at), h)

    @pl.when(h == 1)
    def _():
        greet((b, at), 0)

    @pl.when(jnp.logical_and(h == 1, jnp.logical_not(stays)))
    def _():
        greet((b, at), 1)

    lax.fori_loop(1, GRID, greet_step, 0)
    greet((a, b), other)
    copies[0].wait()
    copies[1].wait()

    def normalize_step(n, carry):
        rows = pl.ds(pl.multiple_of(n * 256, 256), 256)
        normed, scale = layer_norm(homolog[rows, :].astype(F32))
        msa_scale[rows, :] = jnp.broadcast_to(scale, (256, WIDTH))
        normed_msa[0][rows, :] = normed[:, :WIDTH]
        normed_msa[1][rows, :] = normed[:, WIDTH:]
        return carry

    lax.fori_loop(0, 4, normalize_step, 0)
    repeat_factor(factor_weight, spread_factor)
    groups = []
    for g in range(4):
        pieces = [
            normed_msa[part][pl.ds(4 * g + q, 64, stride=BLOCK), :].astype(BF16)
            for q in range(4)
            for part in range(2)
        ]
        groups.append(jnp.concatenate(pieces, axis=1))
    factors = dot(jnp.concatenate(groups, axis=0), spread_factor[...]).astype(BF16)
    left_value = jnp.concatenate(
        [factors[g * 64 : (g + 1) * 64, :WIDTH] for g in range(4)], axis=1
    )
    right_value = jnp.concatenate(
        [factors[g * 64 : (g + 1) * 64, WIDTH:] for g in range(4)], axis=1
    )
    left_ic[...] = left_value
    right_jd[...] = right_value
    before = lax.broadcasted_iota(jnp.int32, (BLOCK * HIDDEN, BLOCK * HIDDEN), 0)
    after = lax.broadcasted_iota(jnp.int32, (BLOCK * HIDDEN, BLOCK * HIDDEN), 1)
    moved = (before == after % BLOCK * HIDDEN + after // BLOCK).astype(F32).astype(BF16)
    turned_factors = dot(jnp.concatenate([left_value, right_value], axis=0), moved).astype(BF16)
    left_ci[...] = turned_factors[:64]
    right_dj[...] = turned_factors[64:]

    for copy in copies[2:]:
        copy.wait()
    keeps_first = jnp.logical_and(h == 0, odd == 0)
    keeps_second = jnp.logical_and(h == 1, stays)
    pl.semaphore_wait(barrier, 31 - relay_stays.astype(jnp.int32) - keeps_second.astype(jnp.int32))

    for slot in range(4):
        src, dst = ((left_ci, relay_left), (right_dj, relay_right))[slot // 2]
        half = pl.ds(slot % 2 * 32, 32)

        @pl.when(jnp.logical_not(relay_stays))
        def _():
            remote(
                src.at[half],
                dst.at[half],
                relay_send_sem.at[slot],
                relay_sem.at[slot],
                relay_chip,
                h,
            ).start()

        @pl.when(relay_stays)
        def _():
            pltpu.make_async_copy(src.at[half], dst.at[half], relay_sem.at[slot]).start()

    def msa_send(src, dst, sems, slot, chip_of, core, send, half=None):
        whole = half is None
        source = src if whole else src.at[pl.ds(half * 32, 32)]
        target = dst.at[slot] if whole else dst.at[slot, pl.ds(half * 32, 32)]

        def step(k, carry):
            place = (GRID - 1 - k) * other + k * h

            @pl.when(jnp.logical_or(place > 0, h != core))
            def _():
                remote(source, target, send, sems.at[slot], chip_of(place), core).start()

            return carry

        lax.fori_loop(0, GRID, step, 0)

        @pl.when(h == core)
        def _():
            pltpu.make_async_copy(source, target, sems.at[slot]).start()

    def column_step(k):
        return column(along_rows(a, k))

    def line_step(k):
        return line(along_columns(b, k))

    def msa_sent(src, dst, core, send):
        @pl.when(h == core)
        def _():
            wait_for(dst.at[pl.ds(0, 7)], send)

        @pl.when(h != core)
        def _():
            wait_for(dst.at[pl.ds(0, 8)], send)

    msa_send(right_jd, msa_direct, msa_sem.at[1], row, column_step, 0, send_sem.at[2])
    msa_send(left_ic, msa_direct, msa_sem.at[1], row, column_step, 1, send_sem.at[3])

    for slot, (src, dst) in enumerate(((pair_input, pair_block), (cotangent, cot_block))):
        half = dst.at[pl.ds(h * 8, 8)]
        sem = block_sem.at[slot, h]

        @pl.when(keeps_first)
        def _():
            pltpu.make_async_copy(src, half, sem).start()

        @pl.when(jnp.logical_not(keeps_first))
        def _():
            remote(src, half, send_sem.at[4 + slot], sem, chip_at(a, b), 0).start()

        @pl.when(keeps_second)
        def _():
            pltpu.make_async_copy(src, half, sem).start()

        @pl.when(jnp.logical_not(keeps_second))
        def _():
            remote(src, half, send_sem.at[6 + slot], sem, chip_at(b, a), 1).start()

    def block_sent(slot, src):
        @pl.when(jnp.logical_not(keeps_first))
        def _():
            wait_for(src, send_sem.at[4 + slot])

        @pl.when(jnp.logical_not(keeps_second))
        def _():
            wait_for(src, send_sem.at[6 + slot])

    relay_slot = 2 * source_row + h
    for slot in range(4):
        half = slot % 2
        src = (relay_left, relay_right)[slot // 2]
        wait_for(src.at[pl.ds(half * 32, 32)], relay_sem.at[slot])
        kind = slot // 2
        msa_send(
            src, msa_relayed, msa_sem.at[0], relay_slot, line_step, kind, send_sem.at[8 + kind], half
        )

    wide_weight[...] = outer_weight[...].astype(F32)
    spread_weight[...] = jnp.zeros(spread_weight.shape, BF16)

    def weight_step(n, carry):
        start = pl.multiple_of(n * WIDTH, WIDTH)

        def lay_out(piece):
            for q in range(4):
                some = pl.ds(start + q * HIDDEN, HIDDEN)
                table_weight[some, :] = piece
                spread_weight[some, q * WIDTH : (q + 1) * WIDTH] = piece

        @pl.when(h == 0)
        def _():
            lay_out(outer_weight[pl.ds(pl.multiple_of(n * HIDDEN, HIDDEN), HIDDEN), :])

        @pl.when(h == 1)
        def _():
            lay_out(wide_weight[pl.ds(n, HIDDEN, stride=HIDDEN), :].astype(BF16))

        return carry

    lax.fori_loop(0, HIDDEN, weight_step, 0)

    def turn_step(n, carry):
        rows = pl.ds(pl.multiple_of(n * 2 * WIDTH, 2 * WIDTH), 2 * WIDTH)
        turned_weight[:, rows] = spread_weight[rows, :].T
        return carry

    lax.fori_loop(0, HIDDEN // 2, turn_step, 0)
    for weight, turned_one in (
        (out_in_weight, out_in_turned),
        (out_out_weight, out_out_turned),
        (in_in_weight, in_in_turned),
        (in_out_weight, in_out_turned),
    ):
        turned_one[...] = weight[...].T

    def outer_step(k, carry):
        n = (b // 2 + k) % 4

        def msa_wait(part, carry):
            slot = 4 * n + part
            wait_for(msa_relayed.at[slot], msa_sem.at[0, slot])
            wait_for(msa_direct.at[slot], msa_sem.at[1, slot])
            return carry

        lax.fori_loop(0, 4, msa_wait, 0)
        four = pl.ds(4 * n, 4)
        outer32[...] += dot(
            msa_relayed[four].reshape(256, BLOCK * HIDDEN),
            msa_direct[four].reshape(256, BLOCK * HIDDEN),
            ((0,), (0,)),
        )
        return carry

    outer32[...] = jnp.zeros(outer32.shape, F32)
    lax.fori_loop(0, 4, outer_step, 0)
    lane_part = lax.broadcasted_iota(jnp.int32, (BLOCK, WIDTH), 1) // HIDDEN

    def project_step(d8, total):
        columns = []
        for part in range(8):
            tile = outer32[pl.ds(pl.multiple_of((8 * d8 + part) * BLOCK, BLOCK), BLOCK), :]
            columns.append(
                jnp.concatenate(
                    [
                        jnp.where(lane_part == q, tile[:, g * WIDTH : (g + 1) * WIDTH], 0.0)
                        for q in range(4)
                        for g in range(4)
                    ],
                    axis=0,
                )
            )
        picked = jnp.concatenate(columns, axis=1).astype(BF16)
        weight = table_weight[pl.ds(pl.multiple_of(d8 * 8 * WIDTH, 8 * WIDTH), 8 * WIDTH), :]
        return total + dot(picked, weight)

    projected = lax.fori_loop(
        0, HIDDEN // 8, project_step, jnp.zeros((BLOCK * BLOCK, WIDTH), F32)
    )
    for part in range(2):
        wait_for(pair_block.at[pl.ds(part * 8, 8)], block_sem.at[0, part])
        wait_for(cot_block.at[pl.ds(part * 8, 8)], block_sem.at[1, part])
    for r in range(BLOCK):
        start = ((r % 4) * 4 + r // 4) * BLOCK
        flat[pl.ds(r * BLOCK, BLOCK), :] = projected[start : start + BLOCK] * (1.0 / SEQUENCES)

    def add_rows(i, value):
        first[pl.ds(i * BLOCK, BLOCK), :] = (
            (pair_block[i].astype(F32) + value).astype(BF16).astype(F32)
        )

    @pl.when(h == 0)
    def _():
        for i in range(BLOCK):
            add_rows(i, flat[pl.ds(i, BLOCK, stride=BLOCK), :])

    @pl.when(h == 1)
    def _():
        for i in range(BLOCK):
            add_rows(i, flat[pl.ds(i * BLOCK, BLOCK), :])

    def send_same(dst, sems, chips, steps, send):
        own = steps(0)

        def step(k):
            chip = chips(steps(GRID - k))
            remote(dst.at[own], dst.at[own], send, sems.at[own], chip, h).start()

        for k in range(1, GRID):
            step(k)

    def send_other(src, dst, sems, chips, steps, send):
        own = steps(0)

        def step(k):
            chip = chips(steps(GRID - 1 - k))
            remote(src, dst.at[own], send, sems.at[own], chip, other).start()

        for k in range(GRID):
            step(k)

    def block_product(totals, left, by_column, right):
        totals = list(totals)
        for t in range(BLOCK):
            across = right(t)
            for p in range(BLOCK):
                one = left[t, pl.ds(p, 1), :] if by_column else left[p, pl.ds(t, 1), :]
                totals[p] = totals[p] + one * across
        return tuple(totals)

    def no_totals():
        return tuple(jnp.zeros((BLOCK, WIDTH), F32) for _ in range(BLOCK))

    def contract(left, left_sem, left_own, by_column, right, right_sem, right_own, steps):
        def arrive(ref, sems, slot, skip):
            if skip is None:
                wait_for(ref.at[slot], sems.at[slot])
            else:

                @pl.when(slot != skip)
                def _():
                    wait_for(ref.at[slot], sems.at[slot])

        def block_step(k, totals):
            slot = steps(k)
            arrive(left, left_sem, slot, left_own)
            arrive(right, right_sem, slot, right_own)
            wide[...] = left[slot].astype(F32)
            return block_product(totals, wide, by_column, lambda t: right[slot, t].astype(F32))

        totals = lax.fori_loop(0, GRID, block_step, no_totals())
        return jnp.concatenate(totals, axis=0)

    def partial(part, n, totals):
        for p in range(BLOCK):
            part[n, p] = totals[p].astype(BF16)

    def sum_of(parts, sems, skip, steps):
        def step(k, total):
            slot = steps(k)
            if skip is None:
                wait_for(parts.at[slot], sems.at[slot])
            else:

                @pl.when(slot != skip)
                def _():
                    wait_for(parts.at[slot], sems.at[slot])

            return total + parts[slot].reshape(BLOCK * BLOCK, WIDTH).astype(F32)

        return lax.fori_loop(0, GRID, step, jnp.zeros((BLOCK * BLOCK, WIDTH), F32))

    def send_part(part, n, dst, slot, sems, chips, core, send):
        remote(part.at[n], dst.at[slot], send, sems.at[slot], chips(n), core).start()

    def turned(value, store):
        flat[...] = value
        for j in range(BLOCK):
            store(j, flat[pl.ds(j, BLOCK, stride=BLOCK), :].astype(BF16))

    def turn_cot(value):
        rounded = value.astype(BF16).astype(F32)
        cot_wide[...] = rounded.reshape(BLOCK, BLOCK, WIDTH)
        flat[...] = rounded
        for j in range(BLOCK):
            cot_turned[j] = flat[pl.ds(j, BLOCK, stride=BLOCK), :]

    def blocked(value):
        return value.astype(BF16).reshape(BLOCK, BLOCK, WIDTH)

    def gated(normed, weight, at):
        projected = dot(normed, weight[:, at * WIDTH : (at + 2) * WIDTH])
        gate, value = jax.nn.sigmoid(projected[:, :WIDTH]), projected[:, WIDTH:]
        return gate, value

    def keep_gated(ref, first_at, gate, value):
        ref[first_at] = value * gate * (1.0 - gate)
        ref[first_at + 1] = gate

    def keep_norm(ref, first_at, normed, scale):
        ref[first_at] = normed
        ref[first_at + 1] = jnp.broadcast_to(scale, normed.shape)

    normed, scale = layer_norm(first[...])
    rounded = normed.astype(BF16)
    left_gate, left_value = gated(rounded, out_in_weight, 0)
    o_left[own_j] = blocked(left_gate * left_value)
    send_same(o_left, pair_sem.at[0], row_chip, step_j, send_sem.at[10])
    right_gate, right_value = gated(rounded, out_in_weight, 2)

    def store_right(j, value):
        o_right_stage[j] = value

    turned(right_gate * right_value, store_right)
    send_other(o_right_stage, o_right, pair_sem.at[1], row_chip, step_j, send_sem.at[11])
    keep_gated(out_kept, 0, left_gate, left_value)
    keep_gated(out_kept, 2, right_gate, right_value)
    keep_norm(out_kept, 4, normed, scale)
    out_kept[6] = jax.nn.sigmoid(dot(rounded, out_in_weight[:, 4 * WIDTH :]))
    mixing = contract(
        o_left,
        pair_sem.at[0],
        own_j,
        False,
        o_right,
        pair_sem.at[1],
        None,
        step_j,
    )
    mixing_normed, mixing_scale = layer_norm(mixing)
    update = dot(mixing_normed.astype(BF16), out_out_weight[...])
    second = (first[...] + out_kept[6] * update).astype(BF16).astype(F32)

    normed, scale = layer_norm(second)
    rounded = normed.astype(BF16)
    right_gate, right_value = gated(rounded, in_in_weight, 2)
    i_right[own_i] = blocked(right_gate * right_value)
    send_same(i_right, pair_sem.at[4], col_chip, step_i, send_sem.at[14])
    left_gate, left_value = gated(rounded, in_in_weight, 0)
    i_left_stage[...] = blocked(left_gate * left_value)
    send_other(i_left_stage, i_left, pair_sem.at[5], col_chip, step_i, send_sem.at[15])
    keep_norm(out_kept, 7, mixing_normed, mixing_scale)
    out_kept[9] = update
    keep_gated(in_kept, 0, left_gate, left_value)
    keep_gated(in_kept, 2, right_gate, right_value)
    keep_norm(in_kept, 4, normed, scale)
    gating = jax.nn.sigmoid(dot(rounded, in_in_weight[:, 4 * WIDTH :]))
    in_kept[6] = gating
    in_kept[7] = second
    upstream = cot_block[...].reshape(BLOCK * BLOCK, WIDTH).astype(F32)
    upstream32[...] = upstream
    in_kept[8] = dot((upstream * gating).astype(BF16), in_out_turned[...])
    mixing = contract(
        i_left,
        pair_sem.at[5],
        None,
        True,
        i_right,
        pair_sem.at[4],
        own_i,
        step_i,
    )

    def input_pullback(kept, left_cot, right_cot, gating_part, weight, upstream):
        pieces = [
            (left_cot * kept[0]).astype(BF16),
            (left_cot * kept[1]).astype(BF16),
            (right_cot * kept[2]).astype(BF16),
            (right_cot * kept[3]).astype(BF16),
        ]
        normed_cot = gating_part + dot(
            jnp.concatenate(pieces, axis=1), weight[: 4 * WIDTH, :]
        )
        return upstream + layer_norm_pullback(kept[4], kept[5], normed_cot)

    normed, scale = layer_norm(mixing)
    turn_cot(layer_norm_pullback(normed, scale, in_kept[8]))

    def incoming_step(k, carry):
        n = step_i(GRID - 1 - k)
        wide[...] = i_right[n].astype(F32)
        totals = block_product(no_totals(), wide, False, lambda t: cot_turned[t])
        partial(left_parts, n, totals)
        send_part(
            left_parts, n, ib_left, own_j, pair_sem.at[2], row_chip, other, send_sem.at[12]
        )
        wide_too[...] = i_left[n].astype(F32)
        totals = block_product(no_totals(), wide_too, False, lambda t: cot_wide[t])

        @pl.when(n != own_i)
        def _():
            partial(right_parts, n, totals)
            send_part(
                right_parts, n, ib_right, own_i, pair_sem.at[3], col_chip, h, send_sem.at[13]
            )

        @pl.when(n == own_i)
        def _():
            partial(ib_right, n, totals)

        return carry

    lax.fori_loop(0, GRID, incoming_step, 0)
    gating = in_kept[6]
    update = dot(normed.astype(BF16), in_out_weight[...])
    result = (in_kept[7] + gating * update).astype(BF16)
    gating_cot = upstream32[...] * update * gating * (1.0 - gating)
    gating_part = dot(gating_cot.astype(BF16), in_in_turned[4 * WIDTH :, :])

    def hand_over(value, stage, got, sem, send):
        stage[...] = value.reshape(2, 8, BLOCK, WIDTH)
        for part in range(2):
            order = remote(stage.at[part], got, send.at[part], sem, (at, b), part)
            if part == 0:
                pl.when(odd == 1)(order.start)
            else:
                order.start()

    @pl.when(h == 0)
    def _():
        hand_over(result, output_stage, output_got, small_sem.at[0], output_sem)

    left_cot = sum_of(ib_left, pair_sem.at[2], None, step_j)
    right_cot = sum_of(ib_right, pair_sem.at[3], own_i, step_i)
    second_cot = input_pullback(
        in_kept, left_cot, right_cot, gating_part, in_in_turned, upstream32[...]
    )

    normed_cot = dot((second_cot * out_kept[6]).astype(BF16), out_out_turned[...])
    turn_cot(layer_norm_pullback(out_kept[7], out_kept[8], normed_cot))

    def outgoing_step(k, carry):
        n = step_j(GRID - 1 - k)
        wide[...] = o_right[n].astype(F32)
        totals = block_product(no_totals(), wide, False, lambda t: cot_turned[t])

        @pl.when(n != own_j)
        def _():
            partial(left_parts2, n, totals)
            send_part(
                left_parts2, n, ob_left, own_j, pair_sem.at[6], row_chip, h, send_sem.at[16]
            )

        @pl.when(n == own_j)
        def _():
            partial(ob_left, n, totals)

        totals = block_product(
            no_totals(), cot_wide, True, lambda t: o_left[n, t].astype(F32)
        )
        partial(right_parts2, n, totals)
        send_part(
            right_parts2, n, ob_right, own_i, pair_sem.at[7], col_chip, other, send_sem.at[17]
        )
        return carry

    lax.fori_loop(0, GRID, outgoing_step, 0)
    gating = out_kept[6]
    gating_cot = second_cot * out_kept[9] * gating * (1.0 - gating)
    gating_part = dot(gating_cot.astype(BF16), out_in_turned[4 * WIDTH :, :])
    flat[...] = sum_of(ob_left, pair_sem.at[6], own_j, step_j)
    left_cot = jnp.concatenate(
        [flat[pl.ds(j, BLOCK, stride=BLOCK), :] for j in range(BLOCK)], axis=0
    )
    right_cot = sum_of(ob_right, pair_sem.at[7], None, step_i)
    gradient = input_pullback(
        out_kept, left_cot, right_cot, gating_part, out_in_turned, second_cot
    )

    @pl.when(h == 0)
    def _():
        hand_over(gradient, gradient_stage, gradient_got, small_sem.at[1], gradient_sem)

    def stack(r, value):
        g, q = r // 4, r % 4
        stacked[g * BLOCK : (g + 1) * BLOCK, q * WIDTH : (q + 1) * WIDTH] = value.astype(BF16)

    flat[...] = gradient

    @pl.when(h == 0)
    def _():
        for r in range(BLOCK):
            stack(r, flat[pl.ds(r, BLOCK, stride=BLOCK), :])

    @pl.when(h == 1)
    def _():
        for r in range(BLOCK):
            stack(r, flat[pl.ds(r * BLOCK, BLOCK), :])

    for x8 in range(HIDDEN // 8):
        chunk = dot(
            stacked[...], turned_weight[:, x8 * 8 * WIDTH : (x8 + 1) * 8 * WIDTH]
        ).astype(BF16)
        for piece in range(8):
            start = (8 * x8 + piece) * BLOCK
            for g in range(4):
                grad_table[start : start + BLOCK, g * WIDTH : (g + 1) * WIDTH] = chunk[
                    g * BLOCK : (g + 1) * BLOCK, piece * WIDTH : (piece + 1) * WIDTH
                ]

    def cot_step(step):
        chips = [along_rows(a, GRID - 1 - 2 * step - n) for n in range(2)]
        sequences = jnp.concatenate(
            [
                msa_relayed[pl.ds(2 * chip, 2)].reshape(2 * 64, BLOCK * HIDDEN)
                for chip in chips
            ],
            axis=0,
        )
        sums = dot(sequences, grad_table[...]).astype(BF16)
        for n, chip in enumerate(chips):
            for core in range(2):
                start = (2 * n + core) * 64
                slot = 2 * chip + core
                cot_parts[slot] = sums[start : start + 64]
                target = cot_got.at[h, a]

                @pl.when(slot == row)
                def _():
                    pltpu.make_async_copy(cot_parts.at[slot], target, cot_sem.at[h, a]).start()

                @pl.when(slot != row)
                def _():
                    remote(
                        cot_parts.at[slot], target, send_sem.at[26], cot_sem.at[h, a], (chip, b), core
                    ).start()

    for step in range(4):
        cot_step(step)
    for core in range(2):

        def cot_sum(k, total, core=core):
            n = along_rows(a, k)
            wait_for(cot_got.at[core, n], cot_sem.at[core, n])
            return total + cot_got[core, n].astype(F32)

        total = lax.fori_loop(0, GRID, cot_sum, jnp.zeros((64, BLOCK * HIDDEN), F32))
        msa_cots[1 - core] = (total * (1.0 / SEQUENCES)).astype(BF16)

    cots = jnp.concatenate(
        [
            jnp.concatenate(
                [msa_cots[kind, :, g * WIDTH : (g + 1) * WIDTH] for kind in range(2)], axis=1
            )
            for g in range(4)
        ],
        axis=0,
    )
    for q in range(4):
        normed_cots = dot(
            cots, spread_factor[q * 2 * WIDTH : (q + 1) * 2 * WIDTH, :], ((1,), (1,))
        )
        for g in range(4):
            rows = pl.ds(4 * g + q, 64, stride=BLOCK)
            value = layer_norm_pullback(
                jnp.concatenate([normed_msa[0][rows, :], normed_msa[1][rows, :]], axis=1),
                msa_scale[rows, :1],
                normed_cots[g * 64 : (g + 1) * 64],
            )
            alignment_first[rows, :] = value[:, :WIDTH]
            alignment_second[rows, :] = value[:, WIDTH:]
    @pl.when(keeps_first)
    def _():
        pair_output[...] = output_stage[0]
        pair_gradient[...] = gradient_stage[0]

    @pl.when(jnp.logical_not(keeps_first))
    def _():
        wait_for(output_got, small_sem.at[0])
        pair_output[...] = output_got[...]
        wait_for(gradient_got, small_sem.at[1])
        pair_gradient[...] = gradient_got[...]

    @pl.when(jnp.logical_not(relay_stays))
    def _():
        for slot in range(4):
            wait_for(relay_left.at[pl.ds(0, 32)], relay_send_sem.at[slot])

    msa_sent(right_jd, msa_direct, 0, send_sem.at[2])
    msa_sent(left_ic, msa_direct, 1, send_sem.at[3])
    block_sent(0, pair_input)
    block_sent(1, cotangent)
    msa_sent(relay_left, msa_relayed, 0, send_sem.at[8])
    msa_sent(relay_right, msa_relayed, 1, send_sem.at[9])
    for number in (10, 13, 14, 16):
        wait_for(o_left.at[pl.ds(0, 7)], send_sem.at[number])
    for number in (11, 12, 15, 17):
        wait_for(o_left, send_sem.at[number])
    wait_for(cot_parts.at[pl.ds(0, 15)], send_sem.at[26])

    @pl.when(h == 0)
    def _():
        wait_for(output_got, output_sem.at[1])
        wait_for(gradient_got, gradient_sem.at[1])

        @pl.when(odd == 1)
        def _():
            wait_for(output_got, output_sem.at[0])
            wait_for(gradient_got, gradient_sem.at[0])


def pair_updates(homolog, factor_weight, pair_input, cotangent, weights):
    gathered = pltpu.VMEM((GRID, BLOCK, BLOCK, WIDTH), BF16)
    block = pltpu.VMEM((BLOCK, BLOCK, WIDTH), BF16)
    flat = pltpu.VMEM((BLOCK * BLOCK, WIDTH), F32)
    shares = pltpu.VMEM((64, BLOCK * HIDDEN), BF16)
    all_sequences = pltpu.VMEM((2 * GRID, 64, BLOCK * HIDDEN), BF16)
    half_block = pltpu.VMEM((8, BLOCK, WIDTH), BF16)
    wide_block = pltpu.VMEM((BLOCK, BLOCK, WIDTH), F32)
    half_wide = pltpu.VMEM((8, BLOCK, WIDTH), F32)
    whole_side = pltpu.VMEM((64 * BLOCK, WIDTH), F32)
    dma = pltpu.SemaphoreType.DMA
    vmem = pl.BlockSpec(memory_space=pltpu.VMEM)
    return pl.pallas_call(
        pair_kernel,
        out_shape=(half_block, half_wide, whole_side, whole_side),
        in_specs=[pl.BlockSpec(memory_space=pl.ANY)] * 9,
        out_specs=(vmem,) * 4,
        scratch_shapes=[
            pltpu.VMEM((64 * BLOCK, 2 * WIDTH), BF16),
            pltpu.VMEM((2 * HIDDEN, 2 * WIDTH), BF16),
            pltpu.VMEM((HIDDEN * HIDDEN, WIDTH), BF16),
            pltpu.VMEM((WIDTH, 5 * WIDTH), BF16),
            pltpu.VMEM((WIDTH, WIDTH), BF16),
            pltpu.VMEM((WIDTH, 5 * WIDTH), BF16),
            pltpu.VMEM((WIDTH, WIDTH), BF16),
            [pltpu.VMEM((64 * BLOCK, WIDTH), F32)] * 2,
            pltpu.VMEM((64 * BLOCK, WIDTH), F32),
            pltpu.VMEM((8 * WIDTH, 2 * WIDTH), BF16),
            shares,
            shares,
            shares,
            shares,
            block,
            block,
            shares,
            shares,
            all_sequences,
            all_sequences,
            gathered,
            gathered,
            block,
            gathered,
            gathered,
            block,
            gathered,
            gathered,
            gathered,
            gathered,
            gathered,
            gathered,
            gathered,
            gathered,
            pltpu.VMEM((HIDDEN * HIDDEN, WIDTH), F32),
            pltpu.VMEM((HIDDEN * WIDTH, WIDTH), BF16),
            pltpu.VMEM((HIDDEN * WIDTH, 4 * WIDTH), BF16),
            pltpu.VMEM((4 * WIDTH, HIDDEN * WIDTH), BF16),
            pltpu.VMEM((5 * WIDTH, WIDTH), BF16),
            pltpu.VMEM((WIDTH, WIDTH), BF16),
            pltpu.VMEM((5 * WIDTH, WIDTH), BF16),
            pltpu.VMEM((WIDTH, WIDTH), BF16),
            pltpu.VMEM((BLOCK * HIDDEN, BLOCK * HIDDEN), F32),
            wide_block,
            wide_block,
            wide_block,
            wide_block,
            flat,
            pltpu.VMEM((10, BLOCK * BLOCK, WIDTH), F32),
            pltpu.VMEM((9, BLOCK * BLOCK, WIDTH), F32),
            flat,
            flat,
            pltpu.VMEM((64, 4 * WIDTH), BF16),
            pltpu.VMEM((BLOCK * HIDDEN, BLOCK * HIDDEN), BF16),
            pltpu.VMEM((2, 64, BLOCK * HIDDEN), BF16),
            all_sequences,
            pltpu.VMEM((2, GRID, 64, BLOCK * HIDDEN), BF16),
            pltpu.VMEM((2, 8, BLOCK, WIDTH), BF16),
            half_block,
            pltpu.VMEM((2, 8, BLOCK, WIDTH), F32),
            half_wide,
            dma((4,)),
            dma((4,)),
            dma((2, 2)),
            dma((2, 2 * GRID)),
            dma((8, GRID)),
            dma((2, GRID)),
            dma((2,)),
            dma((28,)),
            dma((2,)),
            dma((2,)),
            dma((7,)),
        ],
        compiler_params=pltpu.CompilerParams(
            collective_id=1, has_side_effects=True, vmem_limit_bytes=60 << 20
        ),
        name="pair_updates",
    )(homolog, factor_weight, pair_input, cotangent, *weights)


def hand_out_kernel(
    pair_output,
    pair_gradient,
    alignment_first,
    alignment_second,
    pair_output_out,
    pair_gradient_out,
    alignment_gradient,
    copy_sem,
):
    rows = alignment_first.shape[0] // 4
    pairs = [(pair_output, pair_output_out), (pair_gradient, pair_gradient_out)]
    for part in range(4):
        some = pl.ds(part * rows, rows)
        for side, held in enumerate((alignment_first, alignment_second)):
            target = alignment_gradient.at[some, pl.ds(side * WIDTH, WIDTH)]
            pairs.append((held.at[some], target))
    copies = [
        pltpu.make_async_copy(src, dst, copy_sem.at[number])
        for number, (src, dst) in enumerate(pairs)
    ]
    for copy in copies:
        copy.start()
    for copy in copies:
        copy.wait()


def body(
    homolog_features,
    pair_input,
    cotangent,
    homolog_factor_matrix,
    outer_output_weight,
    outgoing_input_weight,
    outgoing_output_weight,
    incoming_input_weight,
    incoming_output_weight,
):
    sequences, residues, depth = homolog_features.shape
    homolog = homolog_features.reshape(sequences * residues, depth)
    factor_weight = homolog_factor_matrix.T
    results = pair_updates(
        homolog,
        factor_weight,
        pair_input,
        cotangent,
        (
            outer_output_weight,
            outgoing_input_weight,
            outgoing_output_weight,
            incoming_input_weight,
            incoming_output_weight,
        ),
    )
    anywhere = pl.BlockSpec(memory_space=pl.ANY)
    pair_output, pair_gradient, alignment_gradient = pl.pallas_call(
        hand_out_kernel,
        out_shape=(
            jax.ShapeDtypeStruct(pair_input.shape, BF16),
            jax.ShapeDtypeStruct(pair_input.shape, F32),
            jax.ShapeDtypeStruct(homolog.shape, F32),
        ),
        in_specs=[pl.BlockSpec(memory_space=pltpu.VMEM)] * 4,
        out_specs=(anywhere,) * 3,
        scratch_shapes=[pltpu.SemaphoreType.DMA((10,))],
        compiler_params=pltpu.CompilerParams(vmem_limit_bytes=16 << 20),
        name="hand_out",
    )(*results)
    return pair_output, pair_gradient, alignment_gradient.reshape(sequences, residues, depth)


def solution(mesh):
    split = P("row", "col", None)
    return jax.shard_map(
        body,
        mesh=mesh,
        in_specs=(split, split, split, P(), P(), P(), P(), P(), P()),
        out_specs=(split, split, split),
        check_vma=False,
    )
```

```python
import jax
import jax.numpy as jnp
from jax import lax
from jax.experimental import pallas as pl
from jax.experimental.pallas import tpu as pltpu
from jax.sharding import PartitionSpec as P

SEQUENCES = 1024
EPSILON = 1e-05
MESH = pl.DeviceIdType.MESH
F32 = jnp.float32
BF16 = jnp.bfloat16
GRID = 8
BLOCK = 16
WIDTH = 128
HIDDEN = 32


def dot(lhs, rhs, dims=((1,), (0,))):
    return lax.dot_general(lhs, rhs, (dims, ((), ())), preferred_element_type=F32)


def layer_norm(inputs):
    centered = inputs - jnp.mean(inputs, axis=-1, keepdims=True)
    spread = jnp.mean(centered * centered, axis=-1, keepdims=True)
    scale = lax.rsqrt(spread + EPSILON)
    return centered * scale, scale


def layer_norm_pullback(normed, scale, upstream):
    along = jnp.mean(upstream * normed, axis=-1, keepdims=True)
    return scale * (upstream - jnp.mean(upstream, axis=-1, keepdims=True) - normed * along)


def repeat_factor(factor_weight, spread_factor):
    hidden_row = lax.broadcasted_iota(jnp.int32, (2 * HIDDEN, 2 * WIDTH), 0)
    hidden_lane = lax.broadcasted_iota(jnp.int32, (2 * HIDDEN, 2 * WIDTH), 1)
    repeats = (hidden_lane % HIDDEN + HIDDEN * (hidden_lane // WIDTH) == hidden_row).astype(F32)
    repeated = dot(factor_weight[...], repeats.astype(BF16), ((0,), (0,)))
    lane_quarter = lax.broadcasted_iota(jnp.int32, (2 * WIDTH, 2 * WIDTH), 1) % WIDTH // HIDDEN
    for q in range(4):
        spread_factor[q * 2 * WIDTH : (q + 1) * 2 * WIDTH, :] = jnp.where(
            lane_quarter == q, repeated, 0.0
        ).astype(BF16)


def pair_kernel(
    homolog_hbm,
    factor_weight_hbm,
    pair_input,
    cotangent,
    outer_weight_hbm,
    out_in_weight_hbm,
    out_out_weight_hbm,
    in_in_weight_hbm,
    in_out_weight_hbm,
    pair_output,
    pair_gradient,
    alignment_first,
    alignment_second,
    homolog,
    factor_weight,
    outer_weight,
    out_in_weight,
    out_out_weight,
    in_in_weight,
    in_out_weight,
    normed_msa,
    msa_scale,
    spread_factor,
    left_ic,
    left_ci,
    right_dj,
    right_jd,
    pair_block,
    cot_block,
    relay_left,
    relay_right,
    msa_relayed,
    msa_direct,
    o_left,
    o_right,
    o_right_stage,
    i_left,
    i_right,
    i_left_stage,
    ib_right,
    ib_left,
    ob_right,
    ob_left,
    left_parts,
    right_parts,
    left_parts2,
    right_parts2,
    wide_weight,
    table_weight,
    spread_weight,
    turned_weight,
    out_in_turned,
    out_out_turned,
    in_in_turned,
    in_out_turned,
    outer32,
    wide,
    wide_too,
    cot_wide,
    cot_turned,
    flat,
    out_kept,
    in_kept,
    first,
    upstream32,
    stacked,
    grad_table,
    msa_cots,
    cot_parts,
    cot_got,
    output_stage,
    output_got,
    gradient_stage,
    gradient_got,
    relay_sem,
    relay_send_sem,
    block_sem,
    msa_sem,
    pair_sem,
    cot_sem,
    small_sem,
    send_sem,
    output_sem,
    gradient_sem,
    input_sem,
):
    row, col = lax.axis_index("row"), lax.axis_index("col")
    a, h, b = row // 2, row % 2, col
    other = 1 - h
    odd = b % 2
    at = (a + 4 * odd) % GRID
    own_i = at * other + b * h
    own_j = b * other + at * h
    stays = jnp.logical_and(a == b, odd == 0)

    def chip_at(i, j):
        return (i + 4 * (j % 2)) % GRID, j

    def row_chip(n):
        return chip_at(at * other + n * h, n * other + b * h)

    def col_chip(n):
        return chip_at(n * other + at * h, b * other + n * h)

    def apart(k):
        m = k // 2
        return m + (m // 2) * (5 - 2 * m), k % 2

    def along_rows(own, k):
        dm, dv = apart(k)
        return (own // 4 + dv) % 2 * 4 + (own % 4 + dm) % 4

    def along_columns(own, k):
        dm, dv = apart(k)
        return (own // 2 + dm) % 4 * 2 + (own % 2 + dv) % 2

    def step_i(k):
        return along_rows(at, k) * other + along_columns(b, k) * h

    def step_j(k):
        return along_columns(b, k) * other + along_rows(at, k) * h

    relay_column = (a % 4 + b // 2 + 2 * (b % 4)) % 4 * 2 + a // 4
    relay_chip = chip_at(b, relay_column)
    source_row = b % 2 * 4 + (b // 2 + 16 - at // 2 - 2 * (at % 4)) % 4
    relay_stays = jnp.logical_and(relay_column == b, relay_chip[0] == a)

    def column(n):
        return n, b

    def line(n):
        return chip_at(at, n)

    def remote(src, dst, send, recv, chip, core):
        return pltpu.make_async_remote_copy(
            src_ref=src,
            dst_ref=dst,
            send_sem=send,
            recv_sem=recv,
            device_id=(2 * chip[0] + core, chip[1]),
            device_id_type=MESH,
        )

    def wait_for(ref, sem):
        pltpu.make_async_copy(ref, ref, sem).wait()

    inputs = (
        (homolog_hbm, homolog),
        (factor_weight_hbm, factor_weight),
        (outer_weight_hbm, outer_weight),
        (out_in_weight_hbm, out_in_weight),
        (out_out_weight_hbm, out_out_weight),
        (in_in_weight_hbm, in_in_weight),
        (in_out_weight_hbm, in_out_weight),
    )
    copies = [
        pltpu.make_async_copy(src, dst, input_sem.at[number])
        for number, (src, dst) in enumerate(inputs)
    ]
    for copy in copies:
        copy.start()

    barrier = pltpu.get_barrier_semaphore()

    def greet(chip, core):
        pl.semaphore_signal(
            barrier, inc=1, device_id=(2 * chip[0] + core, chip[1]), device_id_type=MESH
        )

    def greet_step(k, carry):
        for core in range(2):
            greet(column(along_rows(a, GRID - k)), core)
            greet(line(along_columns(b, GRID - k)), core)
        return carry

    @pl.when(jnp.logical_not(relay_stays))
    def _():
        greet((source_row, at), h)

    @pl.when(h == 1)
    def _():
        greet((b, at), 0)

    @pl.when(jnp.logical_and(h == 1, jnp.logical_not(stays)))
    def _():
        greet((b, at), 1)

    lax.fori_loop(1, GRID, greet_step, 0)
    greet((a, b), other)
    copies[0].wait()
    copies[1].wait()

    def normalize_step(n, carry):
        rows = pl.ds(pl.multiple_of(n * 256, 256), 256)
        normed, scale = layer_norm(homolog[rows, :].astype(F32))
        msa_scale[rows, :] = jnp.broadcast_to(scale, (256, WIDTH))
        normed_msa[0][rows, :] = normed[:, :WIDTH]
        normed_msa[1][rows, :] = normed[:, WIDTH:]
        return carry

    lax.fori_loop(0, 4, normalize_step, 0)
    repeat_factor(factor_weight, spread_factor)
    groups = []
    for g in range(4):
        pieces = [
            normed_msa[part][pl.ds(4 * g + q, 64, stride=BLOCK), :].astype(BF16)
            for q in range(4)
            for part in range(2)
        ]
        groups.append(jnp.concatenate(pieces, axis=1))
    factors = dot(jnp.concatenate(groups, axis=0), spread_factor[...]).astype(BF16)
    left_value = jnp.concatenate(
        [factors[g * 64 : (g + 1) * 64, :WIDTH] for g in range(4)], axis=1
    )
    right_value = jnp.concatenate(
        [factors[g * 64 : (g + 1) * 64, WIDTH:] for g in range(4)], axis=1
    )
    left_ic[...] = left_value
    right_jd[...] = right_value
    before = lax.broadcasted_iota(jnp.int32, (BLOCK * HIDDEN, BLOCK * HIDDEN), 0)
    after = lax.broadcasted_iota(jnp.int32, (BLOCK * HIDDEN, BLOCK * HIDDEN), 1)
    moved = (before == after % BLOCK * HIDDEN + after // BLOCK).astype(F32).astype(BF16)
    turned_factors = dot(jnp.concatenate([left_value, right_value], axis=0), moved).astype(BF16)
    left_ci[...] = turned_factors[:64]
    right_dj[...] = turned_factors[64:]

    for copy in copies[2:]:
        copy.wait()
    keeps_first = jnp.logical_and(h == 0, odd == 0)
    keeps_second = jnp.logical_and(h == 1, stays)
    pl.semaphore_wait(barrier, 31 - relay_stays.astype(jnp.int32) - keeps_second.astype(jnp.int32))

    for slot in range(4):
        src, dst = ((left_ci, relay_left), (right_dj, relay_right))[slot // 2]
        half = pl.ds(slot % 2 * 32, 32)

        @pl.when(jnp.logical_not(relay_stays))
        def _():
            remote(
                src.at[half],
                dst.at[half],
                relay_send_sem.at[slot],
                relay_sem.at[slot],
                relay_chip,
                h,
            ).start()

        @pl.when(relay_stays)
        def _():
            pltpu.make_async_copy(src.at[half], dst.at[half], relay_sem.at[slot]).start()

    def msa_send(src, dst, sems, slot, chip_of, core, send, half=None):
        whole = half is None
        source = src if whole else src.at[pl.ds(half * 32, 32)]
        target = dst.at[slot] if whole else dst.at[slot, pl.ds(half * 32, 32)]

        def step(k, carry):
            place = (GRID - 1 - k) * other + k * h

            @pl.when(jnp.logical_or(place > 0, h != core))
            def _():
                remote(source, target, send, sems.at[slot], chip_of(place), core).start()

            return carry

        lax.fori_loop(0, GRID, step, 0)

        @pl.when(h == core)
        def _():
            pltpu.make_async_copy(source, target, sems.at[slot]).start()

    def column_step(k):
        return column(along_rows(a, k))

    def line_step(k):
        return line(along_columns(b, k))

    def msa_sent(src, dst, core, send):
        @pl.when(h == core)
        def _():
            wait_for(dst.at[pl.ds(0, 7)], send)

        @pl.when(h != core)
        def _():
            wait_for(dst.at[pl.ds(0, 8)], send)

    msa_send(right_jd, msa_direct, msa_sem.at[1], row, column_step, 0, send_sem.at[2])
    msa_send(left_ic, msa_direct, msa_sem.at[1], row, column_step, 1, send_sem.at[3])

    for slot, (src, dst) in enumerate(((pair_input, pair_block), (cotangent, cot_block))):
        half = dst.at[pl.ds(h * 8, 8)]
        sem = block_sem.at[slot, h]

        @pl.when(keeps_first)
        def _():
            pltpu.make_async_copy(src, half, sem).start()

        @pl.when(jnp.logical_not(keeps_first))
        def _():
            remote(src, half, send_sem.at[4 + slot], sem, chip_at(a, b), 0).start()

        @pl.when(keeps_second)
        def _():
            pltpu.make_async_copy(src, half, sem).start()

        @pl.when(jnp.logical_not(keeps_second))
        def _():
            remote(src, half, send_sem.at[6 + slot], sem, chip_at(b, a), 1).start()

    def block_sent(slot, src):
        @pl.when(jnp.logical_not(keeps_first))
        def _():
            wait_for(src, send_sem.at[4 + slot])

        @pl.when(jnp.logical_not(keeps_second))
        def _():
            wait_for(src, send_sem.at[6 + slot])

    relay_slot = 2 * source_row + h
    for slot in range(4):
        half = slot % 2
        src = (relay_left, relay_right)[slot // 2]
        wait_for(src.at[pl.ds(half * 32, 32)], relay_sem.at[slot])
        kind = slot // 2
        msa_send(
            src, msa_relayed, msa_sem.at[0], relay_slot, line_step, kind, send_sem.at[8 + kind], half
        )

    wide_weight[: HIDDEN * HIDDEN, :] = outer_weight[...].astype(F32)
    spread_weight[...] = jnp.zeros(spread_weight.shape, BF16)

    def weight_step(n, carry):
        start = pl.multiple_of(n * WIDTH, WIDTH)

        def lay_out(piece):
            for q in range(4):
                some = pl.ds(start + q * HIDDEN, HIDDEN)
                table_weight[some, :] = piece
                spread_weight[some, q * WIDTH : (q + 1) * WIDTH] = piece

        @pl.when(h == 0)
        def _():
            lay_out(outer_weight[pl.ds(pl.multiple_of(n * HIDDEN, HIDDEN), HIDDEN), :])

        @pl.when(h == 1)
        def _():
            lay_out(wide_weight[pl.ds(n, HIDDEN, stride=HIDDEN), :].astype(BF16))

        return carry

    lax.fori_loop(0, HIDDEN, weight_step, 0)

    def turn_step(n, carry):
        rows = pl.ds(pl.multiple_of(n * 2 * WIDTH, 2 * WIDTH), 2 * WIDTH)
        turned_weight[:, rows] = spread_weight[rows, :].T
        return carry

    lax.fori_loop(0, HIDDEN // 2, turn_step, 0)
    for weight, turned_one in (
        (out_in_weight, out_in_turned),
        (out_out_weight, out_out_turned),
        (in_in_weight, in_in_turned),
        (in_out_weight, in_out_turned),
    ):
        turned_one[...] = weight[...].T

    def outer_step(k, carry):
        n = (b // 2 + k) % 4

        def msa_wait(part, carry):
            slot = 4 * n + part
            wait_for(msa_relayed.at[slot], msa_sem.at[0, slot])
            wait_for(msa_direct.at[slot], msa_sem.at[1, slot])
            return carry

        lax.fori_loop(0, 4, msa_wait, 0)
        four = pl.ds(4 * n, 4)
        outer32[...] += dot(
            msa_relayed[four].reshape(256, BLOCK * HIDDEN),
            msa_direct[four].reshape(256, BLOCK * HIDDEN),
            ((0,), (0,)),
        )
        return carry

    outer32[...] = jnp.zeros(outer32.shape, F32)
    lax.fori_loop(0, 4, outer_step, 0)
    lane_part = lax.broadcasted_iota(jnp.int32, (BLOCK, WIDTH), 1) // HIDDEN

    def project_step(d8, total):
        columns = []
        for part in range(8):
            tile = outer32[pl.ds(pl.multiple_of((8 * d8 + part) * BLOCK, BLOCK), BLOCK), :]
            columns.append(
                jnp.concatenate(
                    [
                        jnp.where(lane_part == q, tile[:, g * WIDTH : (g + 1) * WIDTH], 0.0)
                        for q in range(4)
                        for g in range(4)
                    ],
                    axis=0,
                )
            )
        picked = jnp.concatenate(columns, axis=1).astype(BF16)
        weight = table_weight[pl.ds(pl.multiple_of(d8 * 8 * WIDTH, 8 * WIDTH), 8 * WIDTH), :]
        return total + dot(picked, weight)

    projected = lax.fori_loop(
        0, HIDDEN // 8, project_step, jnp.zeros((BLOCK * BLOCK, WIDTH), F32)
    )
    for part in range(2):
        wait_for(pair_block.at[pl.ds(part * 8, 8)], block_sem.at[0, part])
        wait_for(cot_block.at[pl.ds(part * 8, 8)], block_sem.at[1, part])
    for r in range(BLOCK):
        start = ((r % 4) * 4 + r // 4) * BLOCK
        flat[pl.ds(r * BLOCK, BLOCK), :] = projected[start : start + BLOCK] * (1.0 / SEQUENCES)

    def add_rows(i, value):
        first[pl.ds(i * BLOCK, BLOCK), :] = (
            (pair_block[i].astype(F32) + value).astype(BF16).astype(F32)
        )

    @pl.when(h == 0)
    def _():
        for i in range(BLOCK):
            add_rows(i, flat[pl.ds(i, BLOCK, stride=BLOCK), :])

    @pl.when(h == 1)
    def _():
        for i in range(BLOCK):
            add_rows(i, flat[pl.ds(i * BLOCK, BLOCK), :])

    def send_same(dst, sems, chips, steps, send):
        own = steps(0)

        def step(k):
            chip = chips(steps(GRID - k))
            remote(dst.at[own], dst.at[own], send, sems.at[own], chip, h).start()

        for k in range(1, GRID):
            step(k)

    def send_other(src, dst, sems, chips, steps, send):
        own = steps(0)

        def step(k):
            chip = chips(steps(GRID - 1 - k))
            remote(src, dst.at[own], send, sems.at[own], chip, other).start()

        for k in range(GRID):
            step(k)

    def block_product(totals, left, by_column, right):
        totals = list(totals)
        for t in range(BLOCK):
            across = right(t)
            for p in range(BLOCK):
                one = left[t, pl.ds(p, 1), :] if by_column else left[p, pl.ds(t, 1), :]
                totals[p] = totals[p] + one * across
        return tuple(totals)

    def no_totals():
        return tuple(jnp.zeros((BLOCK, WIDTH), F32) for _ in range(BLOCK))

    def contract(left, left_sem, left_own, by_column, right, right_sem, right_own, steps):
        def arrive(ref, sems, slot, skip):
            if skip is None:
                wait_for(ref.at[slot], sems.at[slot])
            else:

                @pl.when(slot != skip)
                def _():
                    wait_for(ref.at[slot], sems.at[slot])

        def block_step(k, totals):
            slot = steps(k)
            arrive(left, left_sem, slot, left_own)
            arrive(right, right_sem, slot, right_own)
            wide[...] = left[slot].astype(F32)
            return block_product(totals, wide, by_column, lambda t: right[slot, t].astype(F32))

        totals = lax.fori_loop(0, GRID, block_step, no_totals())
        return jnp.concatenate(totals, axis=0)

    def partial(part, n, totals):
        for p in range(BLOCK):
            part[n, p] = totals[p].astype(BF16)

    def sum_of(parts, sems, skip, steps):
        def step(k, total):
            slot = steps(k)
            if skip is None:
                wait_for(parts.at[slot], sems.at[slot])
            else:

                @pl.when(slot != skip)
                def _():
                    wait_for(parts.at[slot], sems.at[slot])

            return total + parts[slot].reshape(BLOCK * BLOCK, WIDTH).astype(F32)

        return lax.fori_loop(0, GRID, step, jnp.zeros((BLOCK * BLOCK, WIDTH), F32))

    def send_part(part, n, dst, slot, sems, chips, core, send):
        remote(part.at[n], dst.at[slot], send, sems.at[slot], chips(n), core).start()

    def turned(value, store):
        flat[...] = value
        for j in range(BLOCK):
            store(j, flat[pl.ds(j, BLOCK, stride=BLOCK), :].astype(BF16))

    def turn_cot(value):
        rounded = value.astype(BF16).astype(F32)
        cot_wide[...] = rounded.reshape(BLOCK, BLOCK, WIDTH)
        flat[...] = rounded
        for j in range(BLOCK):
            cot_turned[j] = flat[pl.ds(j, BLOCK, stride=BLOCK), :]

    def blocked(value):
        return value.astype(BF16).reshape(BLOCK, BLOCK, WIDTH)

    def gated(normed, weight, at):
        projected = dot(normed, weight[:, at * WIDTH : (at + 2) * WIDTH])
        gate, value = jax.nn.sigmoid(projected[:, :WIDTH]), projected[:, WIDTH:]
        return gate, value

    def keep_gated(ref, first_at, gate, value):
        ref[first_at] = value * gate * (1.0 - gate)
        ref[first_at + 1] = gate

    def keep_norm(ref, first_at, normed, scale):
        ref[first_at] = normed
        ref[first_at + 1] = jnp.broadcast_to(scale, normed.shape)

    normed, scale = layer_norm(first[...])
    rounded = normed.astype(BF16)
    left_gate, left_value = gated(rounded, out_in_weight, 0)
    o_left[own_j] = blocked(left_gate * left_value)
    send_same(o_left, pair_sem.at[0], row_chip, step_j, send_sem.at[10])
    right_gate, right_value = gated(rounded, out_in_weight, 2)

    def store_right(j, value):
        o_right_stage[j] = value

    turned(right_gate * right_value, store_right)
    send_other(o_right_stage, o_right, pair_sem.at[1], row_chip, step_j, send_sem.at[11])
    keep_gated(out_kept, 0, left_gate, left_value)
    keep_gated(out_kept, 2, right_gate, right_value)
    keep_norm(out_kept, 4, normed, scale)
    out_kept[6] = jax.nn.sigmoid(dot(rounded, out_in_weight[:, 4 * WIDTH :]))
    mixing = contract(
        o_left,
        pair_sem.at[0],
        own_j,
        False,
        o_right,
        pair_sem.at[1],
        None,
        step_j,
    )
    mixing_normed, mixing_scale = layer_norm(mixing)
    update = dot(mixing_normed.astype(BF16), out_out_weight[...])
    second = (first[...] + out_kept[6] * update).astype(BF16).astype(F32)

    normed, scale = layer_norm(second)
    rounded = normed.astype(BF16)
    right_gate, right_value = gated(rounded, in_in_weight, 2)
    i_right[own_i] = blocked(right_gate * right_value)
    send_same(i_right, pair_sem.at[4], col_chip, step_i, send_sem.at[14])
    left_gate, left_value = gated(rounded, in_in_weight, 0)
    i_left_stage[...] = blocked(left_gate * left_value)
    send_other(i_left_stage, i_left, pair_sem.at[5], col_chip, step_i, send_sem.at[15])
    keep_norm(out_kept, 7, mixing_normed, mixing_scale)
    out_kept[9] = update
    keep_gated(in_kept, 0, left_gate, left_value)
    keep_gated(in_kept, 2, right_gate, right_value)
    keep_norm(in_kept, 4, normed, scale)
    gating = jax.nn.sigmoid(dot(rounded, in_in_weight[:, 4 * WIDTH :]))
    in_kept[6] = gating
    in_kept[7] = second
    upstream = cot_block[...].reshape(BLOCK * BLOCK, WIDTH).astype(F32)
    upstream32[...] = upstream
    in_kept[8] = dot((upstream * gating).astype(BF16), in_out_turned[...])
    mixing = contract(
        i_left,
        pair_sem.at[5],
        None,
        True,
        i_right,
        pair_sem.at[4],
        own_i,
        step_i,
    )

    def input_pullback(kept, left_cot, right_cot, gating_part, weight, upstream):
        pieces = [
            (left_cot * kept[0]).astype(BF16),
            (left_cot * kept[1]).astype(BF16),
            (right_cot * kept[2]).astype(BF16),
            (right_cot * kept[3]).astype(BF16),
        ]
        normed_cot = gating_part + dot(
            jnp.concatenate(pieces, axis=1), weight[: 4 * WIDTH, :]
        )
        return upstream + layer_norm_pullback(kept[4], kept[5], normed_cot)

    normed, scale = layer_norm(mixing)
    turn_cot(layer_norm_pullback(normed, scale, in_kept[8]))

    def incoming_step(k, carry):
        n = step_i(GRID - 1 - k)
        wide[...] = i_right[n].astype(F32)
        totals = block_product(no_totals(), wide, False, lambda t: cot_turned[t])
        partial(left_parts, n, totals)
        send_part(
            left_parts, n, ib_left, own_j, pair_sem.at[2], row_chip, other, send_sem.at[12]
        )
        wide_too[...] = i_left[n].astype(F32)
        totals = block_product(no_totals(), wide_too, False, lambda t: cot_wide[t])

        @pl.when(n != own_i)
        def _():
            partial(right_parts, n, totals)
            send_part(
                right_parts, n, ib_right, own_i, pair_sem.at[3], col_chip, h, send_sem.at[13]
            )

        @pl.when(n == own_i)
        def _():
            partial(ib_right, n, totals)

        return carry

    lax.fori_loop(0, GRID, incoming_step, 0)
    gating = in_kept[6]
    update = dot(normed.astype(BF16), in_out_weight[...])
    result = (in_kept[7] + gating * update).astype(BF16)
    gating_cot = upstream32[...] * update * gating * (1.0 - gating)
    gating_part = dot(gating_cot.astype(BF16), in_in_turned[4 * WIDTH :, :])

    def hand_over(value, stage, got, sem, send):
        stage[...] = value.reshape(2, 8, BLOCK, WIDTH)
        for part in range(2):
            order = remote(stage.at[part], got, send.at[part], sem, (at, b), part)
            if part == 0:
                pl.when(odd == 1)(order.start)
            else:
                order.start()

    @pl.when(h == 0)
    def _():
        hand_over(result, output_stage, output_got, small_sem.at[0], output_sem)

    left_cot = sum_of(ib_left, pair_sem.at[2], None, step_j)
    right_cot = sum_of(ib_right, pair_sem.at[3], own_i, step_i)
    second_cot = input_pullback(
        in_kept, left_cot, right_cot, gating_part, in_in_turned, upstream32[...]
    )

    normed_cot = dot((second_cot * out_kept[6]).astype(BF16), out_out_turned[...])
    turn_cot(layer_norm_pullback(out_kept[7], out_kept[8], normed_cot))

    def outgoing_step(k, carry):
        n = step_j(GRID - 1 - k)
        wide[...] = o_right[n].astype(F32)
        totals = block_product(no_totals(), wide, False, lambda t: cot_turned[t])

        @pl.when(n != own_j)
        def _():
            partial(left_parts2, n, totals)
            send_part(
                left_parts2, n, ob_left, own_j, pair_sem.at[6], row_chip, h, send_sem.at[16]
            )

        @pl.when(n == own_j)
        def _():
            partial(ob_left, n, totals)

        totals = block_product(
            no_totals(), cot_wide, True, lambda t: o_left[n, t].astype(F32)
        )
        partial(right_parts2, n, totals)
        send_part(
            right_parts2, n, ob_right, own_i, pair_sem.at[7], col_chip, other, send_sem.at[17]
        )
        return carry

    lax.fori_loop(0, GRID, outgoing_step, 0)
    gating = out_kept[6]
    gating_cot = second_cot * out_kept[9] * gating * (1.0 - gating)
    gating_part = dot(gating_cot.astype(BF16), out_in_turned[4 * WIDTH :, :])
    flat[...] = sum_of(ob_left, pair_sem.at[6], own_j, step_j)
    left_cot = jnp.concatenate(
        [flat[pl.ds(j, BLOCK, stride=BLOCK), :] for j in range(BLOCK)], axis=0
    )
    right_cot = sum_of(ob_right, pair_sem.at[7], None, step_i)
    gradient = input_pullback(
        out_kept, left_cot, right_cot, gating_part, out_in_turned, second_cot
    )

    @pl.when(h == 0)
    def _():
        hand_over(gradient, gradient_stage, gradient_got, small_sem.at[1], gradient_sem)

    def stack(r, value):
        g, q = r // 4, r % 4
        stacked[g * BLOCK : (g + 1) * BLOCK, q * WIDTH : (q + 1) * WIDTH] = value.astype(BF16)

    flat[...] = gradient

    @pl.when(h == 0)
    def _():
        for r in range(BLOCK):
            stack(r, flat[pl.ds(r, BLOCK, stride=BLOCK), :])

    @pl.when(h == 1)
    def _():
        for r in range(BLOCK):
            stack(r, flat[pl.ds(r * BLOCK, BLOCK), :])

    for x8 in range(HIDDEN // 8):
        chunk = dot(
            stacked[...], turned_weight[:, x8 * 8 * WIDTH : (x8 + 1) * 8 * WIDTH]
        ).astype(BF16)
        for piece in range(8):
            start = (8 * x8 + piece) * BLOCK
            for g in range(4):
                grad_table[start : start + BLOCK, g * WIDTH : (g + 1) * WIDTH] = chunk[
                    g * BLOCK : (g + 1) * BLOCK, piece * WIDTH : (piece + 1) * WIDTH
                ]

    def cot_step(step):
        chips = [along_rows(a, GRID - 1 - 2 * step - n) for n in range(2)]
        sequences = jnp.concatenate(
            [
                msa_relayed[pl.ds(2 * chip, 2)].reshape(2 * 64, BLOCK * HIDDEN)
                for chip in chips
            ],
            axis=0,
        )
        sums = dot(sequences, grad_table[...]).astype(BF16)
        for n, chip in enumerate(chips):
            for core in range(2):
                start = (2 * n + core) * 64
                slot = 2 * chip + core
                cot_parts[slot] = sums[start : start + 64]
                target = cot_got.at[h, a]

                @pl.when(slot == row)
                def _():
                    pltpu.make_async_copy(cot_parts.at[slot], target, cot_sem.at[h, a]).start()

                @pl.when(slot != row)
                def _():
                    remote(
                        cot_parts.at[slot], target, send_sem.at[26], cot_sem.at[h, a], (chip, b), core
                    ).start()

    for step in range(4):
        cot_step(step)
    for core in range(2):

        def cot_sum(k, total, core=core):
            n = along_rows(a, k)
            wait_for(cot_got.at[core, n], cot_sem.at[core, n])
            return total + cot_got[core, n].astype(F32)

        total = lax.fori_loop(0, GRID, cot_sum, jnp.zeros((64, BLOCK * HIDDEN), F32))
        msa_cots[1 - core] = (total * (1.0 / SEQUENCES)).astype(BF16)

    cots = jnp.concatenate(
        [
            jnp.concatenate(
                [msa_cots[kind, :, g * WIDTH : (g + 1) * WIDTH] for kind in range(2)], axis=1
            )
            for g in range(4)
        ],
        axis=0,
    )
    for q in range(4):
        normed_cots = dot(
            cots, spread_factor[q * 2 * WIDTH : (q + 1) * 2 * WIDTH, :], ((1,), (1,))
        )
        for g in range(4):
            rows = pl.ds(4 * g + q, 64, stride=BLOCK)
            value = layer_norm_pullback(
                jnp.concatenate([normed_msa[0][rows, :], normed_msa[1][rows, :]], axis=1),
                msa_scale[rows, :1],
                normed_cots[g * 64 : (g + 1) * 64],
            )
            alignment_first[rows, :] = value[:, :WIDTH]
            alignment_second[rows, :] = value[:, WIDTH:]
    @pl.when(keeps_first)
    def _():
        pair_output[...] = output_stage[0]
        pair_gradient[...] = gradient_stage[0]

    @pl.when(jnp.logical_not(keeps_first))
    def _():
        wait_for(output_got, small_sem.at[0])
        pair_output[...] = output_got[...]
        wait_for(gradient_got, small_sem.at[1])
        pair_gradient[...] = gradient_got[...]

    @pl.when(jnp.logical_not(relay_stays))
    def _():
        for slot in range(4):
            wait_for(relay_left.at[pl.ds(0, 32)], relay_send_sem.at[slot])

    msa_sent(right_jd, msa_direct, 0, send_sem.at[2])
    msa_sent(left_ic, msa_direct, 1, send_sem.at[3])
    block_sent(0, pair_input)
    block_sent(1, cotangent)
    msa_sent(relay_left, msa_relayed, 0, send_sem.at[8])
    msa_sent(relay_right, msa_relayed, 1, send_sem.at[9])
    for number in (10, 13, 14, 16):
        wait_for(o_left.at[pl.ds(0, 7)], send_sem.at[number])
    for number in (11, 12, 15, 17):
        wait_for(o_left, send_sem.at[number])
    wait_for(cot_parts.at[pl.ds(0, 15)], send_sem.at[26])

    @pl.when(h == 0)
    def _():
        wait_for(output_got, output_sem.at[1])
        wait_for(gradient_got, gradient_sem.at[1])

        @pl.when(odd == 1)
        def _():
            wait_for(output_got, output_sem.at[0])
            wait_for(gradient_got, gradient_sem.at[0])


def pair_updates(homolog, factor_weight, pair_input, cotangent, weights):
    gathered = pltpu.VMEM((GRID, BLOCK, BLOCK, WIDTH), BF16)
    block = pltpu.VMEM((BLOCK, BLOCK, WIDTH), BF16)
    flat = pltpu.VMEM((BLOCK * BLOCK, WIDTH), F32)
    shares = pltpu.VMEM((64, BLOCK * HIDDEN), BF16)
    all_sequences = pltpu.VMEM((2 * GRID, 64, BLOCK * HIDDEN), BF16)
    half_block = pltpu.VMEM((8, BLOCK, WIDTH), BF16)
    wide_block = pltpu.VMEM((BLOCK, BLOCK, WIDTH), F32)
    half_wide = pltpu.VMEM((8, BLOCK, WIDTH), F32)
    whole_side = pltpu.VMEM((64 * BLOCK, WIDTH), F32)
    dma = pltpu.SemaphoreType.DMA
    vmem = pl.BlockSpec(memory_space=pltpu.VMEM)
    return pl.pallas_call(
        pair_kernel,
        out_shape=(half_block, half_wide, whole_side, whole_side),
        in_specs=[pl.BlockSpec(memory_space=pl.ANY)] * 9,
        out_specs=(vmem,) * 4,
        scratch_shapes=[
            pltpu.VMEM((64 * BLOCK, 2 * WIDTH), BF16),
            pltpu.VMEM((2 * HIDDEN, 2 * WIDTH), BF16),
            pltpu.VMEM((HIDDEN * HIDDEN, WIDTH), BF16),
            pltpu.VMEM((WIDTH, 5 * WIDTH), BF16),
            pltpu.VMEM((WIDTH, WIDTH), BF16),
            pltpu.VMEM((WIDTH, 5 * WIDTH), BF16),
            pltpu.VMEM((WIDTH, WIDTH), BF16),
            [pltpu.VMEM((64 * BLOCK, WIDTH), F32)] * 2,
            pltpu.VMEM((64 * BLOCK, WIDTH), F32),
            pltpu.VMEM((8 * WIDTH, 2 * WIDTH), BF16),
            shares,
            shares,
            shares,
            shares,
            block,
            block,
            shares,
            shares,
            all_sequences,
            all_sequences,
            gathered,
            gathered,
            block,
            gathered,
            gathered,
            block,
            gathered,
            gathered,
            gathered,
            gathered,
            gathered,
            gathered,
            gathered,
            gathered,
            pltpu.VMEM((HIDDEN * (HIDDEN + 1), WIDTH), F32),
            pltpu.VMEM((HIDDEN * WIDTH, WIDTH), BF16),
            pltpu.VMEM((HIDDEN * WIDTH, 4 * WIDTH), BF16),
            pltpu.VMEM((4 * WIDTH, HIDDEN * WIDTH), BF16),
            pltpu.VMEM((5 * WIDTH, WIDTH), BF16),
            pltpu.VMEM((WIDTH, WIDTH), BF16),
            pltpu.VMEM((5 * WIDTH, WIDTH), BF16),
            pltpu.VMEM((WIDTH, WIDTH), BF16),
            pltpu.VMEM((BLOCK * HIDDEN, BLOCK * HIDDEN), F32),
            wide_block,
            wide_block,
            wide_block,
            wide_block,
            flat,
            pltpu.VMEM((10, BLOCK * BLOCK, WIDTH), F32),
            pltpu.VMEM((9, BLOCK * BLOCK, WIDTH), F32),
            flat,
            flat,
            pltpu.VMEM((64, 4 * WIDTH), BF16),
            pltpu.VMEM((BLOCK * HIDDEN, BLOCK * HIDDEN), BF16),
            pltpu.VMEM((2, 64, BLOCK * HIDDEN), BF16),
            all_sequences,
            pltpu.VMEM((2, GRID, 64, BLOCK * HIDDEN), BF16),
            pltpu.VMEM((2, 8, BLOCK, WIDTH), BF16),
            half_block,
            pltpu.VMEM((2, 8, BLOCK, WIDTH), F32),
            half_wide,
            dma((4,)),
            dma((4,)),
            dma((2, 2)),
            dma((2, 2 * GRID)),
            dma((8, GRID)),
            dma((2, GRID)),
            dma((2,)),
            dma((28,)),
            dma((2,)),
            dma((2,)),
            dma((7,)),
        ],
        compiler_params=pltpu.CompilerParams(
            collective_id=1, has_side_effects=True, vmem_limit_bytes=60 << 20
        ),
        name="pair_updates",
    )(homolog, factor_weight, pair_input, cotangent, *weights)


def hand_out_kernel(
    pair_output,
    pair_gradient,
    alignment_first,
    alignment_second,
    pair_output_out,
    pair_gradient_out,
    alignment_gradient,
    copy_sem,
):
    rows = alignment_first.shape[0] // 4
    pairs = [(pair_output, pair_output_out), (pair_gradient, pair_gradient_out)]
    for part in range(4):
        some = pl.ds(part * rows, rows)
        for side, held in enumerate((alignment_first, alignment_second)):
            target = alignment_gradient.at[some, pl.ds(side * WIDTH, WIDTH)]
            pairs.append((held.at[some], target))
    copies = [
        pltpu.make_async_copy(src, dst, copy_sem.at[number])
        for number, (src, dst) in enumerate(pairs)
    ]
    for copy in copies:
        copy.start()
    for copy in copies:
        copy.wait()


def body(
    homolog_features,
    pair_input,
    cotangent,
    homolog_factor_matrix,
    outer_output_weight,
    outgoing_input_weight,
    outgoing_output_weight,
    incoming_input_weight,
    incoming_output_weight,
):
    sequences, residues, depth = homolog_features.shape
    homolog = homolog_features.reshape(sequences * residues, depth)
    factor_weight = homolog_factor_matrix.T
    results = pair_updates(
        homolog,
        factor_weight,
        pair_input,
        cotangent,
        (
            outer_output_weight,
            outgoing_input_weight,
            outgoing_output_weight,
            incoming_input_weight,
            incoming_output_weight,
        ),
    )
    anywhere = pl.BlockSpec(memory_space=pl.ANY)
    pair_output, pair_gradient, alignment_gradient = pl.pallas_call(
        hand_out_kernel,
        out_shape=(
            jax.ShapeDtypeStruct(pair_input.shape, BF16),
            jax.ShapeDtypeStruct(pair_input.shape, F32),
            jax.ShapeDtypeStruct(homolog.shape, F32),
        ),
        in_specs=[pl.BlockSpec(memory_space=pltpu.VMEM)] * 4,
        out_specs=(anywhere,) * 3,
        scratch_shapes=[pltpu.SemaphoreType.DMA((10,))],
        compiler_params=pltpu.CompilerParams(vmem_limit_bytes=16 << 20),
        name="hand_out",
    )(*results)
    return pair_output, pair_gradient, alignment_gradient.reshape(sequences, residues, depth)


def solution(mesh):
    split = P("row", "col", None)
    return jax.shard_map(
        body,
        mesh=mesh,
        in_specs=(split, split, split, P(), P(), P(), P(), P(), P()),
        out_specs=(split, split, split),
        check_vma=False,
    )
```

```python
import jax
import jax.numpy as jnp
from jax import lax
from jax.experimental import pallas as pl
from jax.experimental.pallas import tpu as pltpu
from jax.sharding import PartitionSpec as P

SEQUENCES = 1024
EPSILON = 1e-05
MESH = pl.DeviceIdType.MESH
F32 = jnp.float32
BF16 = jnp.bfloat16
GRID = 8
BLOCK = 16
WIDTH = 128
HIDDEN = 32


def dot(lhs, rhs, dims=((1,), (0,))):
    return lax.dot_general(lhs, rhs, (dims, ((), ())), preferred_element_type=F32)


def layer_norm(inputs):
    centered = inputs - jnp.mean(inputs, axis=-1, keepdims=True)
    spread = jnp.mean(centered * centered, axis=-1, keepdims=True)
    scale = lax.rsqrt(spread + EPSILON)
    return centered * scale, scale


def layer_norm_pullback(normed, scale, upstream):
    along = jnp.mean(upstream * normed, axis=-1, keepdims=True)
    return scale * (upstream - jnp.mean(upstream, axis=-1, keepdims=True) - normed * along)


def repeat_factor(factor_weight, spread_factor):
    hidden_row = lax.broadcasted_iota(jnp.int32, (2 * HIDDEN, 2 * WIDTH), 0)
    hidden_lane = lax.broadcasted_iota(jnp.int32, (2 * HIDDEN, 2 * WIDTH), 1)
    repeats = (hidden_lane % HIDDEN + HIDDEN * (hidden_lane // WIDTH) == hidden_row).astype(F32)
    repeated = dot(factor_weight[...], repeats.astype(BF16), ((0,), (0,)))
    lane_quarter = lax.broadcasted_iota(jnp.int32, (2 * WIDTH, 2 * WIDTH), 1) % WIDTH // HIDDEN
    for q in range(4):
        spread_factor[q * 2 * WIDTH : (q + 1) * 2 * WIDTH, :] = jnp.where(
            lane_quarter == q, repeated, 0.0
        ).astype(BF16)


def pair_kernel(
    homolog_hbm,
    factor_weight_hbm,
    pair_input,
    cotangent,
    outer_weight_hbm,
    out_in_weight_hbm,
    out_out_weight_hbm,
    in_in_weight_hbm,
    in_out_weight_hbm,
    pair_output,
    pair_gradient,
    alignment_first,
    alignment_second,
    homolog,
    factor_weight,
    outer_weight,
    out_in_weight,
    out_out_weight,
    in_in_weight,
    in_out_weight,
    normed_msa,
    msa_scale,
    spread_factor,
    left_ic,
    left_ci,
    right_dj,
    right_jd,
    pair_block,
    cot_block,
    relay_left,
    relay_right,
    msa_relayed,
    msa_direct,
    o_left,
    o_right,
    o_right_stage,
    i_left,
    i_right,
    i_left_stage,
    ib_right,
    ib_left,
    ob_right,
    ob_left,
    left_parts,
    right_parts,
    left_parts2,
    right_parts2,
    wide_weight,
    table_weight,
    spread_weight,
    turned_weight,
    out_in_turned,
    out_out_turned,
    in_in_turned,
    in_out_turned,
    outer32,
    wide,
    wide_too,
    cot_wide,
    cot_turned,
    flat,
    out_kept,
    in_kept,
    first,
    upstream32,
    stacked,
    grad_table,
    msa_cots,
    cot_parts,
    cot_got,
    output_stage,
    output_got,
    gradient_stage,
    gradient_got,
    relay_sem,
    relay_send_sem,
    block_sem,
    msa_sem,
    pair_sem,
    cot_sem,
    small_sem,
    send_sem,
    output_sem,
    gradient_sem,
    input_sem,
):
    row, col = lax.axis_index("row"), lax.axis_index("col")
    a, h, b = row // 2, row % 2, col
    other = 1 - h
    odd = b % 2
    at = (a + 4 * odd) % GRID
    own_i = at * other + b * h
    own_j = b * other + at * h
    stays = jnp.logical_and(a == b, odd == 0)

    def chip_at(i, j):
        return (i + 4 * (j % 2)) % GRID, j

    def row_chip(n):
        return chip_at(at * other + n * h, n * other + b * h)

    def col_chip(n):
        return chip_at(n * other + at * h, b * other + n * h)

    def apart(k):
        m = k // 2
        return m + (m // 2) * (5 - 2 * m), k % 2

    def along_rows(own, k):
        dm, dv = apart(k)
        return (own // 4 + dv) % 2 * 4 + (own % 4 + dm) % 4

    def along_columns(own, k):
        dm, dv = apart(k)
        return (own // 2 + dm) % 4 * 2 + (own % 2 + dv) % 2

    def step_i(k):
        return along_rows(at, k) * other + along_columns(b, k) * h

    def step_j(k):
        return along_columns(b, k) * other + along_rows(at, k) * h

    relay_column = (a % 4 + b // 2 + 2 * (b % 4)) % 4 * 2 + a // 4
    relay_chip = chip_at(b, relay_column)
    source_row = b % 2 * 4 + (b // 2 + 16 - at // 2 - 2 * (at % 4)) % 4
    relay_stays = jnp.logical_and(relay_column == b, relay_chip[0] == a)

    def column(n):
        return n, b

    def line(n):
        return chip_at(at, n)

    def remote(src, dst, send, recv, chip, core):
        return pltpu.make_async_remote_copy(
            src_ref=src,
            dst_ref=dst,
            send_sem=send,
            recv_sem=recv,
            device_id=(2 * chip[0] + core, chip[1]),
            device_id_type=MESH,
        )

    def wait_for(ref, sem):
        pltpu.make_async_copy(ref, ref, sem).wait()

    inputs = (
        (homolog_hbm, homolog),
        (factor_weight_hbm, factor_weight),
        (outer_weight_hbm, outer_weight),
        (out_in_weight_hbm, out_in_weight),
        (out_out_weight_hbm, out_out_weight),
        (in_in_weight_hbm, in_in_weight),
        (in_out_weight_hbm, in_out_weight),
    )
    copies = [
        pltpu.make_async_copy(src, dst, input_sem.at[number])
        for number, (src, dst) in enumerate(inputs)
    ]
    for copy in copies:
        copy.start()

    barrier = pltpu.get_barrier_semaphore()

    def greet(chip, core):
        pl.semaphore_signal(
            barrier, inc=1, device_id=(2 * chip[0] + core, chip[1]), device_id_type=MESH
        )

    def greet_step(k, carry):
        for core in range(2):
            greet(column(along_rows(a, GRID - k)), core)
            greet(line(along_columns(b, GRID - k)), core)
        return carry

    @pl.when(jnp.logical_not(relay_stays))
    def _():
        greet((source_row, at), h)

    @pl.when(h == 1)
    def _():
        greet((b, at), 0)

    @pl.when(jnp.logical_and(h == 1, jnp.logical_not(stays)))
    def _():
        greet((b, at), 1)

    lax.fori_loop(1, GRID, greet_step, 0)
    greet((a, b), other)
    copies[0].wait()
    copies[1].wait()

    def normalize_step(n, carry):
        rows = pl.ds(pl.multiple_of(n * 256, 256), 256)
        normed, scale = layer_norm(homolog[rows, :].astype(F32))
        msa_scale[rows, :] = jnp.broadcast_to(scale, (256, WIDTH))
        normed_msa[0][rows, :] = normed[:, :WIDTH]
        normed_msa[1][rows, :] = normed[:, WIDTH:]
        return carry

    lax.fori_loop(0, 4, normalize_step, 0)
    repeat_factor(factor_weight, spread_factor)
    groups = []
    for g in range(4):
        pieces = [
            normed_msa[part][pl.ds(4 * g + q, 64, stride=BLOCK), :].astype(BF16)
            for q in range(4)
            for part in range(2)
        ]
        groups.append(jnp.concatenate(pieces, axis=1))
    factors = dot(jnp.concatenate(groups, axis=0), spread_factor[...]).astype(BF16)
    left_value = jnp.concatenate(
        [factors[g * 64 : (g + 1) * 64, :WIDTH] for g in range(4)], axis=1
    )
    right_value = jnp.concatenate(
        [factors[g * 64 : (g + 1) * 64, WIDTH:] for g in range(4)], axis=1
    )
    left_ic[...] = left_value
    right_jd[...] = right_value
    before = lax.broadcasted_iota(jnp.int32, (BLOCK * HIDDEN, BLOCK * HIDDEN), 0)
    after = lax.broadcasted_iota(jnp.int32, (BLOCK * HIDDEN, BLOCK * HIDDEN), 1)
    moved = (before == after % BLOCK * HIDDEN + after // BLOCK).astype(F32).astype(BF16)
    turned_factors = dot(jnp.concatenate([left_value, right_value], axis=0), moved).astype(BF16)
    left_ci[...] = turned_factors[:64]
    right_dj[...] = turned_factors[64:]

    for copy in copies[2:]:
        copy.wait()
    keeps_first = jnp.logical_and(h == 0, odd == 0)
    keeps_second = jnp.logical_and(h == 1, stays)
    pl.semaphore_wait(barrier, 31 - relay_stays.astype(jnp.int32) - keeps_second.astype(jnp.int32))

    for slot in range(4):
        src, dst = ((left_ci, relay_left), (right_dj, relay_right))[slot // 2]
        half = pl.ds(slot % 2 * 32, 32)

        @pl.when(jnp.logical_not(relay_stays))
        def _():
            remote(
                src.at[half],
                dst.at[half],
                relay_send_sem.at[slot],
                relay_sem.at[slot],
                relay_chip,
                h,
            ).start()

        @pl.when(relay_stays)
        def _():
            pltpu.make_async_copy(src.at[half], dst.at[half], relay_sem.at[slot]).start()

    def msa_send(src, dst, sems, slot, chip_of, core, send, half=None):
        whole = half is None
        source = src if whole else src.at[pl.ds(half * 32, 32)]
        target = dst.at[slot] if whole else dst.at[slot, pl.ds(half * 32, 32)]

        def step(k, carry):
            place = (GRID - 1 - k) * other + k * h

            @pl.when(jnp.logical_or(place > 0, h != core))
            def _():
                remote(source, target, send, sems.at[slot], chip_of(place), core).start()

            return carry

        lax.fori_loop(0, GRID, step, 0)

        @pl.when(h == core)
        def _():
            pltpu.make_async_copy(source, target, sems.at[slot]).start()

    def column_step(k):
        return column(along_rows(a, k))

    def line_step(k):
        return line(along_columns(b, k))

    def msa_sent(src, dst, core, send):
        @pl.when(h == core)
        def _():
            wait_for(dst.at[pl.ds(0, 7)], send)

        @pl.when(h != core)
        def _():
            wait_for(dst.at[pl.ds(0, 8)], send)

    msa_send(right_jd, msa_direct, msa_sem.at[1], row, column_step, 0, send_sem.at[2])
    msa_send(left_ic, msa_direct, msa_sem.at[1], row, column_step, 1, send_sem.at[3])

    for slot, (src, dst) in enumerate(((pair_input, pair_block), (cotangent, cot_block))):
        half = dst.at[pl.ds(h * 8, 8)]
        sem = block_sem.at[slot, h]

        @pl.when(keeps_first)
        def _():
            pltpu.make_async_copy(src, half, sem).start()

        @pl.when(jnp.logical_not(keeps_first))
        def _():
            remote(src, half, send_sem.at[4 + slot], sem, chip_at(a, b), 0).start()

        @pl.when(keeps_second)
        def _():
            pltpu.make_async_copy(src, half, sem).start()

        @pl.when(jnp.logical_not(keeps_second))
        def _():
            remote(src, half, send_sem.at[6 + slot], sem, chip_at(b, a), 1).start()

    def block_sent(slot, src):
        @pl.when(jnp.logical_not(keeps_first))
        def _():
            wait_for(src, send_sem.at[4 + slot])

        @pl.when(jnp.logical_not(keeps_second))
        def _():
            wait_for(src, send_sem.at[6 + slot])

    relay_slot = 2 * source_row + h
    for slot in range(4):
        half = slot % 2
        src = (relay_left, relay_right)[slot // 2]
        wait_for(src.at[pl.ds(half * 32, 32)], relay_sem.at[slot])
        kind = slot // 2
        msa_send(
            src, msa_relayed, msa_sem.at[0], relay_slot, line_step, kind, send_sem.at[8 + kind], half
        )

    wide_weight[: HIDDEN * HIDDEN, :] = outer_weight[...].astype(F32)
    spread_weight[...] = jnp.zeros(spread_weight.shape, BF16)

    def weight_step(n, carry):
        start = pl.multiple_of(n * WIDTH, WIDTH)

        def lay_out(piece):
            for q in range(4):
                some = pl.ds(start + q * HIDDEN, HIDDEN)
                table_weight[some, :] = piece
                spread_weight[some, q * WIDTH : (q + 1) * WIDTH] = piece

        @pl.when(h == 0)
        def _():
            lay_out(outer_weight[pl.ds(pl.multiple_of(n * HIDDEN, HIDDEN), HIDDEN), :])

        @pl.when(h == 1)
        def _():
            lay_out(wide_weight[pl.ds(n, HIDDEN, stride=HIDDEN), :].astype(BF16))

        return carry

    lax.fori_loop(0, HIDDEN, weight_step, 0)

    def turn_step(n, carry):
        rows = pl.ds(pl.multiple_of(n * 2 * WIDTH, 2 * WIDTH), 2 * WIDTH)
        turned_weight[:, rows] = spread_weight[rows, :].T
        return carry

    lax.fori_loop(0, HIDDEN // 2, turn_step, 0)
    for weight, turned_one in (
        (out_in_weight, out_in_turned),
        (out_out_weight, out_out_turned),
        (in_in_weight, in_in_turned),
        (in_out_weight, in_out_turned),
    ):
        turned_one[...] = weight[...].T

    own_four = source_row // 2

    def outer_step(k, carry):
        n = (own_four // 2 + k // 2) % 2 * 2 + (own_four % 2 + k % 2) % 2

        def msa_wait(part, carry):
            slot = 4 * n + part
            wait_for(msa_relayed.at[slot], msa_sem.at[0, slot])
            wait_for(msa_direct.at[slot], msa_sem.at[1, slot])
            return carry

        lax.fori_loop(0, 4, msa_wait, 0)
        four = pl.ds(4 * n, 4)
        outer32[...] += dot(
            msa_relayed[four].reshape(256, BLOCK * HIDDEN),
            msa_direct[four].reshape(256, BLOCK * HIDDEN),
            ((0,), (0,)),
        )
        return carry

    outer32[...] = jnp.zeros(outer32.shape, F32)
    lax.fori_loop(0, 4, outer_step, 0)
    lane_part = lax.broadcasted_iota(jnp.int32, (BLOCK, WIDTH), 1) // HIDDEN

    def project_step(d8, total):
        columns = []
        for part in range(8):
            tile = outer32[pl.ds(pl.multiple_of((8 * d8 + part) * BLOCK, BLOCK), BLOCK), :]
            columns.append(
                jnp.concatenate(
                    [
                        jnp.where(lane_part == q, tile[:, g * WIDTH : (g + 1) * WIDTH], 0.0)
                        for q in range(4)
                        for g in range(4)
                    ],
                    axis=0,
                )
            )
        picked = jnp.concatenate(columns, axis=1).astype(BF16)
        weight = table_weight[pl.ds(pl.multiple_of(d8 * 8 * WIDTH, 8 * WIDTH), 8 * WIDTH), :]
        return total + dot(picked, weight)

    projected = lax.fori_loop(
        0, HIDDEN // 8, project_step, jnp.zeros((BLOCK * BLOCK, WIDTH), F32)
    )
    for part in range(2):
        wait_for(pair_block.at[pl.ds(part * 8, 8)], block_sem.at[0, part])
        wait_for(cot_block.at[pl.ds(part * 8, 8)], block_sem.at[1, part])
    for r in range(BLOCK):
        start = ((r % 4) * 4 + r // 4) * BLOCK
        flat[pl.ds(r * BLOCK, BLOCK), :] = projected[start : start + BLOCK] * (1.0 / SEQUENCES)

    def add_rows(i, value):
        first[pl.ds(i * BLOCK, BLOCK), :] = (
            (pair_block[i].astype(F32) + value).astype(BF16).astype(F32)
        )

    @pl.when(h == 0)
    def _():
        for i in range(BLOCK):
            add_rows(i, flat[pl.ds(i, BLOCK, stride=BLOCK), :])

    @pl.when(h == 1)
    def _():
        for i in range(BLOCK):
            add_rows(i, flat[pl.ds(i * BLOCK, BLOCK), :])

    def send_same(dst, sems, chips, steps, send):
        own = steps(0)

        def step(k):
            chip = chips(steps(GRID - k))
            remote(dst.at[own], dst.at[own], send, sems.at[own], chip, h).start()

        for k in range(1, GRID):
            step(k)

    def send_other(src, dst, sems, chips, steps, send):
        own = steps(0)

        def step(k):
            chip = chips(steps(GRID - 1 - k))
            remote(src, dst.at[own], send, sems.at[own], chip, other).start()

        for k in range(GRID):
            step(k)

    def block_product(totals, left, by_column, right):
        totals = list(totals)
        for t in range(BLOCK):
            across = right(t)
            for p in range(BLOCK):
                one = left[t, pl.ds(p, 1), :] if by_column else left[p, pl.ds(t, 1), :]
                totals[p] = totals[p] + one * across
        return tuple(totals)

    def no_totals():
        return tuple(jnp.zeros((BLOCK, WIDTH), F32) for _ in range(BLOCK))

    def contract(left, left_sem, left_own, by_column, right, right_sem, right_own, steps):
        def arrive(ref, sems, slot, skip):
            if skip is None:
                wait_for(ref.at[slot], sems.at[slot])
            else:

                @pl.when(slot != skip)
                def _():
                    wait_for(ref.at[slot], sems.at[slot])

        def block_step(k, totals):
            slot = steps(k)
            arrive(left, left_sem, slot, left_own)
            arrive(right, right_sem, slot, right_own)
            wide[...] = left[slot].astype(F32)
            return block_product(totals, wide, by_column, lambda t: right[slot, t].astype(F32))

        totals = lax.fori_loop(0, GRID, block_step, no_totals())
        return jnp.concatenate(totals, axis=0)

    def partial(part, n, totals):
        for p in range(BLOCK):
            part[n, p] = totals[p].astype(BF16)

    def sum_of(parts, sems, skip, steps):
        def step(k, total):
            slot = steps(k)
            if skip is None:
                wait_for(parts.at[slot], sems.at[slot])
            else:

                @pl.when(slot != skip)
                def _():
                    wait_for(parts.at[slot], sems.at[slot])

            return total + parts[slot].reshape(BLOCK * BLOCK, WIDTH).astype(F32)

        return lax.fori_loop(0, GRID, step, jnp.zeros((BLOCK * BLOCK, WIDTH), F32))

    def send_part(part, n, dst, slot, sems, chips, core, send):
        remote(part.at[n], dst.at[slot], send, sems.at[slot], chips(n), core).start()

    def turned(value, store):
        flat[...] = value
        for j in range(BLOCK):
            store(j, flat[pl.ds(j, BLOCK, stride=BLOCK), :].astype(BF16))

    def turn_cot(value):
        rounded = value.astype(BF16).astype(F32)
        cot_wide[...] = rounded.reshape(BLOCK, BLOCK, WIDTH)
        flat[...] = rounded
        for j in range(BLOCK):
            cot_turned[j] = flat[pl.ds(j, BLOCK, stride=BLOCK), :]

    def blocked(value):
        return value.astype(BF16).reshape(BLOCK, BLOCK, WIDTH)

    def gated(normed, weight, at):
        projected = dot(normed, weight[:, at * WIDTH : (at + 2) * WIDTH])
        gate, value = jax.nn.sigmoid(projected[:, :WIDTH]), projected[:, WIDTH:]
        return gate, value

    def keep_gated(ref, first_at, gate, value):
        ref[first_at] = value * gate * (1.0 - gate)
        ref[first_at + 1] = gate

    def keep_norm(ref, first_at, normed, scale):
        ref[first_at] = normed
        ref[first_at + 1] = jnp.broadcast_to(scale, normed.shape)

    normed, scale = layer_norm(first[...])
    rounded = normed.astype(BF16)
    left_gate, left_value = gated(rounded, out_in_weight, 0)
    o_left[own_j] = blocked(left_gate * left_value)
    send_same(o_left, pair_sem.at[0], row_chip, step_j, send_sem.at[10])
    right_gate, right_value = gated(rounded, out_in_weight, 2)

    def store_right(j, value):
        o_right_stage[j] = value

    turned(right_gate * right_value, store_right)
    send_other(o_right_stage, o_right, pair_sem.at[1], row_chip, step_j, send_sem.at[11])
    keep_gated(out_kept, 0, left_gate, left_value)
    keep_gated(out_kept, 2, right_gate, right_value)
    keep_norm(out_kept, 4, normed, scale)
    out_kept[6] = jax.nn.sigmoid(dot(rounded, out_in_weight[:, 4 * WIDTH :]))
    mixing = contract(
        o_left,
        pair_sem.at[0],
        own_j,
        False,
        o_right,
        pair_sem.at[1],
        None,
        step_j,
    )
    mixing_normed, mixing_scale = layer_norm(mixing)
    update = dot(mixing_normed.astype(BF16), out_out_weight[...])
    second = (first[...] + out_kept[6] * update).astype(BF16).astype(F32)

    normed, scale = layer_norm(second)
    rounded = normed.astype(BF16)
    right_gate, right_value = gated(rounded, in_in_weight, 2)
    i_right[own_i] = blocked(right_gate * right_value)
    send_same(i_right, pair_sem.at[4], col_chip, step_i, send_sem.at[14])
    left_gate, left_value = gated(rounded, in_in_weight, 0)
    i_left_stage[...] = blocked(left_gate * left_value)
    send_other(i_left_stage, i_left, pair_sem.at[5], col_chip, step_i, send_sem.at[15])
    keep_norm(out_kept, 7, mixing_normed, mixing_scale)
    out_kept[9] = update
    keep_gated(in_kept, 0, left_gate, left_value)
    keep_gated(in_kept, 2, right_gate, right_value)
    keep_norm(in_kept, 4, normed, scale)
    gating = jax.nn.sigmoid(dot(rounded, in_in_weight[:, 4 * WIDTH :]))
    in_kept[6] = gating
    in_kept[7] = second
    upstream = cot_block[...].reshape(BLOCK * BLOCK, WIDTH).astype(F32)
    upstream32[...] = upstream
    in_kept[8] = dot((upstream * gating).astype(BF16), in_out_turned[...])
    mixing = contract(
        i_left,
        pair_sem.at[5],
        None,
        True,
        i_right,
        pair_sem.at[4],
        own_i,
        step_i,
    )

    def input_pullback(kept, left_cot, right_cot, gating_part, weight, upstream):
        pieces = [
            (left_cot * kept[0]).astype(BF16),
            (left_cot * kept[1]).astype(BF16),
            (right_cot * kept[2]).astype(BF16),
            (right_cot * kept[3]).astype(BF16),
        ]
        normed_cot = gating_part + dot(
            jnp.concatenate(pieces, axis=1), weight[: 4 * WIDTH, :]
        )
        return upstream + layer_norm_pullback(kept[4], kept[5], normed_cot)

    normed, scale = layer_norm(mixing)
    turn_cot(layer_norm_pullback(normed, scale, in_kept[8]))

    def incoming_step(k, carry):
        n = step_i(GRID - 1 - k)
        wide[...] = i_right[n].astype(F32)
        totals = block_product(no_totals(), wide, False, lambda t: cot_turned[t])
        partial(left_parts, n, totals)
        send_part(
            left_parts, n, ib_left, own_j, pair_sem.at[2], row_chip, other, send_sem.at[12]
        )
        wide_too[...] = i_left[n].astype(F32)
        totals = block_product(no_totals(), wide_too, False, lambda t: cot_wide[t])

        @pl.when(n != own_i)
        def _():
            partial(right_parts, n, totals)
            send_part(
                right_parts, n, ib_right, own_i, pair_sem.at[3], col_chip, h, send_sem.at[13]
            )

        @pl.when(n == own_i)
        def _():
            partial(ib_right, n, totals)

        return carry

    lax.fori_loop(0, GRID, incoming_step, 0)
    gating = in_kept[6]
    update = dot(normed.astype(BF16), in_out_weight[...])
    result = (in_kept[7] + gating * update).astype(BF16)
    gating_cot = upstream32[...] * update * gating * (1.0 - gating)
    gating_part = dot(gating_cot.astype(BF16), in_in_turned[4 * WIDTH :, :])

    def hand_over(value, stage, got, sem, send):
        stage[...] = value.reshape(2, 8, BLOCK, WIDTH)
        for part in range(2):
            order = remote(stage.at[part], got, send.at[part], sem, (at, b), part)
            if part == 0:
                pl.when(odd == 1)(order.start)
            else:
                order.start()

    @pl.when(h == 0)
    def _():
        hand_over(result, output_stage, output_got, small_sem.at[0], output_sem)

    left_cot = sum_of(ib_left, pair_sem.at[2], None, step_j)
    right_cot = sum_of(ib_right, pair_sem.at[3], own_i, step_i)
    second_cot = input_pullback(
        in_kept, left_cot, right_cot, gating_part, in_in_turned, upstream32[...]
    )

    normed_cot = dot((second_cot * out_kept[6]).astype(BF16), out_out_turned[...])
    turn_cot(layer_norm_pullback(out_kept[7], out_kept[8], normed_cot))

    def outgoing_step(k, carry):
        n = step_j(GRID - 1 - k)
        wide[...] = o_right[n].astype(F32)
        totals = block_product(no_totals(), wide, False, lambda t: cot_turned[t])

        @pl.when(n != own_j)
        def _():
            partial(left_parts2, n, totals)
            send_part(
                left_parts2, n, ob_left, own_j, pair_sem.at[6], row_chip, h, send_sem.at[16]
            )

        @pl.when(n == own_j)
        def _():
            partial(ob_left, n, totals)

        totals = block_product(
            no_totals(), cot_wide, True, lambda t: o_left[n, t].astype(F32)
        )
        partial(right_parts2, n, totals)
        send_part(
            right_parts2, n, ob_right, own_i, pair_sem.at[7], col_chip, other, send_sem.at[17]
        )
        return carry

    lax.fori_loop(0, GRID, outgoing_step, 0)
    gating = out_kept[6]
    gating_cot = second_cot * out_kept[9] * gating * (1.0 - gating)
    gating_part = dot(gating_cot.astype(BF16), out_in_turned[4 * WIDTH :, :])
    flat[...] = sum_of(ob_left, pair_sem.at[6], own_j, step_j)
    left_cot = jnp.concatenate(
        [flat[pl.ds(j, BLOCK, stride=BLOCK), :] for j in range(BLOCK)], axis=0
    )
    right_cot = sum_of(ob_right, pair_sem.at[7], None, step_i)
    gradient = input_pullback(
        out_kept, left_cot, right_cot, gating_part, out_in_turned, second_cot
    )

    @pl.when(h == 0)
    def _():
        hand_over(gradient, gradient_stage, gradient_got, small_sem.at[1], gradient_sem)

    def stack(r, value):
        g, q = r // 4, r % 4
        stacked[g * BLOCK : (g + 1) * BLOCK, q * WIDTH : (q + 1) * WIDTH] = value.astype(BF16)

    flat[...] = gradient

    @pl.when(h == 0)
    def _():
        for r in range(BLOCK):
            stack(r, flat[pl.ds(r, BLOCK, stride=BLOCK), :])

    @pl.when(h == 1)
    def _():
        for r in range(BLOCK):
            stack(r, flat[pl.ds(r * BLOCK, BLOCK), :])

    for x8 in range(HIDDEN // 8):
        chunk = dot(
            stacked[...], turned_weight[:, x8 * 8 * WIDTH : (x8 + 1) * 8 * WIDTH]
        ).astype(BF16)
        for piece in range(8):
            start = (8 * x8 + piece) * BLOCK
            for g in range(4):
                grad_table[start : start + BLOCK, g * WIDTH : (g + 1) * WIDTH] = chunk[
                    g * BLOCK : (g + 1) * BLOCK, piece * WIDTH : (piece + 1) * WIDTH
                ]

    def cot_step(step):
        places = [2 * step + n for n in range(2)]
        chips = [along_rows(a, (GRID - 1 - place) * other + place * h) for place in places]
        sequences = jnp.concatenate(
            [
                msa_relayed[pl.ds(2 * chip, 2)].reshape(2 * 64, BLOCK * HIDDEN)
                for chip in chips
            ],
            axis=0,
        )
        sums = dot(sequences, grad_table[...]).astype(BF16)
        for n, chip in enumerate(chips):
            for core in range(2):
                start = (2 * n + core) * 64
                slot = 2 * chip + core
                cot_parts[slot] = sums[start : start + 64]
                target = cot_got.at[h, a]

                @pl.when(slot == row)
                def _():
                    pltpu.make_async_copy(cot_parts.at[slot], target, cot_sem.at[h, a]).start()

                @pl.when(slot != row)
                def _():
                    remote(
                        cot_parts.at[slot], target, send_sem.at[26], cot_sem.at[h, a], (chip, b), core
                    ).start()

    for step in range(4):
        cot_step(step)
    for core in range(2):

        def cot_sum(k, total, core=core):
            n = along_rows(a, k)
            wait_for(cot_got.at[core, n], cot_sem.at[core, n])
            return total + cot_got[core, n].astype(F32)

        total = lax.fori_loop(0, GRID, cot_sum, jnp.zeros((64, BLOCK * HIDDEN), F32))
        msa_cots[1 - core] = (total * (1.0 / SEQUENCES)).astype(BF16)

    cots = jnp.concatenate(
        [
            jnp.concatenate(
                [msa_cots[kind, :, g * WIDTH : (g + 1) * WIDTH] for kind in range(2)], axis=1
            )
            for g in range(4)
        ],
        axis=0,
    )
    for q in range(4):
        normed_cots = dot(
            cots, spread_factor[q * 2 * WIDTH : (q + 1) * 2 * WIDTH, :], ((1,), (1,))
        )
        for g in range(4):
            rows = pl.ds(4 * g + q, 64, stride=BLOCK)
            value = layer_norm_pullback(
                jnp.concatenate([normed_msa[0][rows, :], normed_msa[1][rows, :]], axis=1),
                msa_scale[rows, :1],
                normed_cots[g * 64 : (g + 1) * 64],
            )
            alignment_first[rows, :] = value[:, :WIDTH]
            alignment_second[rows, :] = value[:, WIDTH:]
    @pl.when(keeps_first)
    def _():
        pair_output[...] = output_stage[0]
        pair_gradient[...] = gradient_stage[0]

    @pl.when(jnp.logical_not(keeps_first))
    def _():
        wait_for(output_got, small_sem.at[0])
        pair_output[...] = output_got[...]
        wait_for(gradient_got, small_sem.at[1])
        pair_gradient[...] = gradient_got[...]

    @pl.when(jnp.logical_not(relay_stays))
    def _():
        for slot in range(4):
            wait_for(relay_left.at[pl.ds(0, 32)], relay_send_sem.at[slot])

    msa_sent(right_jd, msa_direct, 0, send_sem.at[2])
    msa_sent(left_ic, msa_direct, 1, send_sem.at[3])
    block_sent(0, pair_input)
    block_sent(1, cotangent)
    msa_sent(relay_left, msa_relayed, 0, send_sem.at[8])
    msa_sent(relay_right, msa_relayed, 1, send_sem.at[9])
    for number in (10, 13, 14, 16):
        wait_for(o_left.at[pl.ds(0, 7)], send_sem.at[number])
    for number in (11, 12, 15, 17):
        wait_for(o_left, send_sem.at[number])
    wait_for(cot_parts.at[pl.ds(0, 15)], send_sem.at[26])

    @pl.when(h == 0)
    def _():
        wait_for(output_got, output_sem.at[1])
        wait_for(gradient_got, gradient_sem.at[1])

        @pl.when(odd == 1)
        def _():
            wait_for(output_got, output_sem.at[0])
            wait_for(gradient_got, gradient_sem.at[0])


def pair_updates(homolog, factor_weight, pair_input, cotangent, weights):
    gathered = pltpu.VMEM((GRID, BLOCK, BLOCK, WIDTH), BF16)
    block = pltpu.VMEM((BLOCK, BLOCK, WIDTH), BF16)
    flat = pltpu.VMEM((BLOCK * BLOCK, WIDTH), F32)
    shares = pltpu.VMEM((64, BLOCK * HIDDEN), BF16)
    all_sequences = pltpu.VMEM((2 * GRID, 64, BLOCK * HIDDEN), BF16)
    half_block = pltpu.VMEM((8, BLOCK, WIDTH), BF16)
    wide_block = pltpu.VMEM((BLOCK, BLOCK, WIDTH), F32)
    half_wide = pltpu.VMEM((8, BLOCK, WIDTH), F32)
    whole_side = pltpu.VMEM((64 * BLOCK, WIDTH), F32)
    dma = pltpu.SemaphoreType.DMA
    vmem = pl.BlockSpec(memory_space=pltpu.VMEM)
    return pl.pallas_call(
        pair_kernel,
        out_shape=(half_block, half_wide, whole_side, whole_side),
        in_specs=[pl.BlockSpec(memory_space=pl.ANY)] * 9,
        out_specs=(vmem,) * 4,
        scratch_shapes=[
            pltpu.VMEM((64 * BLOCK, 2 * WIDTH), BF16),
            pltpu.VMEM((2 * HIDDEN, 2 * WIDTH), BF16),
            pltpu.VMEM((HIDDEN * HIDDEN, WIDTH), BF16),
            pltpu.VMEM((WIDTH, 5 * WIDTH), BF16),
            pltpu.VMEM((WIDTH, WIDTH), BF16),
            pltpu.VMEM((WIDTH, 5 * WIDTH), BF16),
            pltpu.VMEM((WIDTH, WIDTH), BF16),
            [pltpu.VMEM((64 * BLOCK, WIDTH), F32)] * 2,
            pltpu.VMEM((64 * BLOCK, WIDTH), F32),
            pltpu.VMEM((8 * WIDTH, 2 * WIDTH), BF16),
            shares,
            shares,
            shares,
            shares,
            block,
            block,
            shares,
            shares,
            all_sequences,
            all_sequences,
            gathered,
            gathered,
            block,
            gathered,
            gathered,
            block,
            gathered,
            gathered,
            gathered,
            gathered,
            gathered,
            gathered,
            gathered,
            gathered,
            pltpu.VMEM((HIDDEN * (HIDDEN + 1), WIDTH), F32),
            pltpu.VMEM((HIDDEN * WIDTH, WIDTH), BF16),
            pltpu.VMEM((HIDDEN * WIDTH, 4 * WIDTH), BF16),
            pltpu.VMEM((4 * WIDTH, HIDDEN * WIDTH), BF16),
            pltpu.VMEM((5 * WIDTH, WIDTH), BF16),
            pltpu.VMEM((WIDTH, WIDTH), BF16),
            pltpu.VMEM((5 * WIDTH, WIDTH), BF16),
            pltpu.VMEM((WIDTH, WIDTH), BF16),
            pltpu.VMEM((BLOCK * HIDDEN, BLOCK * HIDDEN), F32),
            wide_block,
            wide_block,
            wide_block,
            wide_block,
            flat,
            pltpu.VMEM((10, BLOCK * BLOCK, WIDTH), F32),
            pltpu.VMEM((9, BLOCK * BLOCK, WIDTH), F32),
            flat,
            flat,
            pltpu.VMEM((64, 4 * WIDTH), BF16),
            pltpu.VMEM((BLOCK * HIDDEN, BLOCK * HIDDEN), BF16),
            pltpu.VMEM((2, 64, BLOCK * HIDDEN), BF16),
            all_sequences,
            pltpu.VMEM((2, GRID, 64, BLOCK * HIDDEN), BF16),
            pltpu.VMEM((2, 8, BLOCK, WIDTH), BF16),
            half_block,
            pltpu.VMEM((2, 8, BLOCK, WIDTH), F32),
            half_wide,
            dma((4,)),
            dma((4,)),
            dma((2, 2)),
            dma((2, 2 * GRID)),
            dma((8, GRID)),
            dma((2, GRID)),
            dma((2,)),
            dma((28,)),
            dma((2,)),
            dma((2,)),
            dma((7,)),
        ],
        compiler_params=pltpu.CompilerParams(
            collective_id=1, has_side_effects=True, vmem_limit_bytes=60 << 20
        ),
        name="pair_updates",
    )(homolog, factor_weight, pair_input, cotangent, *weights)


def hand_out_kernel(
    pair_output,
    pair_gradient,
    alignment_first,
    alignment_second,
    pair_output_out,
    pair_gradient_out,
    alignment_gradient,
    copy_sem,
):
    rows = alignment_first.shape[0] // 4
    pairs = [(pair_output, pair_output_out), (pair_gradient, pair_gradient_out)]
    for part in range(4):
        some = pl.ds(part * rows, rows)
        for side, held in enumerate((alignment_first, alignment_second)):
            target = alignment_gradient.at[some, pl.ds(side * WIDTH, WIDTH)]
            pairs.append((held.at[some], target))
    copies = [
        pltpu.make_async_copy(src, dst, copy_sem.at[number])
        for number, (src, dst) in enumerate(pairs)
    ]
    for copy in copies:
        copy.start()
    for copy in copies:
        copy.wait()


def body(
    homolog_features,
    pair_input,
    cotangent,
    homolog_factor_matrix,
    outer_output_weight,
    outgoing_input_weight,
    outgoing_output_weight,
    incoming_input_weight,
    incoming_output_weight,
):
    sequences, residues, depth = homolog_features.shape
    homolog = homolog_features.reshape(sequences * residues, depth)
    factor_weight = homolog_factor_matrix.T
    results = pair_updates(
        homolog,
        factor_weight,
        pair_input,
        cotangent,
        (
            outer_output_weight,
            outgoing_input_weight,
            outgoing_output_weight,
            incoming_input_weight,
            incoming_output_weight,
        ),
    )
    anywhere = pl.BlockSpec(memory_space=pl.ANY)
    pair_output, pair_gradient, alignment_gradient = pl.pallas_call(
        hand_out_kernel,
        out_shape=(
            jax.ShapeDtypeStruct(pair_input.shape, BF16),
            jax.ShapeDtypeStruct(pair_input.shape, F32),
            jax.ShapeDtypeStruct(homolog.shape, F32),
        ),
        in_specs=[pl.BlockSpec(memory_space=pltpu.VMEM)] * 4,
        out_specs=(anywhere,) * 3,
        scratch_shapes=[pltpu.SemaphoreType.DMA((10,))],
        compiler_params=pltpu.CompilerParams(vmem_limit_bytes=16 << 20),
        name="hand_out",
    )(*results)
    return pair_output, pair_gradient, alignment_gradient.reshape(sequences, residues, depth)


def solution(mesh):
    split = P("row", "col", None)
    return jax.shard_map(
        body,
        mesh=mesh,
        in_specs=(split, split, split, P(), P(), P(), P(), P(), P()),
        out_specs=(split, split, split),
        check_vma=False,
    )
```
